32 devices in a mesh: ctx: 4 (over z), head: 4 (over y, x), rep: 2 (over core).
Axes of the slice: x: 2, y: 2, z: 4, core: 2. Of those that a mesh axis runs over, the one named last changes fastest.
Arguments:
- prefill_query: bfloat16 [2, 1024, 8192], P('rep', 'ctx', 'head'), may hold values from -6 to 6
- prefill_key: bfloat16 [2, 1024, 8192], P('rep', 'ctx', 'head'), may hold values from -0.5390625 to 0.5390625
- prefill_value: bfloat16 [2, 1024, 8192], P('rep', 'ctx', 'head'), as said below
- prefill_rate: float32 [2, 64, 1024], P('rep', 'head', 'ctx'), as said below
- out_weight: bfloat16 [8192, 6144], P('head'), may hold values from -0.0625 to 0.0625
- decode_query: bfloat16 [32, 2, 8192], P(('ctx', 'rep'), None, 'head'), may hold values from -6 to 6
- decode_key: bfloat16 [32, 2, 8192], P(('ctx', 'rep'), None, 'head'), may hold values from -0.5390625 to 0.5390625
- decode_value: bfloat16 [32, 2, 8192], P(('ctx', 'rep'), None, 'head'), may hold values from -6 to 6
- decode_rate: float32 [32, 64, 2], P(('ctx', 'rep'), 'head'), may hold values from 0.01 to 0.5
- prompt_of_row: int32 [32], P(('ctx', 'rep')), may hold values from 0 to 1
Outputs:
- prefill_out: bfloat16 [2, 1024, 6144], P('rep', 'ctx', 'head')
- decode_out: bfloat16 [32, 2, 6144], P(('ctx', 'rep'), None, 'head')
The draws below stay inside these ranges and needn't reach their ends.
Inputs may be any that keep to these rules, and one draw needn't show every extreme that they name: `prefill_value`: values with row and column scales. `prefill_rate`: positive decay rates.
All inputs are finite; a program needn't handle non-finite values.
Results may differ from the reference program's by a relative error of at most 0.0055.
Values may be sent and summed in bfloat16 or wider, within the bound.
No kernel may reach another device: no remote copies, remote signals or barrier semaphores. Data moves between devices by JAX's collectives and lax.ppermute only.
A program may use at most 128 MiB of HBM per device.

```python
import math
import jax
import jax.numpy as jnp
from jax import lax

D = 6144
HEAD_COUNT = 64
HEAD_DIM = 128
BLOCK = 256
TOK_DEV = 256
STEPS = 2
PROMPT_COUNT = 2
PROMPT_LENGTH = 1024
ROWS = 32
FEATURES = 8192


def draw_prefill_value(key, part):
    random_subkeys = jax.random.split(jax.random.fold_in(key, 11), 3)
    shape = (PROMPT_COUNT, PROMPT_LENGTH, FEATURES)
    baseline_level = jax.random.normal(random_subkeys[0], shape, jnp.float32)
    row_scale = jnp.exp(jax.random.uniform(random_subkeys[1], (PROMPT_COUNT, PROMPT_LENGTH, 1), jnp.float32, 0.0, math.log(10.0)))
    col_scale = jnp.exp(jax.random.uniform(random_subkeys[2], (1, 1, FEATURES), jnp.float32, 0.0, math.log(10.0)))
    return (0.1 * baseline_level * row_scale * col_scale).astype(jnp.bfloat16)


def draw_prefill_rate(key, part):
    random_subkeys = jax.random.split(jax.random.fold_in(key, 23), 7)
    fast_share = 0.5
    fast = jax.random.uniform(random_subkeys[0], (PROMPT_COUNT, HEAD_COUNT, 1), jnp.float32) < fast_share
    fast_rate = jnp.exp(jax.random.uniform(random_subkeys[1], (PROMPT_COUNT, HEAD_COUNT, 1), jnp.float32, math.log(1.0 / 50.0), math.log(1.0 / 20.0)))
    slow_rate = jnp.exp(jax.random.uniform(random_subkeys[2], (PROMPT_COUNT, HEAD_COUNT, 1), jnp.float32, math.log(0.05), math.log(0.3))) / PROMPT_LENGTH
    baseline_level = jnp.where(fast, fast_rate, slow_rate)
    groups = PROMPT_LENGTH // TOK_DEV
    group_multiplier = jnp.exp(jax.random.uniform(random_subkeys[3], (PROMPT_COUNT, HEAD_COUNT, groups), jnp.float32, math.log(0.5), math.log(2.0)))
    group_multiplier = jnp.repeat(group_multiplier, TOK_DEV, axis=2)
    jitter_amplitude = jax.random.uniform(random_subkeys[4], (PROMPT_COUNT, HEAD_COUNT, PROMPT_LENGTH), jnp.float32, 0.5, 1.5)
    spike_locations = jax.random.randint(random_subkeys[5], (PROMPT_COUNT, 2), 0, PROMPT_LENGTH)
    position_index = jnp.arange(PROMPT_LENGTH, dtype=jnp.int32)
    spike_selector = jnp.any(position_index[None, None, :] == spike_locations[:, :, None], axis=1)[:, None, :]
    spike_penalty = jax.random.uniform(random_subkeys[6], (PROMPT_COUNT, HEAD_COUNT, PROMPT_LENGTH), jnp.float32, 0.22, 0.6)
    decay_rate = baseline_level * group_multiplier * jitter_amplitude + jnp.where(spike_selector, spike_penalty, 0.0)
    return decay_rate.astype(jnp.float32)


def set_ends(values, key, least, top_value):
    dims = values.shape
    spot = [jax.random.randint(jax.random.fold_in(key, axis), (), 0, dims[axis]) for axis in range(len(dims))]
    values = values.at[tuple(spot)].set(least)
    longest = dims.index(max(dims))
    spot[longest] = (spot[longest] + 1) % dims[longest]
    return values.at[tuple(spot)].set(top_value)


def block_scale(stream_key, shape, cuts, low, high):
    def one(position, blocks):
        draws = jax.random.uniform(jax.random.fold_in(jax.random.fold_in(stream_key, 6), position), (blocks,), jnp.float32, low / len(cuts), high / len(cuts))
        return jnp.repeat(jnp.exp(draws), shape[position] // blocks).reshape((-1,) + (1,) * (len(shape) - position - 1))

    factor_of = one(*cuts[0])
    for cut in cuts[1:]:
        factor_of = factor_of * one(*cut)
    return factor_of


def normal_values(rng, shape, deviation, most, cuts=(), kind=jnp.bfloat16):
    values = jax.random.normal(rng, shape, jnp.float32) * deviation
    if len(cuts) > 0:
        values = block_scale(rng, shape, cuts, -0.22, 0.18) * values
    return jnp.clip(values, min=-most, max=most).astype(kind)


def setup_inputs(seed: int = 0) -> dict:
    seeds = jax.random.split(jax.random.key(seed), 11)
    prefill_query = normal_values(seeds[0], (PROMPT_COUNT, PROMPT_LENGTH, FEATURES), 1.0, 6.0, ((0, 2), (1, 4), (2, 4)))
    prefill_key = normal_values(seeds[1], (PROMPT_COUNT, PROMPT_LENGTH, FEATURES), 0.09, 0.5390625, ((0, 2), (1, 4), (2, 4)))
    prefill_value = draw_prefill_value(jax.random.fold_in(seeds[10], 71), 0)
    prefill_rate = draw_prefill_rate(jax.random.fold_in(seeds[10], 71), 0)
    out_weight = normal_values(seeds[4], (FEATURES, D), FEATURES ** -0.5, 0.0625, ((0, 4),))
    decode_query = normal_values(seeds[5], (ROWS, STEPS, FEATURES), 1.0, 6.0, ((0, 8), (2, 4)))
    decode_key = normal_values(seeds[6], (ROWS, STEPS, FEATURES), 0.09, 0.5390625, ((0, 8), (2, 4)))
    decode_value = normal_values(seeds[7], (ROWS, STEPS, FEATURES), 1.0, 6.0, ((0, 8), (2, 4)))
    decode_rate = jnp.clip(jnp.exp(math.log(0.5) - 3.912023 * jax.random.uniform(seeds[8], (ROWS, HEAD_COUNT, STEPS), jnp.float32) ** block_scale(seeds[8], (ROWS, HEAD_COUNT, STEPS), ((0, 8), (1, 4)), -0.2, 0.2)), 0.01, 0.5)
    prompt_of_row = set_ends(jax.random.randint(seeds[9], (ROWS,), 0, PROMPT_COUNT), jax.random.fold_in(seeds[9], 1), 0, PROMPT_COUNT - 1).astype(jnp.int32)
    return {"prefill_query": prefill_query, "prefill_key": prefill_key, "prefill_value": prefill_value, "prefill_rate": prefill_rate, "out_weight": out_weight, "decode_query": decode_query, "decode_key": decode_key, "decode_value": decode_value, "decode_rate": decode_rate, "prompt_of_row": prompt_of_row}


EPSILON = 1e-06
NEGATIVE = -1e+30
HIGH = lax.Precision.HIGHEST

def normalize(array):
    return array * lax.rsqrt(lax.optimization_barrier(jnp.mean(array * array, axis=-1, keepdims=True)) + EPSILON)

def reference(prefill_query, prefill_key, prefill_value, prefill_rate, out_weight, decode_query, decode_key, decode_value, decode_rate, prompt_of_row):
    prompts = prefill_query.shape[0]
    count = PROMPT_LENGTH // BLOCK

    def blocked(array):
        return array.reshape(prompts, count, BLOCK, HEAD_COUNT, HEAD_DIM).transpose(1, 0, 2, 3, 4)
    q_blocks = blocked(prefill_query)
    k_blocks = blocked(prefill_key)
    v_blocks = blocked(prefill_value)
    g_blocks = (-prefill_rate).reshape(prompts, HEAD_COUNT, count, BLOCK).transpose(2, 0, 1, 3)
    lower_mask = jnp.arange(BLOCK)[:, None] >= jnp.arange(BLOCK)[None, :]

    def advance(state, inputs):
        q_blk, k_blk, v_blk, g_blk = inputs
        q_f = q_blk.astype(jnp.float32)
        k_f = k_blk.astype(jnp.float32)
        v_f = v_blk.astype(jnp.float32)
        cumul = jnp.cumsum(g_blk, axis=-1)
        total = cumul[..., -1]
        decay = jnp.exp(jnp.where(lower_mask, cumul[..., :, None] - cumul[..., None, :], NEGATIVE))
        scores = jnp.einsum('pthd,pshd->phts', q_f, k_f)
        weights = (scores * decay).astype(jnp.bfloat16)
        weights = lax.optimization_barrier(weights).astype(jnp.float32)
        intra = jnp.einsum('phts,pshe->pthe', weights, v_f)
        inter = jnp.einsum('pthd,phde->pthe', q_f, state, precision=HIGH) * jnp.exp(cumul).transpose(0, 2, 1)[..., None]
        k_weighted = k_f * jnp.exp(total[..., None] - cumul).transpose(0, 2, 1)[..., None]
        new_state = jnp.exp(total)[..., None, None] * state + jnp.einsum('pshd,pshe->phde', k_weighted, v_f, precision=HIGH)
        return (new_state, intra + inter)
    start = jnp.zeros((prompts, HEAD_COUNT, HEAD_DIM, HEAD_DIM), jnp.float32)
    finals, outputs = lax.scan(advance, start, (q_blocks, k_blocks, v_blocks, g_blocks))
    attended = outputs.transpose(1, 0, 2, 3, 4).reshape(prompts, PROMPT_LENGTH, HEAD_COUNT, HEAD_DIM)
    hidden = normalize(attended).astype(jnp.bfloat16).reshape(prompts, PROMPT_LENGTH, HEAD_COUNT * HEAD_DIM)
    prefill_out = lax.map(lambda hidden_one: jnp.dot(hidden_one, out_weight, preferred_element_type=jnp.float32).astype(jnp.bfloat16), hidden)
    rows = decode_query.shape[0]

    def split_heads(array):
        return array.reshape(rows, STEPS, HEAD_COUNT, HEAD_DIM).astype(jnp.float32)
    d_query = split_heads(decode_query)
    d_key = split_heads(decode_key)
    d_value = split_heads(decode_value)
    cumul = jnp.cumsum(-decode_rate, axis=-1)
    onehot = (prompt_of_row[:, None] == jnp.arange(prompts, dtype=jnp.int32)[None, :]).astype(jnp.float32)
    start_terms = jnp.einsum('rthd,phde->prthe', d_query, finals, precision=HIGH)
    baseline_level = jnp.einsum('rp,prthe->rthe', onehot, start_terms, precision=HIGH) * jnp.exp(cumul).transpose(0, 2, 1)[..., None]
    step_mask = jnp.arange(STEPS)[:, None] >= jnp.arange(STEPS)[None, :]
    decay = jnp.exp(jnp.where(step_mask, cumul[..., :, None] - cumul[..., None, :], NEGATIVE))
    scores = jnp.einsum('rthd,rshd->rhts', d_query, d_key, precision=HIGH)
    intra = jnp.einsum('rhts,rshe->rthe', scores * decay, d_value, precision=HIGH)
    decode_hidden = normalize(baseline_level + intra).astype(jnp.bfloat16).reshape(rows * STEPS, HEAD_COUNT * HEAD_DIM)
    decode_out = jnp.dot(decode_hidden, out_weight, preferred_element_type=jnp.float32).astype(jnp.bfloat16).reshape(rows, STEPS, D)
    return (prefill_out, decode_out)
```

```python
import functools

import jax
import jax.numpy as jnp
from jax import lax
from jax.experimental import pallas as pl
from jax.experimental.pallas import tpu as pltpu
from jax.sharding import PartitionSpec as P

HEAD_DIM = 128
EPSILON = 1e-06
NEGATIVE = -1e30
HIGH = lax.Precision.HIGHEST
CHUNKS = 2
VMEM_BYTES = 40 * 2**20
F32 = jnp.float32
BF16 = jnp.bfloat16
NT = (((1,), (1,)), ((), ()))
TN = (((0,), (0,)), ((), ()))


def params():
    return pltpu.CompilerParams(vmem_limit_bytes=VMEM_BYTES)


def cost(flops, moved, exps=0):
    return pl.CostEstimate(flops=int(flops), bytes_accessed=int(moved), transcendentals=int(exps))


def normalize(array):
    return array * lax.rsqrt(jnp.mean(array * array, axis=-1, keepdims=True) + EPSILON)


def lower_ones(length):
    rows = lax.broadcasted_iota(jnp.int32, (length, length), 0)
    cols = lax.broadcasted_iota(jnp.int32, (length, length), 1)
    return rows >= cols


def decay_columns(rate, lower):
    return -lax.dot_general(lower.astype(F32), rate, NT, precision=HIGH, preferred_element_type=F32)


def decay_rows(rate, lower):
    return -lax.dot_general(rate, lower.astype(F32), NT, precision=HIGH, preferred_element_type=F32)


def head_slice(index):
    return slice(index * HEAD_DIM, (index + 1) * HEAD_DIM)


def halves(array):
    top = array.astype(BF16)
    return top, (array - top.astype(F32)).astype(BF16)


def state_kernel(k_ref, v_ref, rate_ref, own_ref):
    length = k_ref.shape[0]
    columns = decay_columns(rate_ref[...], lower_ones(length))
    factor = jnp.exp(columns[length - 1 :, :] - columns)
    for i in range(own_ref.shape[0]):
        values = v_ref[:, head_slice(i)]
        weighted = k_ref[:, head_slice(i)].astype(F32) * factor[:, i : i + 1]
        top, rest = halves(weighted)
        own_ref[i] = lax.dot_general(top, values, TN, preferred_element_type=F32) + lax.dot_general(
            rest, values, TN, preferred_element_type=F32
        )


def local_kernel(q_ref, k_ref, v_ref, rate_ref, local_ref):
    lower = lower_ones(q_ref.shape[0])
    rate = rate_ref[...]
    columns = decay_columns(rate, lower)
    rows = decay_rows(rate, lower)
    for i in range(rate.shape[0]):
        at = head_slice(i)
        scores = lax.dot_general(q_ref[:, at], k_ref[:, at], NT, preferred_element_type=F32)
        decay = jnp.exp(jnp.where(lower, columns[:, i : i + 1] - rows[i : i + 1, :], NEGATIVE))
        weights = (scores * decay).astype(BF16)
        local_ref[:, at] = jnp.dot(weights, v_ref[:, at], preferred_element_type=F32)


def hidden_kernel(q_ref, local_ref, state_ref, rate_ref, decode_ref, hidden_ref):
    length = q_ref.shape[0]
    factor = jnp.exp(decay_columns(rate_ref[...], lower_ones(length)))
    for i in range(state_ref.shape[0]):
        at = head_slice(i)
        inter = jnp.dot(q_ref[:, at], state_ref[i], preferred_element_type=F32)
        attended = local_ref[:, at] + inter * factor[:, i : i + 1]
        hidden_ref[:length, at] = normalize(attended).astype(BF16)
    hidden_ref[length:, :] = decode_ref[...]


def start_kernel(q_ref, own_ref, scale_ref, out_ref):
    for i in range(own_ref.shape[0]):
        at = head_slice(i)
        top, rest = halves(own_ref[i])
        queries = q_ref[:, at]
        terms = jnp.dot(queries, top, preferred_element_type=F32) + jnp.dot(
            queries, rest, preferred_element_type=F32
        )
        out_ref[:, at] = (terms * scale_ref[i : i + 1, :]).astype(BF16)


def project_kernel(place_ref, hidden_ref, weight_ref, out_ref):
    out_ref[...] = jnp.dot(
        hidden_ref[...], weight_ref[...], preferred_element_type=F32
    ).astype(out_ref.dtype)


def finish_kernel(own_p, ax_p, ay_p, bx_p, by_p, own_d, ax_d, ay_d, bx_d, by_d, prefill_ref, decode_ref):
    width = own_p.shape[2]
    rows = decode_ref.shape[0]

    def total(own, x_ref, y_ref, half):
        return own[half] + x_ref[0].astype(F32) + y_ref[0].astype(F32)

    prefill_ref[:, :width] = total(own_p, ax_p, ay_p, 0).astype(BF16)
    prefill_ref[:, width:] = total(own_p, bx_p, by_p, 1).astype(BF16)
    decode_ref[:, :width] = total(own_d, ax_d, ay_d, 0)[:rows].astype(BF16)
    decode_ref[:, width:] = total(own_d, bx_d, by_d, 1)[:rows].astype(BF16)


def swap(array, axis, size, bit):
    return lax.ppermute(array, axis, [(i, i ^ bit) for i in range(size)])


def body(
    prefill_query,
    prefill_key,
    prefill_value,
    prefill_rate,
    out_weight,
    decode_query,
    decode_key,
    decode_value,
    decode_rate,
    prompt_of_row,
    *,
    groups,
    reps,
    parts,
):
    length = prefill_query.shape[1]
    features = prefill_query.shape[2]
    heads = prefill_rate.shape[1]
    rows_here, steps = decode_query.shape[0], decode_query.shape[1]
    d_rows = rows_here * steps
    d_pad = -(-d_rows // 16) * 16
    total_rows = length + d_pad
    group = lax.axis_index("ctx")
    rep = lax.axis_index("rep")

    block_heads = 4 if heads % 4 == 0 else heads
    blocks = heads // block_heads
    wide = block_heads * HEAD_DIM
    rate = prefill_rate.reshape(blocks, block_heads, length)
    spec_tokens = pl.BlockSpec((None, length, wide), lambda i: (0, 0, i))
    spec_rate = pl.BlockSpec((None, block_heads, length), lambda i: (i, 0, 0))
    spec_state = pl.BlockSpec((block_heads, HEAD_DIM, HEAD_DIM), lambda i: (i, 0, 0))
    spec_local = pl.BlockSpec((length, wide), lambda i: (0, i))
    token_bytes = length * features * 2
    state_bytes = heads * HEAD_DIM * HEAD_DIM * 4

    own = pl.pallas_call(
        state_kernel,
        grid=(blocks,),
        in_specs=[spec_tokens, spec_tokens, spec_rate],
        out_specs=spec_state,
        out_shape=jax.ShapeDtypeStruct((heads, HEAD_DIM, HEAD_DIM), F32),
        compiler_params=params(),
        cost_estimate=cost(4 * length * features * HEAD_DIM, 2 * token_bytes + state_bytes),
        name="own_state",
    )(prefill_key, prefill_value, rate)
    log_total = -jnp.sum(prefill_rate[0], axis=-1)
    keep = jnp.exp(log_total)

    queries = decode_query.reshape(d_rows, features)
    log_top = log_total.astype(BF16)
    log_left = log_total - log_top.astype(F32)
    log_mid = log_left.astype(BF16)
    log_low = (log_left - log_mid.astype(F32)).astype(BF16)
    row_prompt = jnp.repeat(prompt_of_row, steps).astype(BF16)
    facts = jnp.concatenate([log_top, log_mid, log_low, row_prompt])
    facts = jnp.pad(facts, (0, features - facts.shape[0]))[None]
    message = jnp.concatenate([queries, facts], axis=0)
    message = jnp.pad(message, ((0, (-message.shape[0]) % 16), (0, 0)))
    slots = message[None]
    bit = 1
    while bit < groups:
        slots = jnp.concatenate([slots, swap(slots, "ctx", groups, bit)], axis=0)
        bit *= 2
    slot_facts = slots[:, d_rows, :].astype(F32)
    slot_logs = (
        slot_facts[:, :heads] + slot_facts[:, heads : 2 * heads] + slot_facts[:, 2 * heads : 3 * heads]
    )
    slot_prompts = slot_facts[:, 3 * heads : 3 * heads + d_rows]
    slot_groups = jnp.arange(groups, dtype=jnp.int32) ^ group
    later = jnp.sum(jnp.where((slot_groups > group)[:, None], slot_logs, 0.0), axis=0)
    scale = jnp.broadcast_to(jnp.exp(later)[:, None], (heads, HEAD_DIM))
    slot_queries = slots[:, :d_rows, :]
    both = jnp.concatenate([slot_queries[None], swap(slot_queries, "rep", reps, 1)[None]], axis=0)
    all_rows = reps * groups * d_rows
    part = pl.pallas_call(
        start_kernel,
        grid=(blocks,),
        in_specs=[
            pl.BlockSpec((all_rows, wide), lambda i: (0, i)),
            spec_state,
            pl.BlockSpec((None, block_heads, HEAD_DIM), lambda i: (i, 0, 0)),
        ],
        out_specs=pl.BlockSpec((all_rows, wide), lambda i: (0, i)),
        out_shape=jax.ShapeDtypeStruct((all_rows, features), BF16),
        compiler_params=params(),
        cost_estimate=cost(4 * all_rows * features * HEAD_DIM, state_bytes + all_rows * features * 4),
        name="decode_start",
    )(both.reshape(all_rows, features), own, scale.reshape(blocks, block_heads, HEAD_DIM))
    part = part.reshape(reps, groups, d_rows, features)
    other = swap(part[1], "rep", reps, 1)
    mine = (slot_prompts == rep.astype(F32))[:, :, None]
    base = jnp.where(mine, part[0], other)
    bit = groups // 2
    while bit >= 1:
        got = swap(base[bit:], "ctx", groups, bit)
        base = (base[:bit].astype(F32) + got.astype(F32)).astype(BF16 if bit > 1 else F32)
        bit //= 2

    def split_heads(array):
        return array.reshape(rows_here, steps, heads, HEAD_DIM).astype(F32)

    d_query, d_key, d_value = split_heads(decode_query), split_heads(decode_key), split_heads(decode_value)
    d_cumul = jnp.cumsum(-decode_rate, axis=-1)
    step_mask = jnp.arange(steps)[:, None] >= jnp.arange(steps)[None, :]
    d_decay = jnp.exp(
        jnp.where(step_mask, d_cumul[..., :, None] - d_cumul[..., None, :], NEGATIVE)
    )
    d_scores = jnp.einsum("rthd,rshd->rhts", d_query, d_key, precision=HIGH)
    d_intra = jnp.einsum("rhts,rshe->rthe", d_scores * d_decay, d_value, precision=HIGH)
    d_base = split_heads(base[0]) * jnp.exp(d_cumul).transpose(0, 2, 1)[..., None]
    decode_hidden = normalize(d_base + d_intra).astype(BF16).reshape(d_rows, features)
    decode_hidden = jnp.pad(decode_hidden, ((0, d_pad - d_rows), (0, 0)))

    chunks = CHUNKS if heads % CHUNKS == 0 else 1
    span = heads // chunks

    def pick(array, chunk):
        if isinstance(chunk, int):
            return array[:span]
        return lax.dynamic_slice_in_dim(array, jnp.clip(chunk, 0, chunks - 1) * span, span, 0)

    received = []
    for step in range(chunks + groups - 2):
        chunk = 0 if step == 0 else step - group
        value = pick(own, chunk)
        if received:
            value = value + pick(keep, chunk)[:, None, None] * received[-1].astype(F32)
        received.append(
            lax.ppermute(value.astype(BF16), "ctx", [(i, i + 1) for i in range(groups - 1)])
        )
    entering = []
    for chunk in range(chunks):
        state = received[chunk]
        for g in range(2, groups):
            state = jnp.where(group == g, received[chunk + g - 1], state)
        entering.append(state)
    entering = jnp.concatenate(entering, axis=0)

    local = pl.pallas_call(
        local_kernel,
        grid=(blocks,),
        in_specs=[spec_tokens, spec_tokens, spec_tokens, spec_rate],
        out_specs=spec_local,
        out_shape=jax.ShapeDtypeStruct((length, features), F32),
        compiler_params=params(),
        cost_estimate=cost(
            4 * length * length * features, 5 * token_bytes, heads * length * length
        ),
        name="local_attention",
    )(prefill_query, prefill_key, prefill_value, rate)

    hidden = pl.pallas_call(
        hidden_kernel,
        grid=(blocks,),
        in_specs=[
            spec_tokens,
            spec_local,
            spec_state,
            spec_rate,
            pl.BlockSpec((d_pad, wide), lambda i: (0, i)),
        ],
        out_specs=pl.BlockSpec((total_rows, wide), lambda i: (0, i)),
        out_shape=jax.ShapeDtypeStruct((total_rows, features), BF16),
        compiler_params=params(),
        cost_estimate=cost(2 * length * features * HEAD_DIM, 4 * token_bytes + state_bytes // 2),
        name="hidden",
    )(prefill_query, local, entering, rate, decode_hidden)

    out_columns = out_weight.shape[1]
    if parts != 4 or (out_columns // parts) % 512 != 0:
        terms = jnp.dot(hidden, out_weight, preferred_element_type=F32)
        summed = lax.psum_scatter(terms, "head", scatter_dimension=1, tiled=True)
        prefill_out = summed[:length].astype(BF16)[None]
        decode_out = summed[length : length + d_rows].astype(BF16)
        return prefill_out, decode_out.reshape(rows_here, steps, -1)

    half = out_columns // parts // 2
    tiles = 2
    tile = half // tiles
    me = lax.axis_index("head")
    x_side, y_side, far = me ^ 1, me ^ 2, me ^ 3

    def project(places, dtype):
        count = len(places)
        return pl.pallas_call(
            project_kernel,
            grid_spec=pltpu.PrefetchScalarGridSpec(
                num_scalar_prefetch=1,
                grid=(count, tiles),
                in_specs=[
                    pl.BlockSpec((total_rows, features), lambda i, j, place: (0, 0)),
                    pl.BlockSpec((features, tile), lambda i, j, place: (0, place[i] * tiles + j)),
                ],
                out_specs=pl.BlockSpec((None, total_rows, tile), lambda i, j, place: (i, 0, j)),
            ),
            out_shape=jax.ShapeDtypeStruct((count, total_rows, half), dtype),
            compiler_params=params(),
            cost_estimate=cost(
                2 * total_rows * features * half * count,
                count * half * (features * 2 + total_rows * 4) + total_rows * features * 2,
            ),
            name="project",
        )(jnp.stack(places).astype(jnp.int32), hidden, out_weight)

    far_a = swap(project([far * 2], BF16), "head", parts, 1)
    far_b = swap(project([far * 2 + 1], BF16), "head", parts, 2)
    x_a = swap(project([x_side * 2], BF16), "head", parts, 1)
    y_b = swap(project([y_side * 2 + 1], BF16), "head", parts, 2)
    relay = project([y_side * 2, x_side * 2 + 1], F32)
    mine_f = project([me * 2, me * 2 + 1], F32)
    y_a = swap((relay[:1] + far_a.astype(F32)).astype(BF16), "head", parts, 2)
    x_b = swap((relay[1:] + far_b.astype(F32)).astype(BF16), "head", parts, 1)

    row_tile = 64 if length % 64 == 0 else length
    def at_rows(count):
        return pl.BlockSpec((count, row_tile, half), lambda i: (0, i, 0))

    def at_tail(count):
        return pl.BlockSpec((count, 16, half), lambda i: (0, length // 16, 0))

    if d_pad != 16 or length % 16 != 0:
        both_halves = [
            mine_f[0] + x_a[0].astype(F32) + y_a[0].astype(F32),
            mine_f[1] + x_b[0].astype(F32) + y_b[0].astype(F32),
        ]
        summed = jnp.concatenate(both_halves, axis=1).astype(BF16)
        return summed[:length][None], summed[length : length + d_rows].reshape(rows_here, steps, -1)
    pieces = (mine_f, x_a, y_a, x_b, y_b)
    prefill_out, decode_out = pl.pallas_call(
        finish_kernel,
        grid=(length // row_tile,),
        in_specs=[at_rows(p.shape[0]) for p in pieces] + [at_tail(p.shape[0]) for p in pieces],
        out_specs=[
            pl.BlockSpec((None, row_tile, 2 * half), lambda i: (0, i, 0)),
            pl.BlockSpec((d_rows, 2 * half), lambda i: (0, 0)),
        ],
        out_shape=[
            jax.ShapeDtypeStruct((1, length, 2 * half), BF16),
            jax.ShapeDtypeStruct((d_rows, 2 * half), BF16),
        ],
        compiler_params=params(),
        cost_estimate=cost(6 * total_rows * half, 20 * total_rows * half),
        name="finish",
    )(*pieces, *pieces)
    return prefill_out, decode_out.reshape(rows_here, steps, -1)


def solution(mesh):
    return jax.shard_map(
        functools.partial(
            body, groups=mesh.shape["ctx"], reps=mesh.shape["rep"], parts=mesh.shape["head"]
        ),
        mesh=mesh,
        in_specs=(
            P("rep", "ctx", "head"),
            P("rep", "ctx", "head"),
            P("rep", "ctx", "head"),
            P("rep", "head", "ctx"),
            P("head", None),
            P(("ctx", "rep"), None, "head"),
            P(("ctx", "rep"), None, "head"),
            P(("ctx", "rep"), None, "head"),
            P(("ctx", "rep"), "head", None),
            P(("ctx", "rep")),
        ),
        out_specs=(P("rep", "ctx", "head"), P(("ctx", "rep"), None, "head")),
        check_vma=False,
    )
```

```python
import functools

import jax
import jax.numpy as jnp
from jax import lax
from jax.experimental import pallas as pl
from jax.experimental.pallas import tpu as pltpu
from jax.sharding import PartitionSpec as P

HEAD_DIM = 128
EPSILON = 1e-06
NEGATIVE = -1e30
HIGH = lax.Precision.HIGHEST
CHUNKS = 4
LAG = 2
VMEM_BYTES = 16 * 2**20
F32 = jnp.float32
BF16 = jnp.bfloat16
NT = (((1,), (1,)), ((), ()))
TN = (((0,), (0,)), ((), ()))


def params():
    return pltpu.CompilerParams(vmem_limit_bytes=VMEM_BYTES)


def cost(flops, moved, exps=0):
    return pl.CostEstimate(flops=int(flops), bytes_accessed=int(moved), transcendentals=int(exps))


def normalize(array):
    return array * lax.rsqrt(jnp.mean(array * array, axis=-1, keepdims=True) + EPSILON)


def lower_ones(length):
    rows = lax.broadcasted_iota(jnp.int32, (length, length), 0)
    cols = lax.broadcasted_iota(jnp.int32, (length, length), 1)
    return rows >= cols


def decay_columns(rate, lower):
    return -lax.dot_general(lower.astype(F32), rate, NT, precision=HIGH, preferred_element_type=F32)


def decay_rows(rate, lower):
    return -lax.dot_general(rate, lower.astype(F32), NT, precision=HIGH, preferred_element_type=F32)


def identity(size):
    rows = lax.broadcasted_iota(jnp.int32, (size, size), 0)
    cols = lax.broadcasted_iota(jnp.int32, (size, size), 1)
    return rows, cols


def head_slice(index):
    return slice(index * HEAD_DIM, (index + 1) * HEAD_DIM)


def halves(array):
    top = array.astype(BF16)
    return top, (array - top.astype(F32)).astype(BF16)

VMEM = pl.BlockSpec(memory_space=pltpu.VMEM)
SMEM = pl.BlockSpec(memory_space=pltpu.SMEM)
ANY = pl.BlockSpec(memory_space=pl.ANY)
HBM = pl.BlockSpec(memory_space=pltpu.HBM)


def call(kernel, name, in_specs, out_shape, scratch=(), estimate=None, out_specs=None):
    if out_specs is None:
        out_specs = jax.tree.map(lambda _: VMEM, out_shape)
    return pl.pallas_call(
        kernel,
        in_specs=in_specs,
        out_specs=out_specs,
        out_shape=out_shape,
        scratch_shapes=list(scratch),
        compiler_params=params(),
        cost_estimate=estimate,
        name=name,
    )


def sds(shape, dtype):
    return jax.ShapeDtypeStruct(shape, dtype)


def state_kernel(span, k_hbm, v_hbm, rate_ref, own_ref, first_ref, second_ref, log_ref, col_ref, row_ref, k_ref, v_ref, sems):
    heads = own_ref.shape[0]
    wide = span * HEAD_DIM
    copies = []
    for c in range(heads // span):
        at = pl.ds(c * wide, wide)
        copies.append(pltpu.make_async_copy(k_hbm.at[0, :, at], k_ref.at[:, at], sems.at[0, c]))
        copies.append(pltpu.make_async_copy(v_hbm.at[0, :, at], v_ref.at[:, at], sems.at[1, c]))
    for copy in copies:
        copy.start()
    length = k_ref.shape[0]
    rate = rate_ref[0]
    lower = lower_ones(length)
    columns = decay_columns(rate, lower)
    col_ref[...] = columns
    row_ref[...] = decay_rows(rate, lower)
    total = columns[length - 1 :, :]
    factor = jnp.exp(total - columns)
    for i in range(heads):
        if i % span == 0:
            copies[2 * (i // span)].wait()
            copies[2 * (i // span) + 1].wait()
        at = head_slice(i)
        values = v_ref[:, at]
        weighted = k_ref[:, at].astype(F32) * factor[:, i : i + 1]
        top, rest = halves(weighted)
        both = lax.dot_general(
            jnp.concatenate([top, rest], axis=1), values, TN, preferred_element_type=F32
        )
        state = both[:HEAD_DIM] + both[HEAD_DIM:]
        own_ref[i] = state
        if i < span:
            first_ref[i] = state.astype(BF16)
        elif i < 2 * span:
            second_ref[i - span] = state.astype(BF16)
        log_ref[:, at] = jnp.broadcast_to(total[:, i : i + 1], (1, HEAD_DIM))


def chain_kernel(step, place_ref, own_ref, log_ref, got_ref, *rest):
    out_ref = rest[-1]
    span = out_ref.shape[0]
    chunks = own_ref.shape[0] // span
    chunk = jnp.clip(step - LAG * place_ref[0], 0, chunks - 1)
    wide = span * HEAD_DIM
    keep = jnp.exp(log_ref[:, pl.ds(pl.multiple_of(chunk * wide, HEAD_DIM), wide)])
    for i in range(span):
        out_ref[i] = (
            own_ref[chunk * span + i] + keep[:, head_slice(i)] * got_ref[i].astype(F32)
        ).astype(BF16)


def local_kernel(first, q_ref, k_ref, v_ref, col_ref, row_ref, *rest):
    local_ref = rest[-1]
    lower = lower_ones(q_ref.shape[1])
    for i in range(local_ref.shape[1] // HEAD_DIM):
        h = first + i
        at = head_slice(h)
        scores = lax.dot_general(q_ref[0, :, at], k_ref[:, at], NT, preferred_element_type=F32)
        decay = jnp.exp(
            jnp.where(lower, col_ref[:, h : h + 1] - row_ref[h : h + 1, :], NEGATIVE)
        )
        weights = (scores * decay).astype(BF16)
        local_ref[:, head_slice(i)] = jnp.dot(weights, v_ref[:, at], preferred_element_type=F32)


def hidden_kernel(chunks, groups, place_ref, q_ref, col_ref, decode_ref, *rest):
    locals_ref, got, hidden_ref = rest[:chunks], rest[chunks:-1], rest[-1]
    length = q_ref.shape[1]
    factor = jnp.exp(col_ref[...])
    span = got[0].shape[0]
    group = place_ref[0]
    for chunk in range(chunks):
        for i in range(span):
            state = got[chunk][i]
            for g in range(2, groups):
                state = jnp.where(group == g, got[chunk + LAG * (g - 1)][i], state)
            h = chunk * span + i
            at = head_slice(h)
            inter = jnp.dot(q_ref[0, :, at], state, preferred_element_type=F32)
            attended = locals_ref[chunk][:, head_slice(i)] + inter * factor[:, h : h + 1]
            hidden_ref[:length, at] = normalize(attended).astype(BF16)
    hidden_ref[length:, :] = decode_ref[...]


def flat_rows(ref, rows_ref):
    rows, steps = ref.shape[0], ref.shape[1]
    for r in range(rows):
        rows_ref[r * steps : (r + 1) * steps, :] = ref[r].astype(F32)


def message_kernel(q_ref, log_ref, prompt_ref, *rest):
    out_ref, rows_ref = rest[-2:]
    rows, steps = q_ref.shape[0], q_ref.shape[1]
    d_rows = rows * steps
    features = q_ref.shape[2]
    rows_ref[...] = jnp.zeros_like(rows_ref)
    flat_rows(q_ref, rows_ref)
    log = log_ref[...]
    top = log.astype(BF16).astype(F32)
    mid = (log - top).astype(BF16).astype(F32)
    rows_ref[d_rows : d_rows + 1, :] = top
    rows_ref[d_rows + 1 : d_rows + 2, :] = mid
    rows_ref[d_rows + 2 : d_rows + 3, :] = log - top - mid
    lane = lax.broadcasted_iota(jnp.int32, (1, features), 1)
    prompts = jnp.zeros((1, features), F32)
    for r in range(rows):
        here = (lane >= r * steps) & (lane < (r + 1) * steps)
        prompts = jnp.where(here, prompt_ref[r].astype(F32), prompts)
    rows_ref[d_rows + 3 : d_rows + 4, :] = prompts
    out_ref[...] = rows_ref[...].astype(BF16)


def start_kernel(groups, d_rows, place_ref, near_ref, far_ref, own_ref, *rest):
    near_out, far_out = rest[-2:]
    unit = near_ref.shape[0] // groups
    group = place_ref[0]
    later = jnp.zeros((1, near_ref.shape[1]), F32)
    for j in range(1, groups):
        facts = near_ref[j * unit : (j + 1) * unit, :].astype(F32)[d_rows : d_rows + 3]
        facts = jnp.sum(facts, axis=0, keepdims=True)
        later = later + jnp.where((group ^ j) > group, facts, 0.0)
    scale = jnp.exp(later)

    def strip(terms):
        return jnp.concatenate(
            [terms[j * unit : j * unit + d_rows] for j in range(groups)], axis=0
        )

    for i in range(own_ref.shape[0]):
        at = head_slice(i)
        top, low = halves(own_ref[i])
        both = jnp.concatenate([top, low], axis=1)
        for source, target in ((near_ref, near_out), (far_ref, far_out)):
            terms = jnp.dot(source[:, at], both, preferred_element_type=F32)
            terms = (terms[:, :HEAD_DIM] + terms[:, HEAD_DIM:]) * scale[:, at]
            target[:, at] = strip(terms).astype(target.dtype)


def select_kernel(groups, d_rows, place_ref, near_ref, mine_ref, other_ref, *rest):
    outs = rest[-groups:]
    unit = near_ref.shape[0] // groups
    rep = place_ref[1].astype(F32)
    wide = -(-d_rows // HEAD_DIM) * HEAD_DIM
    rows = lax.broadcasted_iota(jnp.int32, (d_rows, wide), 0)
    cols = lax.broadcasted_iota(jnp.int32, (d_rows, wide), 1)
    other = other_ref[...].astype(F32)
    for j in range(groups):
        facts = near_ref[j * unit : (j + 1) * unit, :wide].astype(F32)[d_rows + 3 : d_rows + 4]
        prompt = jnp.sum(jnp.where(rows == cols, facts, 0.0), axis=1, keepdims=True)
        at = slice(j * d_rows, (j + 1) * d_rows)
        picked = jnp.where(prompt == rep, mine_ref[at], other[at])
        outs[j][...] = picked.astype(outs[j].dtype)


def decode_kernel(groups, q_ref, k_ref, v_ref, rate_ref, base_ref, *rest):
    got = rest[: groups - 1]
    out_ref, q_rows, k_rows, v_rows, rate_rows = rest[-5:]
    steps = q_ref.shape[1]
    d_rows = q_rows.shape[0]
    flat_rows(q_ref, q_rows)
    flat_rows(k_ref, k_rows)
    flat_rows(v_ref, v_rows)
    flat_rows(rate_ref, rate_rows)
    rows, cols = identity(d_rows)
    seen = (rows // steps == cols // steps) & (rows >= cols)
    ones = seen.astype(F32)
    rates = rate_rows[...]
    down = -jnp.dot(ones, rates, precision=HIGH, preferred_element_type=F32)
    across = -lax.dot_general(
        rates, ones, (((0,), (1,)), ((), ())), precision=HIGH, preferred_element_type=F32
    )
    grow = jnp.exp(down)
    out_ref[...] = jnp.zeros_like(out_ref)
    for i in range(rates.shape[1]):
        at = head_slice(i)
        scores = lax.dot_general(
            q_rows[:, at], k_rows[:, at], NT, precision=HIGH, preferred_element_type=F32
        )
        decay = jnp.exp(jnp.where(seen, down[:, i : i + 1] - across[i : i + 1, :], NEGATIVE))
        intra = jnp.dot(scores * decay, v_rows[:, at], precision=HIGH, preferred_element_type=F32)
        base = base_ref[:, at]
        for ref in got:
            base = base + ref[:, at].astype(F32)
        q_rows[:, at] = normalize(base * grow[:, i : i + 1] + intra)
    pad = out_ref.shape[0] - d_rows
    value = q_rows[...]
    if pad:
        value = jnp.concatenate([value, jnp.zeros((pad, value.shape[1]), F32)], axis=0)
    out_ref[...] = value.astype(BF16)


def project_kernel(pieces, place_ref, hidden_ref, weight_ref, *outs):
    half = outs[0].shape[1]
    rows = hidden_ref[...]
    for (bits, part), out_ref in zip(pieces, outs):
        column = pl.multiple_of(((place_ref[2] ^ bits) * 2 + part) * half, HEAD_DIM)
        out_ref[...] = jnp.dot(
            rows, weight_ref[:, pl.ds(column, half)], preferred_element_type=F32
        ).astype(out_ref.dtype)


def relay_kernel(own_ref, got_ref, out_ref):
    out_ref[...] = (own_ref[...] + got_ref[...].astype(F32)).astype(BF16)


def finish_kernel(own_a, own_b, ax, ay, bx, by, prefill_hbm, decode_ref, out_ref, sems):
    width = own_a.shape[1]
    rows, steps = decode_ref.shape[0], decode_ref.shape[1]
    length = out_ref.shape[0]
    count = sems.shape[0]
    size = length // count
    copies = []
    for c in range(count):
        at = slice(c * size, (c + 1) * size)
        for at_cols, own, x_ref, y_ref in ((0, own_a, ax, ay), (width, own_b, bx, by)):
            total = own[at] + x_ref[at].astype(F32) + y_ref[at].astype(F32)
            out_ref[at, at_cols : at_cols + width] = total.astype(BF16)
        copy = pltpu.make_async_copy(
            out_ref.at[pl.ds(c * size, size)], prefill_hbm.at[0, pl.ds(c * size, size)], sems.at[c]
        )
        copy.start()
        copies.append(copy)
    for at_cols, own, x_ref, y_ref in ((0, own_a, ax, ay), (width, own_b, bx, by)):
        tail = own[length:] + x_ref[length:].astype(F32) + y_ref[length:].astype(F32)
        tail = tail.astype(BF16).astype(F32)
        for r in range(rows):
            decode_ref[r, :, at_cols : at_cols + width] = tail[r * steps : (r + 1) * steps].astype(BF16)
    for copy in copies:
        copy.wait()


def swap(array, axis, size, bit):
    return lax.ppermute(array, axis, [(i, i ^ bit) for i in range(size)])


def body(
    prefill_query,
    prefill_key,
    prefill_value,
    prefill_rate,
    out_weight,
    decode_query,
    decode_key,
    decode_value,
    decode_rate,
    prompt_of_row,
    *,
    groups,
    reps,
    parts,
):
    length = prefill_query.shape[1]
    features = prefill_query.shape[2]
    heads = prefill_rate.shape[1]
    rows_here, steps = decode_query.shape[0], decode_query.shape[1]
    d_rows = rows_here * steps
    d_pad = -(-d_rows // 16) * 16
    unit = -(-(d_rows + 4) // 16) * 16
    total_rows = length + d_pad
    place = jnp.stack([lax.axis_index("ctx"), lax.axis_index("rep"), lax.axis_index("head")])
    place = place.astype(jnp.int32)
    chunks = CHUNKS if heads % CHUNKS == 0 else heads
    span = heads // chunks
    wide = span * HEAD_DIM
    chunk_shape = (span, HEAD_DIM, HEAD_DIM)

    own, first, second, log_row, columns, rows, keys, values = call(
        functools.partial(state_kernel, span),
        "own_state",
        [HBM, HBM, VMEM],
        [
            sds((heads, HEAD_DIM, HEAD_DIM), F32),
            sds(chunk_shape, BF16),
            sds(chunk_shape, BF16),
            sds((1, features), F32),
            sds((length, heads), F32),
            sds((heads, length), F32),
            pltpu.VMEM((length, features), BF16),
            pltpu.VMEM((length, features), BF16),
        ],
        [pltpu.SemaphoreType.DMA((2, chunks))],
        cost(4 * length * features * HEAD_DIM, 4 * length * features),
    )(prefill_key, prefill_value, prefill_rate)

    def message(*after):
        return call(
            message_kernel,
            "decode_message",
            [VMEM, VMEM, SMEM] + [ANY] * len(after),
            sds((unit, features), BF16),
            [pltpu.VMEM((unit, features), F32)],
            cost(unit * features, unit * features * 8),
        )(decode_query, log_row, prompt_of_row, *after)

    def local(chunk, *after):
        return call(
            functools.partial(local_kernel, chunk * span),
            "local_attention",
            [VMEM] * 5 + [ANY] * len(after),
            sds((length, wide), F32),
            (),
            cost(4 * length * length * wide, 6 * length * wide, span * length * length),
        )(prefill_query, keys, values, columns, rows, *after)

    def start_terms(near, far, *after):
        return call(
            functools.partial(start_kernel, groups, d_rows),
            "decode_start",
            [SMEM, VMEM, VMEM, VMEM] + [ANY] * len(after),
            [sds((groups * d_rows, features), F32), sds((groups * d_rows, features), BF16)],
            (),
            cost(8 * groups * unit * features * HEAD_DIM, heads * HEAD_DIM * HEAD_DIM * 4),
        )(place, near, far, own, *after)

    def select_terms(near, mine, other, *after):
        return call(
            functools.partial(select_kernel, groups, d_rows),
            "decode_select",
            [SMEM, VMEM, VMEM, VMEM] + [ANY] * len(after),
            [sds((d_rows, features), F32)] + [sds((d_rows, features), BF16)] * (groups - 1),
            (),
            cost(groups * d_rows * features, groups * d_rows * features * 8),
        )(place, near, mine, other, *after)

    def decode_rows(base, got, *after):
        flat = pltpu.VMEM((d_rows, features), F32)
        return call(
            functools.partial(decode_kernel, groups),
            "decode_rows",
            [VMEM] * (5 + len(got)) + [ANY] * len(after),
            sds((d_pad, features), BF16),
            [flat, flat, flat, pltpu.VMEM((d_rows, heads), F32)],
            cost(4 * d_rows * features * d_rows, d_rows * features * 20),
        )(
            decode_query,
            decode_key,
            decode_value,
            jnp.transpose(decode_rate, (0, 2, 1)),
            base,
            *got,
            *after,
        )

    right = [(i, i + 1) for i in range(groups - 1)]
    steps_all = chunks + LAG * (groups - 2)
    received, locals_done, slot = [], [], {}

    def side_work(step, after):
        made = []
        if step == 0:
            slot["message"] = message(*after)
            slot["ctx"] = [swap(slot["message"], "ctx", groups, j) for j in range(1, groups)]
            made.append(slot["message"])
        if step == 2:
            slot["near"] = jnp.concatenate([slot["message"]] + slot["ctx"], axis=0)
            slot["far"] = swap(slot["near"], "rep", reps, 1)
        if step == 3:
            slot["mine"], away = start_terms(slot["near"], slot["far"], *after)
            slot["other"] = swap(away, "rep", reps, 1)
            made.append(slot["mine"])
        if step == 5:
            base, *terms = select_terms(slot["near"], slot["mine"], slot["other"], *after)
            slot["base"] = base
            slot["got"] = [
                swap(term, "ctx", groups, j) for j, term in zip(range(1, groups), terms)
            ]
            made.append(base)
        return made

    local_at = {1: 0, 2: 1, 4: 2, 6: 3}
    for step in range(steps_all):
        if step == 0:
            value = first
        elif step < LAG:
            value = second if chunks > 1 else first
        else:
            after = slot.pop("after", [])
            value = call(
                functools.partial(chain_kernel, step),
                "chain",
                [SMEM, VMEM, VMEM, VMEM] + [ANY] * len(after),
                sds(chunk_shape, BF16),
                (),
                cost(2 * span * HEAD_DIM * HEAD_DIM, 8 * span * HEAD_DIM * HEAD_DIM),
            )(place, own, log_row, received[step - LAG], *after)
        received.append(lax.ppermute(value, "ctx", right))
        ready = [received[step - LAG]] if step >= LAG else []
        made = side_work(step, ready)
        if step in local_at and local_at[step] < chunks:
            locals_done.append(local(len(locals_done), *ready))
            made.append(locals_done[-1])
        slot["after"] = made
    while len(locals_done) < chunks:
        locals_done.append(local(len(locals_done)))
    if "message" not in slot:
        side_work(0, [])
    for step, name in ((2, "near"), (3, "mine"), (5, "base")):
        if name not in slot:
            side_work(step, [])
    decode_hidden = decode_rows(slot["base"], slot["got"])

    hidden = call(
        functools.partial(hidden_kernel, chunks, groups),
        "hidden",
        [SMEM] + [VMEM] * (3 + chunks + len(received)),
        sds((total_rows, features), BF16),
        (),
        cost(2 * length * features * HEAD_DIM, 8 * length * features),
    )(place, prefill_query, columns, decode_hidden, *locals_done, *received)

    out_columns = out_weight.shape[1]
    if parts != 4 or (out_columns // parts) % 256 != 0 or length % 64 != 0:
        terms = jnp.dot(hidden, out_weight, preferred_element_type=F32)
        summed = lax.psum_scatter(terms, "head", scatter_dimension=1, tiled=True)
        prefill_out = summed[:length].astype(BF16)[None]
        decode_out = summed[length : length + d_rows].astype(BF16)
        return prefill_out, decode_out.reshape(rows_here, steps, -1)

    half = out_columns // parts // 2
    weight = pltpu.with_memory_space_constraint(out_weight, pltpu.VMEM)

    def project(pieces, dtype, *after):
        return call(
            functools.partial(project_kernel, pieces),
            "project",
            [SMEM, VMEM, VMEM],
            [sds((total_rows, half), dtype) for _ in pieces],
            (),
            cost(2 * total_rows * features * half * len(pieces), features * half * 2 * len(pieces)),
        )(place, hidden, weight)

    def relay(own_term, got):
        return call(
            relay_kernel,
            "relay",
            [VMEM, VMEM],
            sds((total_rows, half), BF16),
            (),
            cost(total_rows * half, total_rows * half * 8),
        )(own_term, got)

    far_a = swap(project([(3, 0)], BF16)[0], "head", parts, 1)
    far_b = swap(project([(3, 1)], BF16)[0], "head", parts, 2)
    x_a = swap(project([(1, 0)], BF16)[0], "head", parts, 1)
    y_b = swap(project([(2, 1)], BF16)[0], "head", parts, 2)
    pass_a, pass_b = project([(2, 0), (1, 1)], F32)
    own_a, own_b = project([(0, 0), (0, 1)], F32)
    y_a = swap(relay(pass_a, far_a), "head", parts, 2)
    x_b = swap(relay(pass_b, far_b), "head", parts, 1)

    prefill_out, decode_out = call(
        finish_kernel,
        "finish",
        [VMEM] * 6,
        [sds((1, length, 2 * half), BF16), sds((rows_here, steps, 2 * half), BF16)],
        [pltpu.VMEM((length, 2 * half), BF16), pltpu.SemaphoreType.DMA((4,))],
        cost(6 * total_rows * half, 20 * total_rows * half),
        out_specs=[HBM, VMEM],
    )(own_a, own_b, x_a, y_a, x_b, y_b)
    return prefill_out, decode_out


def solution(mesh):
    return jax.shard_map(
        functools.partial(
            body, groups=mesh.shape["ctx"], reps=mesh.shape["rep"], parts=mesh.shape["head"]
        ),
        mesh=mesh,
        in_specs=(
            P("rep", "ctx", "head"),
            P("rep", "ctx", "head"),
            P("rep", "ctx", "head"),
            P("rep", "head", "ctx"),
            P("head", None),
            P(("ctx", "rep"), None, "head"),
            P(("ctx", "rep"), None, "head"),
            P(("ctx", "rep"), None, "head"),
            P(("ctx", "rep"), "head", None),
            P(("ctx", "rep")),
        ),
        out_specs=(P("rep", "ctx", "head"), P(("ctx", "rep"), None, "head")),
        check_vma=False,
    )
```

```python
import functools

import jax
import jax.numpy as jnp
from jax import lax
from jax.experimental import pallas as pl
from jax.experimental.pallas import tpu as pltpu
from jax.sharding import PartitionSpec as P

HEAD_DIM = 128
EPSILON = 1e-06
NEGATIVE = -1e30
HIGH = lax.Precision.HIGHEST
CHUNKS = 4
LAG = 2
VMEM_BYTES = 12 * 2**20
PARTS_OF_COPY = 2
F32 = jnp.float32
BF16 = jnp.bfloat16
NT = (((1,), (1,)), ((), ()))
TN = (((0,), (0,)), ((), ()))


def params():
    return pltpu.CompilerParams(vmem_limit_bytes=VMEM_BYTES)


def cost(flops, moved, exps=0):
    return pl.CostEstimate(flops=int(flops), bytes_accessed=int(moved), transcendentals=int(exps))


def normalize(array):
    return array * lax.rsqrt(jnp.mean(array * array, axis=-1, keepdims=True) + EPSILON)


def lower_ones(length):
    rows = lax.broadcasted_iota(jnp.int32, (length, length), 0)
    cols = lax.broadcasted_iota(jnp.int32, (length, length), 1)
    return rows >= cols


def decay_columns(rate, lower):
    return -lax.dot_general(lower.astype(F32), rate, NT, precision=HIGH, preferred_element_type=F32)


def decay_rows(rate, lower):
    return -lax.dot_general(rate, lower.astype(F32), NT, precision=HIGH, preferred_element_type=F32)


def identity(size):
    rows = lax.broadcasted_iota(jnp.int32, (size, size), 0)
    cols = lax.broadcasted_iota(jnp.int32, (size, size), 1)
    return rows, cols


def head_slice(index):
    return slice(index * HEAD_DIM, (index + 1) * HEAD_DIM)


def halves(array):
    top = array.astype(BF16)
    return top, (array - top.astype(F32)).astype(BF16)

VMEM = pl.BlockSpec(memory_space=pltpu.VMEM)
SMEM = pl.BlockSpec(memory_space=pltpu.SMEM)
ANY = pl.BlockSpec(memory_space=pl.ANY)
HBM = pl.BlockSpec(memory_space=pltpu.HBM)


def call(kernel, name, in_specs, out_shape, scratch=(), estimate=None, out_specs=None):
    if out_specs is None:
        out_specs = jax.tree.map(lambda _: VMEM, out_shape)
    return pl.pallas_call(
        kernel,
        in_specs=in_specs,
        out_specs=out_specs,
        out_shape=out_shape,
        scratch_shapes=list(scratch),
        compiler_params=params(),
        cost_estimate=estimate,
        name=name,
    )


def sds(shape, dtype):
    return jax.ShapeDtypeStruct(shape, dtype)


def state_kernel(span, *refs):
    k_hbm, v_hbm, rate_hbm, q_hbm, dq_hbm, dk_hbm, dv_hbm = refs[:7]
    own_ref, first_ref, second_ref, log_ref, col_ref, row_ref = refs[7:13]
    k_ref, v_ref, q_ref, dq_ref, dk_ref, dv_ref = refs[13:19]
    rate_ref, sems, more = refs[19:]
    heads = own_ref.shape[0]
    wide = span * HEAD_DIM
    rate_copy = pltpu.make_async_copy(rate_hbm, rate_ref, more.at[0])
    rate_copy.start()
    copies = []
    for c in range(heads // span):
        at = pl.ds(c * wide, wide)
        copies.append(pltpu.make_async_copy(k_hbm.at[0, :, at], k_ref.at[:, at], sems.at[0, c]))
        copies.append(pltpu.make_async_copy(v_hbm.at[0, :, at], v_ref.at[:, at], sems.at[1, c]))
    others = [
        pltpu.make_async_copy(source, target, more.at[1 + i])
        for i, (source, target) in enumerate(
            ((dq_hbm, dq_ref), (dk_hbm, dk_ref), (dv_hbm, dv_ref), (q_hbm, q_ref))
        )
    ]
    for copy in copies + others:
        copy.start()
    length = k_ref.shape[0]
    lower = lower_ones(length)
    rate_copy.wait()
    rate = rate_ref[0]
    columns = decay_columns(rate, lower)
    col_ref[...] = columns
    row_ref[...] = decay_rows(rate, lower)
    total = columns[length - 1 :, :]
    factor = jnp.exp(total - columns)
    for i in range(heads):
        if i % span == 0:
            copies[2 * (i // span)].wait()
            copies[2 * (i // span) + 1].wait()
        at = head_slice(i)
        values = v_ref[:, at]
        weighted = k_ref[:, at].astype(F32) * factor[:, i : i + 1]
        top, rest = halves(weighted)
        both = lax.dot_general(
            jnp.concatenate([top, rest], axis=1), values, TN, preferred_element_type=F32
        )
        state = both[:HEAD_DIM] + both[HEAD_DIM:]
        own_ref[i] = state
        if i < span:
            first_ref[i] = state.astype(BF16)
        elif i < 2 * span:
            second_ref[i - span] = state.astype(BF16)
        log_ref[:, at] = jnp.broadcast_to(total[:, i : i + 1], (1, HEAD_DIM))
    for copy in others:
        copy.wait()


def chain_kernel(step, place_ref, own_ref, log_ref, got_ref, *rest):
    out_ref = rest[-1]
    span = out_ref.shape[0]
    chunks = own_ref.shape[0] // span
    chunk = jnp.clip(step - LAG * place_ref[0], 0, chunks - 1)
    wide = span * HEAD_DIM
    keep = jnp.exp(log_ref[:, pl.ds(pl.multiple_of(chunk * wide, HEAD_DIM), wide)])
    for i in range(span):
        out_ref[i] = (
            own_ref[chunk * span + i] + keep[:, head_slice(i)] * got_ref[i].astype(F32)
        ).astype(BF16)


def local_kernel(first, q_ref, k_ref, v_ref, col_ref, row_ref, *rest):
    local_ref, token_ref = rest[-2:]
    token_ref[...] = jnp.zeros_like(token_ref)
    lower = lower_ones(q_ref.shape[1])
    for i in range(local_ref.shape[1] // HEAD_DIM):
        h = first + i
        at = head_slice(h)
        scores = lax.dot_general(q_ref[0, :, at], k_ref[:, at], NT, preferred_element_type=F32)
        decay = jnp.exp(
            jnp.where(lower, col_ref[:, h : h + 1] - row_ref[h : h + 1, :], NEGATIVE)
        )
        weights = (scores * decay).astype(BF16)
        local_ref[:, head_slice(i)] = jnp.dot(weights, v_ref[:, at], preferred_element_type=F32)


def hidden_kernel(first, place_ref, q_ref, col_ref, local_ref, *rest):
    got, hidden_ref = rest[:-1], rest[-1]
    group = place_ref[0]
    for i in range(got[0].shape[0]):
        state = got[0][i]
        for g in range(1, len(got)):
            state = jnp.where(group == g + 1, got[g][i], state)
        h = first + i
        at = head_slice(i)
        inter = jnp.dot(q_ref[0, :, head_slice(h)], state, preferred_element_type=F32)
        attended = local_ref[:, at] + inter * jnp.exp(col_ref[:, h : h + 1])
        hidden_ref[:, at] = normalize(attended).astype(BF16)


def flat_rows(ref, rows_ref):
    rows, steps = ref.shape[0], ref.shape[1]
    for r in range(rows):
        rows_ref[r * steps : (r + 1) * steps, :] = ref[r].astype(F32)


def message_kernel(q_ref, log_ref, prompt_ref, *rest):
    out_ref, rows_ref = rest[-2:]
    rows, steps = q_ref.shape[0], q_ref.shape[1]
    d_rows = rows * steps
    features = q_ref.shape[2]
    rows_ref[...] = jnp.zeros_like(rows_ref)
    flat_rows(q_ref, rows_ref)
    log = log_ref[...]
    top = log.astype(BF16).astype(F32)
    mid = (log - top).astype(BF16).astype(F32)
    rows_ref[d_rows : d_rows + 1, :] = top
    rows_ref[d_rows + 1 : d_rows + 2, :] = mid
    rows_ref[d_rows + 2 : d_rows + 3, :] = log - top - mid
    lane = lax.broadcasted_iota(jnp.int32, (1, features), 1)
    prompts = jnp.zeros((1, features), F32)
    for r in range(rows):
        here = (lane >= r * steps) & (lane < (r + 1) * steps)
        prompts = jnp.where(here, prompt_ref[r].astype(F32), prompts)
    rows_ref[d_rows + 3 : d_rows + 4, :] = prompts
    out_ref[...] = rows_ref[...].astype(BF16)


def start_kernel(groups, d_rows, place_ref, near_ref, far_ref, own_ref, *rest):
    near_out, far_out = rest[-2:]
    unit = near_ref.shape[0] // groups
    group = place_ref[0]
    later = jnp.zeros((1, near_ref.shape[1]), F32)
    for j in range(1, groups):
        facts = near_ref[j * unit : (j + 1) * unit, :].astype(F32)[d_rows : d_rows + 3]
        facts = jnp.sum(facts, axis=0, keepdims=True)
        later = later + jnp.where((group ^ j) > group, facts, 0.0)
    scale = jnp.exp(later)

    def strip(terms):
        return jnp.concatenate(
            [terms[j * unit : j * unit + d_rows] for j in range(groups)], axis=0
        )

    for i in range(own_ref.shape[0]):
        at = head_slice(i)
        top, low = halves(own_ref[i])
        both = jnp.concatenate([top, low], axis=1)
        for source, target in ((near_ref, near_out), (far_ref, far_out)):
            terms = jnp.dot(source[:, at], both, preferred_element_type=F32)
            terms = (terms[:, :HEAD_DIM] + terms[:, HEAD_DIM:]) * scale[:, at]
            target[:, at] = strip(terms).astype(target.dtype)


def select_kernel(groups, d_rows, place_ref, near_ref, mine_ref, other_ref, *rest):
    outs = rest[-groups:]
    unit = near_ref.shape[0] // groups
    rep = place_ref[1].astype(F32)
    wide = -(-d_rows // HEAD_DIM) * HEAD_DIM
    rows = lax.broadcasted_iota(jnp.int32, (d_rows, wide), 0)
    cols = lax.broadcasted_iota(jnp.int32, (d_rows, wide), 1)
    other = other_ref[...].astype(F32)
    for j in range(groups):
        facts = near_ref[j * unit : (j + 1) * unit, :wide].astype(F32)[d_rows + 3 : d_rows + 4]
        prompt = jnp.sum(jnp.where(rows == cols, facts, 0.0), axis=1, keepdims=True)
        at = slice(j * d_rows, (j + 1) * d_rows)
        picked = jnp.where(prompt == rep, mine_ref[at], other[at])
        outs[j][...] = picked.astype(outs[j].dtype)


def decode_kernel(groups, q_ref, k_ref, v_ref, rate_ref, base_ref, *rest):
    got = rest[: groups - 1]
    out_ref, q_rows, k_rows, v_rows, rate_rows = rest[-5:]
    steps = q_ref.shape[1]
    d_rows = q_rows.shape[0]
    flat_rows(q_ref, q_rows)
    flat_rows(k_ref, k_rows)
    flat_rows(v_ref, v_rows)
    flat_rows(rate_ref, rate_rows)
    rows, cols = identity(d_rows)
    seen = (rows // steps == cols // steps) & (rows >= cols)
    ones = seen.astype(F32)
    rates = rate_rows[...]
    down = -jnp.dot(ones, rates, precision=HIGH, preferred_element_type=F32)
    across = -lax.dot_general(
        rates, ones, (((0,), (1,)), ((), ())), precision=HIGH, preferred_element_type=F32
    )
    grow = jnp.exp(down)
    out_ref[...] = jnp.zeros_like(out_ref)
    for i in range(rates.shape[1]):
        at = head_slice(i)
        scores = lax.dot_general(
            q_rows[:, at], k_rows[:, at], NT, precision=HIGH, preferred_element_type=F32
        )
        decay = jnp.exp(jnp.where(seen, down[:, i : i + 1] - across[i : i + 1, :], NEGATIVE))
        intra = jnp.dot(scores * decay, v_rows[:, at], precision=HIGH, preferred_element_type=F32)
        base = base_ref[:, at]
        for ref in got:
            base = base + ref[:, at].astype(F32)
        q_rows[:, at] = normalize(base * grow[:, i : i + 1] + intra)
    pad = out_ref.shape[0] - d_rows
    value = q_rows[...]
    if pad:
        value = jnp.concatenate([value, jnp.zeros((pad, value.shape[1]), F32)], axis=0)
    out_ref[...] = value.astype(BF16)


def project_kernel(pieces, chunks, place_ref, decode_ref, *rest):
    hidden, weight_hbm = rest[:chunks], rest[chunks]
    outs = rest[chunks + 1 : chunks + 1 + len(pieces)]
    weight_ref, sems = rest[-2:]
    half = outs[0].shape[1]
    depth = hidden[0].shape[1]
    part = depth // PARTS_OF_COPY
    copies = []
    for n, (bits, side) in enumerate(pieces):
        column = pl.multiple_of(((place_ref[2] ^ bits) * 2 + side) * half, HEAD_DIM)
        for k in range(chunks * PARTS_OF_COPY):
            copy = pltpu.make_async_copy(
                weight_hbm.at[pl.ds(k * part, part), pl.ds(column, half)],
                weight_ref.at[n, pl.ds(k * part, part)],
                sems.at[n, k],
            )
            copy.start()
            copies.append(copy)
    for n, out_ref in enumerate(outs):
        total = None
        for c in range(chunks):
            rows = jnp.concatenate(
                [hidden[c][...], decode_ref[:, c * depth : (c + 1) * depth]], axis=0
            )
            for k in range(c * PARTS_OF_COPY, (c + 1) * PARTS_OF_COPY):
                copies[n * chunks * PARTS_OF_COPY + k].wait()
            term = jnp.dot(
                rows, weight_ref[n, c * depth : (c + 1) * depth], preferred_element_type=F32
            )
            total = term if total is None else total + term
        out_ref[...] = total.astype(out_ref.dtype)


def relay_kernel(own_ref, got_ref, out_ref):
    out_ref[...] = (own_ref[...] + got_ref[...].astype(F32)).astype(BF16)


def finish_kernel(own_a, own_b, ax, ay, bx, by, prefill_hbm, decode_ref, out_ref, sems):
    width = own_a.shape[1]
    rows, steps = decode_ref.shape[0], decode_ref.shape[1]
    length = out_ref.shape[0]
    count = sems.shape[0]
    size = length // count
    copies = []
    for c in range(count):
        at = slice(c * size, (c + 1) * size)
        for at_cols, own, x_ref, y_ref in ((0, own_a, ax, ay), (width, own_b, bx, by)):
            total = own[at] + x_ref[at].astype(F32) + y_ref[at].astype(F32)
            out_ref[at, at_cols : at_cols + width] = total.astype(BF16)
        copy = pltpu.make_async_copy(
            out_ref.at[pl.ds(c * size, size)], prefill_hbm.at[0, pl.ds(c * size, size)], sems.at[c]
        )
        copy.start()
        copies.append(copy)
    for at_cols, own, x_ref, y_ref in ((0, own_a, ax, ay), (width, own_b, bx, by)):
        tail = own[length:] + x_ref[length:].astype(F32) + y_ref[length:].astype(F32)
        tail = tail.astype(BF16).astype(F32)
        for r in range(rows):
            decode_ref[r, :, at_cols : at_cols + width] = tail[r * steps : (r + 1) * steps].astype(BF16)
    for copy in copies:
        copy.wait()


def swap(array, axis, size, bit):
    return lax.ppermute(array, axis, [(i, i ^ bit) for i in range(size)])


def body(
    prefill_query,
    prefill_key,
    prefill_value,
    prefill_rate,
    out_weight,
    decode_query,
    decode_key,
    decode_value,
    decode_rate,
    prompt_of_row,
    *,
    groups,
    reps,
    parts,
):
    length = prefill_query.shape[1]
    features = prefill_query.shape[2]
    heads = prefill_rate.shape[1]
    rows_here, steps = decode_query.shape[0], decode_query.shape[1]
    d_rows = rows_here * steps
    d_pad = -(-d_rows // 16) * 16
    unit = -(-(d_rows + 4) // 16) * 16
    total_rows = length + d_pad
    place = jnp.stack([lax.axis_index("ctx"), lax.axis_index("rep"), lax.axis_index("head")])
    place = place.astype(jnp.int32)
    chunks = CHUNKS if heads % CHUNKS == 0 else heads
    span = heads // chunks
    wide = span * HEAD_DIM
    chunk_shape = (span, HEAD_DIM, HEAD_DIM)

    def in_hbm(array):
        return pltpu.with_memory_space_constraint(array, pltpu.HBM)

    def in_vmem(array):
        return pltpu.with_memory_space_constraint(array, pltpu.VMEM)

    decode_shape = (rows_here, steps, features)
    own, first, second, log_row, columns, rows, keys, values, queries, d_query, d_key, d_value = call(
        functools.partial(state_kernel, span),
        "own_state",
        [HBM] * 7,
        [
            pltpu.VMEM((heads, HEAD_DIM, HEAD_DIM), F32),
            sds(chunk_shape, BF16),
            sds(chunk_shape, BF16),
            pltpu.VMEM((1, features), F32),
            pltpu.VMEM((length, heads), F32),
            pltpu.VMEM((heads, length), F32),
            pltpu.VMEM((length, features), BF16),
            pltpu.VMEM((length, features), BF16),
            pltpu.VMEM((1, length, features), BF16),
            pltpu.VMEM(decode_shape, BF16),
            pltpu.VMEM(decode_shape, BF16),
            pltpu.VMEM(decode_shape, BF16),
        ],
        [
            pltpu.VMEM((1, heads, length), F32),
            pltpu.SemaphoreType.DMA((2, chunks)),
            pltpu.SemaphoreType.DMA((5,)),
        ],
        cost(4 * length * features * HEAD_DIM, 4 * length * features),
    )(
        *[
            in_hbm(array)
            for array in (
                prefill_key,
                prefill_value,
                prefill_rate,
                prefill_query,
                decode_query,
                decode_key,
                decode_value,
            )
        ]
    )
    own, log_row, columns, rows, keys, values, queries, d_query, d_key, d_value = map(
        in_vmem, (own, log_row, columns, rows, keys, values, queries, d_query, d_key, d_value)
    )

    def message(*after):
        return call(
            message_kernel,
            "decode_message",
            [VMEM, VMEM, SMEM] + [ANY] * len(after),
            sds((unit, features), BF16),
            [pltpu.VMEM((unit, features), F32)],
            cost(unit * features, unit * features * 8),
        )(d_query, log_row, prompt_of_row, *after)

    def local(chunk, *after):
        return call(
            functools.partial(local_kernel, chunk * span),
            "local_attention",
            [VMEM] * 5 + [ANY] * len(after),
            [pltpu.VMEM((length, wide), F32), sds((8, HEAD_DIM), F32)],
            (),
            cost(4 * length * length * wide, 6 * length * wide, span * length * length),
        )(queries, keys, values, columns, rows, *after)

    def start_terms(near, far, *after):
        return call(
            functools.partial(start_kernel, groups, d_rows),
            "decode_start",
            [SMEM, VMEM, VMEM, VMEM] + [ANY] * len(after),
            [sds((groups * d_rows, features), F32), sds((groups * d_rows, features), BF16)],
            (),
            cost(8 * groups * unit * features * HEAD_DIM, heads * HEAD_DIM * HEAD_DIM * 4),
        )(place, near, far, own, *after)

    def select_terms(near, mine, other, *after):
        return call(
            functools.partial(select_kernel, groups, d_rows),
            "decode_select",
            [SMEM, VMEM, VMEM, VMEM] + [ANY] * len(after),
            [sds((d_rows, features), F32)] + [sds((d_rows, features), BF16)] * (groups - 1),
            (),
            cost(groups * d_rows * features, groups * d_rows * features * 8),
        )(place, near, mine, other, *after)

    def decode_rows(base, got, *after):
        flat = pltpu.VMEM((d_rows, features), F32)
        return call(
            functools.partial(decode_kernel, groups),
            "decode_rows",
            [VMEM] * (5 + len(got)) + [ANY] * len(after),
            sds((d_pad, features), BF16),
            [flat, flat, flat, pltpu.VMEM((d_rows, heads), F32)],
            cost(4 * d_rows * features * d_rows, d_rows * features * 20),
        )(
            d_query,
            d_key,
            d_value,
            jnp.transpose(decode_rate, (0, 2, 1)),
            base,
            *got,
            *after,
        )

    right = [(i, i + 1) for i in range(groups - 1)]
    steps_all = chunks + LAG * (groups - 2)
    received, locals_done, waits = [], [], {}
    decode = {}

    def add_local(*after):
        if len(locals_done) < chunks:
            made, token = local(len(locals_done), *after)
            locals_done.append(in_vmem(made))
            return [token]
        return []

    def send_message(*after):
        decode["message"] = message(*after)
        decode["ctx"] = [swap(decode["message"], "ctx", groups, j) for j in range(1, groups)]
        return [decode["message"]]

    def share_message(*after):
        decode["near"] = jnp.concatenate([decode["message"]] + decode["ctx"], axis=0)
        decode["far"] = swap(decode["near"], "rep", reps, 1)
        return [decode["near"]]

    def start_rows(*after):
        decode["mine"], away = start_terms(decode["near"], decode["far"], *after)
        decode["other"] = swap(away, "rep", reps, 1)
        return [decode["mine"]]

    def select_rows(*after):
        base, *terms = select_terms(decode["near"], decode["mine"], decode["other"], *after)
        decode["got"] = [swap(term, "ctx", groups, j) for j, term in zip(range(1, groups), terms)]
        decode["base"] = base
        return [base]

    plan = {
        1: [add_local],
        2: [send_message],
        3: [add_local],
        4: [share_message, add_local],
        5: [start_rows],
        6: [select_rows],
        7: [add_local],
    }
    for step in range(steps_all):
        if step == 0:
            value = first
        elif step < LAG:
            value = second if chunks > 1 else first
        else:
            after = waits.pop(step - 1, [])
            value = call(
                functools.partial(chain_kernel, step),
                "chain",
                [SMEM, VMEM, VMEM, VMEM] + [ANY] * len(after),
                sds(chunk_shape, BF16),
                (),
                cost(2 * span * HEAD_DIM * HEAD_DIM, 8 * span * HEAD_DIM * HEAD_DIM),
            )(place, own, log_row, received[step - LAG], *after)
        received.append(lax.ppermute(value, "ctx", right))
        ready = [received[step - LAG]] if step >= LAG else []
        waits[step] = [token for work in plan.pop(step, []) for token in work(*ready)]
    for step in sorted(plan):
        for work in plan[step]:
            work()
    while len(locals_done) < chunks:
        add_local()
    decode_hidden = decode_rows(decode["base"], decode["got"])

    hidden = [
        call(
            functools.partial(hidden_kernel, chunk * span),
            "hidden",
            [SMEM] + [VMEM] * (3 + groups - 1),
            sds((length, wide), BF16),
            (),
            cost(2 * length * wide * HEAD_DIM, 8 * length * wide),
        )(
            place,
            queries,
            columns,
            locals_done[chunk],
            *[received[chunk + LAG * g] for g in range(groups - 1)],
        )
        for chunk in range(chunks)
    ]

    out_columns = out_weight.shape[1]
    if parts != 4 or (out_columns // parts) % 256 != 0 or length % 64 != 0:
        rows_all = jnp.concatenate([jnp.concatenate(hidden, axis=1), decode_hidden], axis=0)
        terms = jnp.dot(rows_all, out_weight, preferred_element_type=F32)
        summed = lax.psum_scatter(terms, "head", scatter_dimension=1, tiled=True)
        prefill_out = summed[:length].astype(BF16)[None]
        decode_out = summed[length : length + d_rows].astype(BF16)
        return prefill_out, decode_out.reshape(rows_here, steps, -1)

    half = out_columns // parts // 2
    weight = in_hbm(out_weight)

    def project(pieces, dtype, *after):
        return call(
            functools.partial(project_kernel, pieces, chunks),
            "project",
            [SMEM, VMEM] + [VMEM] * chunks + [HBM],
            [sds((total_rows, half), dtype) for _ in pieces],
            [
                pltpu.VMEM((len(pieces), features, half), BF16),
                pltpu.SemaphoreType.DMA((len(pieces), chunks * PARTS_OF_COPY)),
            ],
            cost(2 * total_rows * features * half * len(pieces), features * half * 2 * len(pieces)),
        )(place, decode_hidden, *hidden, weight)

    def relay(own_term, got):
        return call(
            relay_kernel,
            "relay",
            [VMEM, VMEM],
            sds((total_rows, half), BF16),
            (),
            cost(total_rows * half, total_rows * half * 8),
        )(own_term, got)

    far_a = swap(project([(3, 0)], BF16)[0], "head", parts, 1)
    far_b = swap(project([(3, 1)], BF16)[0], "head", parts, 2)
    x_a = swap(project([(1, 0)], BF16)[0], "head", parts, 1)
    y_b = swap(project([(2, 1)], BF16)[0], "head", parts, 2)
    pass_a, pass_b = project([(2, 0), (1, 1)], F32)
    own_a, own_b = project([(0, 0), (0, 1)], F32)
    y_a = swap(relay(pass_a, far_a), "head", parts, 2)
    x_b = swap(relay(pass_b, far_b), "head", parts, 1)

    prefill_out, decode_out = call(
        finish_kernel,
        "finish",
        [VMEM] * 6,
        [sds((1, length, 2 * half), BF16), sds((rows_here, steps, 2 * half), BF16)],
        [pltpu.VMEM((length, 2 * half), BF16), pltpu.SemaphoreType.DMA((4,))],
        cost(6 * total_rows * half, 20 * total_rows * half),
        out_specs=[HBM, VMEM],
    )(own_a, own_b, x_a, y_a, x_b, y_b)
    return prefill_out, decode_out


def solution(mesh):
    return jax.shard_map(
        functools.partial(
            body, groups=mesh.shape["ctx"], reps=mesh.shape["rep"], parts=mesh.shape["head"]
        ),
        mesh=mesh,
        in_specs=(
            P("rep", "ctx", "head"),
            P("rep", "ctx", "head"),
            P("rep", "ctx", "head"),
            P("rep", "head", "ctx"),
            P("head", None),
            P(("ctx", "rep"), None, "head"),
            P(("ctx", "rep"), None, "head"),
            P(("ctx", "rep"), None, "head"),
            P(("ctx", "rep"), "head", None),
            P(("ctx", "rep")),
        ),
        out_specs=(P("rep", "ctx", "head"), P(("ctx", "rep"), None, "head")),
        check_vma=False,
    )
```

```python
import functools

import jax
import jax.numpy as jnp
from jax import lax
from jax.experimental import pallas as pl
from jax.experimental.pallas import tpu as pltpu
from jax.sharding import PartitionSpec as P

HEAD_DIM = 128
EPSILON = 1e-06
NEGATIVE = -1e30
HIGH = lax.Precision.HIGHEST
CHUNKS = 4
LAG = 2
VMEM_BYTES = 8 * 2**20
F32 = jnp.float32
BF16 = jnp.bfloat16
NT = (((1,), (1,)), ((), ()))
TN = (((0,), (0,)), ((), ()))


def params():
    return pltpu.CompilerParams(vmem_limit_bytes=VMEM_BYTES)


def cost(flops, moved, exps=0):
    return pl.CostEstimate(flops=int(flops), bytes_accessed=int(moved), transcendentals=int(exps))


def normalize(array):
    return array * lax.rsqrt(jnp.mean(array * array, axis=-1, keepdims=True) + EPSILON)


def lower_ones(length):
    rows = lax.broadcasted_iota(jnp.int32, (length, length), 0)
    cols = lax.broadcasted_iota(jnp.int32, (length, length), 1)
    return rows >= cols


def decay_columns(rate, lower):
    return -lax.dot_general(lower.astype(F32), rate, NT, precision=HIGH, preferred_element_type=F32)


def decay_rows(rate, lower):
    return -lax.dot_general(rate, lower.astype(F32), NT, precision=HIGH, preferred_element_type=F32)


def identity(size):
    rows = lax.broadcasted_iota(jnp.int32, (size, size), 0)
    cols = lax.broadcasted_iota(jnp.int32, (size, size), 1)
    return rows, cols


def head_slice(index):
    return slice(index * HEAD_DIM, (index + 1) * HEAD_DIM)


def halves(array):
    top = array.astype(BF16)
    return top, (array - top.astype(F32)).astype(BF16)

VMEM = pl.BlockSpec(memory_space=pltpu.VMEM)
SMEM = pl.BlockSpec(memory_space=pltpu.SMEM)
ANY = pl.BlockSpec(memory_space=pl.ANY)
HBM = pl.BlockSpec(memory_space=pltpu.HBM)


def call(kernel, name, in_specs, out_shape, scratch=(), estimate=None, out_specs=None):
    if out_specs is None:
        out_specs = jax.tree.map(lambda _: VMEM, out_shape)
    return pl.pallas_call(
        kernel,
        in_specs=in_specs,
        out_specs=out_specs,
        out_shape=out_shape,
        scratch_shapes=list(scratch),
        compiler_params=params(),
        cost_estimate=estimate,
        name=name,
    )


def sds(shape, dtype):
    return jax.ShapeDtypeStruct(shape, dtype)


def state_kernel(span, place_ref, *refs):
    k_hbm, v_hbm, rate_hbm, q_hbm, dq_hbm, dk_hbm, dv_hbm = refs[:7]
    own_ref, first_ref, second_ref, log_ref, col_ref, row_ref = refs[7:13]
    k_ref, v_ref, q_ref, dq_ref, dk_ref, dv_ref = refs[13:19]
    rate_ref, sems, more = refs[19:]
    heads = own_ref.shape[0]
    rate_copy = pltpu.make_async_copy(rate_hbm, rate_ref, more.at[0])
    rate_copy.start()
    copies = [
        pltpu.make_async_copy(k_hbm.at[0], k_ref, sems.at[0]),
        pltpu.make_async_copy(v_hbm.at[0], v_ref, sems.at[1]),
    ]
    others = [
        pltpu.make_async_copy(source, target, more.at[1 + i])
        for i, (source, target) in enumerate(
            ((dq_hbm, dq_ref), (dk_hbm, dk_ref), (dv_hbm, dv_ref), (q_hbm, q_ref))
        )
    ]
    for copy in copies + others:
        copy.start()
    length = k_ref.shape[0]
    lower = lower_ones(length)
    rate_copy.wait()
    rate = rate_ref[0]
    columns = decay_columns(rate, lower)
    col_ref[...] = columns
    row_ref[...] = decay_rows(rate, lower)
    total = columns[length - 1 :, :]
    factor = jnp.exp(total - columns)
    for copy in copies:
        copy.wait()
    for i in range(heads):
        at = head_slice(i)
        values = v_ref[:, at]
        weighted = k_ref[:, at].astype(F32) * factor[:, i : i + 1]
        top, rest = halves(weighted)
        both = lax.dot_general(
            jnp.concatenate([top, rest], axis=1), values, TN, preferred_element_type=F32
        )
        state = both[:HEAD_DIM] + both[HEAD_DIM:]
        own_ref[i] = state
        if i < span:
            first_ref[i] = state.astype(BF16)
        elif i < 2 * span:
            second_ref[i - span] = state.astype(BF16)
        log_ref[:, at] = jnp.broadcast_to(total[:, i : i + 1], (1, HEAD_DIM))
    for copy in others:
        copy.wait()


def chain_kernel(step, place_ref, own_ref, log_ref, got_ref, *rest):
    out_ref = rest[-1]
    span = out_ref.shape[0]
    chunks = own_ref.shape[0] // span
    chunk = jnp.clip(step - LAG * place_ref[0], 0, chunks - 1)
    wide = span * HEAD_DIM
    keep = jnp.exp(log_ref[:, pl.ds(pl.multiple_of(chunk * wide, HEAD_DIM), wide)])
    for i in range(span):
        out_ref[i] = (
            own_ref[chunk * span + i] + keep[:, head_slice(i)] * got_ref[i].astype(F32)
        ).astype(BF16)


def local_kernel(first, q_ref, k_ref, v_ref, col_ref, row_ref, *rest):
    local_ref, token_ref = rest[-2:]
    token_ref[...] = jnp.zeros_like(token_ref)
    lower = lower_ones(q_ref.shape[1])
    for i in range(local_ref.shape[1] // HEAD_DIM):
        h = first + i
        at = head_slice(h)
        scores = lax.dot_general(q_ref[0, :, at], k_ref[:, at], NT, preferred_element_type=F32)
        decay = jnp.exp(
            jnp.where(lower, col_ref[:, h : h + 1] - row_ref[h : h + 1, :], NEGATIVE)
        )
        weights = (scores * decay).astype(BF16)
        local_ref[:, head_slice(i)] = jnp.dot(weights, v_ref[:, at], preferred_element_type=F32)


def hidden_kernel(first, place_ref, q_ref, col_ref, local_ref, *rest):
    got, hidden_ref = rest[:-1], rest[-1]
    group = place_ref[0]
    for i in range(got[0].shape[0]):
        state = got[0][i]
        for g in range(1, len(got)):
            state = jnp.where(group == g + 1, got[g][i], state)
        h = first + i
        at = head_slice(i)
        whole = head_slice(h)
        inter = jnp.dot(q_ref[0, :, whole], state, preferred_element_type=F32)
        attended = local_ref[:, whole] + inter * jnp.exp(col_ref[:, h : h + 1])
        hidden_ref[:, at] = normalize(attended).astype(BF16)


def flat_rows(ref, rows_ref):
    rows, steps = ref.shape[0], ref.shape[1]
    for r in range(rows):
        rows_ref[r * steps : (r + 1) * steps, :] = ref[r].astype(F32)


def message_kernel(q_ref, log_ref, prompt_ref, *rest):
    out_ref, rows_ref = rest[-2:]
    rows, steps = q_ref.shape[0], q_ref.shape[1]
    d_rows = rows * steps
    features = q_ref.shape[2]
    rows_ref[...] = jnp.zeros_like(rows_ref)
    flat_rows(q_ref, rows_ref)
    log = log_ref[...]
    top = log.astype(BF16).astype(F32)
    mid = (log - top).astype(BF16).astype(F32)
    rows_ref[d_rows : d_rows + 1, :] = top
    rows_ref[d_rows + 1 : d_rows + 2, :] = mid
    rows_ref[d_rows + 2 : d_rows + 3, :] = log - top - mid
    lane = lax.broadcasted_iota(jnp.int32, (1, features), 1)
    prompts = jnp.zeros((1, features), F32)
    for r in range(rows):
        here = (lane >= r * steps) & (lane < (r + 1) * steps)
        prompts = jnp.where(here, prompt_ref[r].astype(F32), prompts)
    rows_ref[d_rows + 3 : d_rows + 4, :] = prompts
    out_ref[...] = rows_ref[...].astype(BF16)


def join_kernel(first_ref, second_ref, *rest):
    out_ref = rest[-1]
    size = first_ref.shape[0]
    out_ref[:size] = first_ref[...]
    out_ref[size:] = second_ref[...]


def start_kernel(groups, d_rows, place_ref, near_ref, far_ref, own_ref, *rest):
    near_out, far_out = rest[-2:]
    unit = near_ref.shape[0] // groups
    group = place_ref[0]
    later = jnp.zeros((1, near_ref.shape[1]), F32)
    for j in range(1, groups):
        facts = near_ref[j * unit : (j + 1) * unit, :].astype(F32)[d_rows : d_rows + 3]
        facts = jnp.sum(facts, axis=0, keepdims=True)
        later = later + jnp.where((group ^ j) > group, facts, 0.0)
    scale = jnp.exp(later)

    def strip(terms):
        return jnp.concatenate(
            [terms[j * unit : j * unit + d_rows] for j in range(groups)], axis=0
        )

    for i in range(own_ref.shape[0]):
        at = head_slice(i)
        top, low = halves(own_ref[i])
        both = jnp.concatenate([top, low], axis=1)
        for source, target in ((near_ref, near_out), (far_ref, far_out)):
            terms = jnp.dot(source[:, at], both, preferred_element_type=F32)
            terms = (terms[:, :HEAD_DIM] + terms[:, HEAD_DIM:]) * scale[:, at]
            target[:, at] = strip(terms).astype(target.dtype)


def select_kernel(groups, d_rows, place_ref, near_ref, mine_ref, other_ref, *rest):
    keep_ref, send_ref = rest[-2:]
    half = groups // 2
    unit = near_ref.shape[0] // groups
    rep = place_ref[1].astype(F32)
    wide = -(-d_rows // HEAD_DIM) * HEAD_DIM
    rows = lax.broadcasted_iota(jnp.int32, (d_rows, wide), 0)
    cols = lax.broadcasted_iota(jnp.int32, (d_rows, wide), 1)
    other = other_ref[...].astype(F32)
    picked = []
    for j in range(groups):
        facts = near_ref[j * unit : (j + 1) * unit, :wide].astype(F32)[d_rows + 3 : d_rows + 4]
        prompt = jnp.sum(jnp.where(rows == cols, facts, 0.0), axis=1, keepdims=True)
        at = slice(j * d_rows, (j + 1) * d_rows)
        picked.append(jnp.where(prompt == rep, mine_ref[at], other[at]))
    keep_ref[...] = jnp.concatenate(picked[:half], axis=0)
    send_ref[...] = jnp.concatenate(picked[half:], axis=0).astype(BF16)


def merge_kernel(kept_ref, got_ref, *rest):
    keep_ref, send_ref = rest[-2:]
    total = kept_ref[...] + got_ref[...].astype(F32)
    keep_ref[...] = total[: keep_ref.shape[0]]
    send_ref[...] = total[keep_ref.shape[0] :].astype(BF16)


def decode_kernel(q_ref, k_ref, v_ref, rate_ref, base_ref, got_ref, *rest):
    out_ref, q_rows, k_rows, v_rows, rate_rows = rest[-5:]
    steps = q_ref.shape[1]
    d_rows = q_rows.shape[0]
    flat_rows(q_ref, q_rows)
    flat_rows(k_ref, k_rows)
    flat_rows(v_ref, v_rows)
    flat_rows(rate_ref, rate_rows)
    rows, cols = identity(d_rows)
    seen = (rows // steps == cols // steps) & (rows >= cols)
    ones = seen.astype(F32)
    rates = rate_rows[...]
    down = -jnp.dot(ones, rates, precision=HIGH, preferred_element_type=F32)
    across = -lax.dot_general(
        rates, ones, (((0,), (1,)), ((), ())), precision=HIGH, preferred_element_type=F32
    )
    grow = jnp.exp(down)
    out_ref[...] = jnp.zeros_like(out_ref)
    for i in range(rates.shape[1]):
        at = head_slice(i)
        scores = lax.dot_general(
            q_rows[:, at], k_rows[:, at], NT, precision=HIGH, preferred_element_type=F32
        )
        decay = jnp.exp(jnp.where(seen, down[:, i : i + 1] - across[i : i + 1, :], NEGATIVE))
        intra = jnp.dot(scores * decay, v_rows[:, at], precision=HIGH, preferred_element_type=F32)
        base = base_ref[:, at] + got_ref[:, at].astype(F32)
        q_rows[:, at] = normalize(base * grow[:, i : i + 1] + intra)
    pad = out_ref.shape[0] - d_rows
    value = q_rows[...]
    if pad:
        value = jnp.concatenate([value, jnp.zeros((pad, value.shape[1]), F32)], axis=0)
    out_ref[...] = value.astype(BF16)


def project_kernel(pieces, chunks, place_ref, decode_ref, *rest):
    hidden, weight_ref, outs = rest[:chunks], rest[chunks], rest[chunks + 1 :]
    half = outs[0].shape[1]
    depth = hidden[0].shape[1]
    rows = jnp.concatenate(
        [
            jnp.concatenate([ref[...], decode_ref[:, c * depth : (c + 1) * depth]], axis=0)
            for c, ref in enumerate(hidden)
        ],
        axis=1,
    )
    for (bits, side), out_ref in zip(pieces, outs):
        column = pl.multiple_of(((place_ref[2] ^ bits) * 2 + side) * half, HEAD_DIM)
        out_ref[...] = jnp.dot(
            rows, weight_ref[:, pl.ds(column, half)], preferred_element_type=F32
        ).astype(out_ref.dtype)


def relay_kernel(own_ref, got_ref, out_ref):
    out_ref[...] = (own_ref[...] + got_ref[...].astype(F32)).astype(BF16)


def finish_kernel(own_a, own_b, ax, ay, bx, by, prefill_hbm, decode_ref, out_ref, sems):
    width = own_a.shape[1]
    rows, steps = decode_ref.shape[0], decode_ref.shape[1]
    length = out_ref.shape[0]
    count = sems.shape[0]
    size = length // count
    copies = []
    for c in range(count):
        at = slice(c * size, (c + 1) * size)
        for at_cols, own, x_ref, y_ref in ((0, own_a, ax, ay), (width, own_b, bx, by)):
            total = own[at] + x_ref[at].astype(F32) + y_ref[at].astype(F32)
            out_ref[at, at_cols : at_cols + width] = total.astype(BF16)
        copy = pltpu.make_async_copy(
            out_ref.at[pl.ds(c * size, size)], prefill_hbm.at[0, pl.ds(c * size, size)], sems.at[c]
        )
        copy.start()
        copies.append(copy)
    for at_cols, own, x_ref, y_ref in ((0, own_a, ax, ay), (width, own_b, bx, by)):
        tail = own[length:] + x_ref[length:].astype(F32) + y_ref[length:].astype(F32)
        tail = tail.astype(BF16).astype(F32)
        for r in range(rows):
            decode_ref[r, :, at_cols : at_cols + width] = tail[r * steps : (r + 1) * steps].astype(BF16)
    for copy in copies:
        copy.wait()


def swap(array, axis, size, bit):
    return lax.ppermute(array, axis, [(i, i ^ bit) for i in range(size)])


def body(
    prefill_query,
    prefill_key,
    prefill_value,
    prefill_rate,
    out_weight,
    decode_query,
    decode_key,
    decode_value,
    decode_rate,
    prompt_of_row,
    *,
    groups,
    reps,
    parts,
):
    length = prefill_query.shape[1]
    features = prefill_query.shape[2]
    heads = prefill_rate.shape[1]
    rows_here, steps = decode_query.shape[0], decode_query.shape[1]
    d_rows = rows_here * steps
    d_pad = -(-d_rows // 16) * 16
    unit = -(-(d_rows + 4) // 16) * 16
    total_rows = length + d_pad
    place = jnp.stack([lax.axis_index("ctx"), lax.axis_index("rep"), lax.axis_index("head")])
    place = place.astype(jnp.int32)
    chunks = CHUNKS if heads % CHUNKS == 0 else heads
    span = heads // chunks
    wide = span * HEAD_DIM
    chunk_shape = (span, HEAD_DIM, HEAD_DIM)

    def in_hbm(array):
        return pltpu.with_memory_space_constraint(array, pltpu.HBM)

    def in_vmem(array):
        return pltpu.with_memory_space_constraint(array, pltpu.VMEM)

    decode_shape = (rows_here, steps, features)
    own, first, second, log_row, columns, rows, keys, values, queries, d_query, d_key, d_value = call(
        functools.partial(state_kernel, span),
        "own_state",
        [SMEM] + [HBM] * 7,
        [
            pltpu.VMEM((heads, HEAD_DIM, HEAD_DIM), F32),
            sds(chunk_shape, BF16),
            sds(chunk_shape, BF16),
            pltpu.VMEM((1, features), F32),
            pltpu.VMEM((length, heads), F32),
            pltpu.VMEM((heads, length), F32),
            pltpu.VMEM((length, features), BF16),
            pltpu.VMEM((length, features), BF16),
            pltpu.VMEM((1, length, features), BF16),
            pltpu.VMEM(decode_shape, BF16),
            pltpu.VMEM(decode_shape, BF16),
            pltpu.VMEM(decode_shape, BF16),
        ],
        [
            pltpu.VMEM((1, heads, length), F32),
            pltpu.SemaphoreType.DMA((2,)),
            pltpu.SemaphoreType.DMA((5,)),
        ],
        cost(4 * length * features * HEAD_DIM, 4 * length * features),
    )(
        place,
        *[
            in_hbm(array)
            for array in (
                prefill_key,
                prefill_value,
                prefill_rate,
                prefill_query,
                decode_query,
                decode_key,
                decode_value,
            )
        ]
    )
    own, log_row, columns, rows, keys, values, queries, d_query, d_key, d_value = map(
        in_vmem, (own, log_row, columns, rows, keys, values, queries, d_query, d_key, d_value)
    )

    def message(*after):
        return call(
            message_kernel,
            "decode_message",
            [VMEM, VMEM, SMEM] + [ANY] * len(after),
            sds((unit, features), BF16),
            [pltpu.VMEM((unit, features), F32)],
            cost(unit * features, unit * features * 8),
        )(d_query, log_row, prompt_of_row, *after)

    def local(*after):
        return call(
            functools.partial(local_kernel, 0),
            "local_attention",
            [VMEM] * 5 + [ANY] * len(after),
            [pltpu.VMEM((length, features), F32), sds((8, HEAD_DIM), F32)],
            (),
            cost(4 * length * length * features, 6 * length * features, heads * length * length),
        )(queries, keys, values, columns, rows, *after)

    def join(first, second, *after):
        return call(
            join_kernel,
            "decode_join",
            [VMEM, VMEM] + [ANY] * len(after),
            sds((2 * first.shape[0], features), BF16),
            (),
            cost(first.size, first.size * 8),
        )(first, second, *after)

    def start_terms(near, far, *after):
        return call(
            functools.partial(start_kernel, groups, d_rows),
            "decode_start",
            [SMEM, VMEM, VMEM, VMEM] + [ANY] * len(after),
            [sds((groups * d_rows, features), F32), sds((groups * d_rows, features), BF16)],
            (),
            cost(8 * groups * unit * features * HEAD_DIM, heads * HEAD_DIM * HEAD_DIM * 4),
        )(place, near, far, own, *after)

    def select_terms(near, mine, other, *after):
        return call(
            functools.partial(select_kernel, groups, d_rows),
            "decode_select",
            [SMEM, VMEM, VMEM, VMEM] + [ANY] * len(after),
            [
                sds((groups // 2 * d_rows, features), F32),
                sds((groups // 2 * d_rows, features), BF16),
            ],
            (),
            cost(groups * d_rows * features, groups * d_rows * features * 8),
        )(place, near, mine, other, *after)

    def merge_terms(kept, got, *after):
        shape = (kept.shape[0] // 2, features)
        return call(
            merge_kernel,
            "decode_merge",
            [VMEM, VMEM] + [ANY] * len(after),
            [sds(shape, F32), sds(shape, BF16)],
            (),
            cost(kept.size, kept.size * 10),
        )(kept, got, *after)

    def decode_rows(base, got, *after):
        flat = pltpu.VMEM((d_rows, features), F32)
        return call(
            decode_kernel,
            "decode_rows",
            [VMEM] * 6 + [ANY] * len(after),
            sds((d_pad, features), BF16),
            [flat, flat, flat, pltpu.VMEM((d_rows, heads), F32)],
            cost(4 * d_rows * features * d_rows, d_rows * features * 20),
        )(
            d_query,
            d_key,
            d_value,
            jnp.transpose(decode_rate, (0, 2, 1)),
            base,
            got,
            *after,
        )

    right = [(i, i + 1) for i in range(groups - 1)]
    steps_all = chunks + LAG * (groups - 2)
    received, waits = [], {}
    decode = {}
    attended_here, local_token = local()
    attended_here = in_vmem(attended_here)

    def add_local(*after):
        return [local_token]

    def send_message(*after):
        decode["near"] = message(*after)
        decode["got"] = swap(decode["near"], "ctx", groups, 1)
        decode["bit"] = 1
        return [decode["near"]]

    def share_message(*after):
        decode["near"] = join(decode["near"], decode["got"], *after)
        decode["bit"] *= 2
        if decode["bit"] < groups:
            decode["got"] = swap(decode["near"], "ctx", groups, decode["bit"])
        else:
            decode["far"] = swap(decode["near"], "rep", reps, 1)
        return [decode["near"]]

    def start_rows(*after):
        decode["mine"], away = start_terms(decode["near"], decode["far"], *after)
        decode["other"] = swap(away, "rep", reps, 1)
        return [decode["mine"]]

    def select_rows(*after):
        decode["base"], send = select_terms(
            decode["near"], decode["mine"], decode["other"], *after
        )
        decode["bit"] = groups // 2
        decode["got"] = swap(send, "ctx", groups, decode["bit"])
        return [decode["base"]]

    def merge_rows(*after):
        decode["base"], send = merge_terms(decode["base"], decode["got"], *after)
        decode["bit"] //= 2
        decode["got"] = swap(send, "ctx", groups, decode["bit"])
        return [decode["base"]]

    levels = groups.bit_length() - 1
    work = [send_message] + [share_message] * levels + [start_rows, select_rows]
    work += [merge_rows] * (levels - 1)
    plan = {step: [work[step - LAG]] for step in range(LAG, len(work) + LAG)}
    plan[1] = [add_local]
    for step in range(steps_all):
        if step == 0:
            value = first
        elif step < LAG:
            value = second if chunks > 1 else first
        else:
            after = waits.pop(step - 1, [])
            value = call(
                functools.partial(chain_kernel, step),
                "chain",
                [SMEM, VMEM, VMEM, VMEM] + [ANY] * len(after),
                sds(chunk_shape, BF16),
                (),
                cost(2 * span * HEAD_DIM * HEAD_DIM, 8 * span * HEAD_DIM * HEAD_DIM),
            )(place, own, log_row, received[step - LAG], *after)
        received.append(lax.ppermute(value, "ctx", right))
        ready = [value, received[step - 1]] if step >= LAG else []
        waits[step] = [token for work in plan.pop(step, []) for token in work(*ready)]
    for step in sorted(plan):
        for work in plan[step]:
            work()
    decode_hidden = decode_rows(decode["base"], decode["got"])

    hidden = [
        call(
            functools.partial(hidden_kernel, chunk * span),
            "hidden",
            [SMEM] + [VMEM] * (3 + groups - 1),
            sds((length, wide), BF16),
            (),
            cost(2 * length * wide * HEAD_DIM, 8 * length * wide),
        )(
            place,
            queries,
            columns,
            attended_here,
            *[received[chunk + LAG * g] for g in range(groups - 1)],
        )
        for chunk in range(chunks)
    ]

    out_columns = out_weight.shape[1]
    if parts != 4 or (out_columns // parts) % 256 != 0 or length % 64 != 0:
        rows_all = jnp.concatenate([jnp.concatenate(hidden, axis=1), decode_hidden], axis=0)
        terms = jnp.dot(rows_all, out_weight, preferred_element_type=F32)
        summed = lax.psum_scatter(terms, "head", scatter_dimension=1, tiled=True)
        prefill_out = summed[:length].astype(BF16)[None]
        decode_out = summed[length : length + d_rows].astype(BF16)
        return prefill_out, decode_out.reshape(rows_here, steps, -1)

    half = out_columns // parts // 2
    weight = out_weight

    def project(pieces, dtype, *after):
        return call(
            functools.partial(project_kernel, pieces, chunks),
            "project",
            [SMEM, VMEM] + [VMEM] * chunks + [VMEM],
            [sds((total_rows, half), dtype) for _ in pieces],
            (),
            cost(2 * total_rows * features * half * len(pieces), features * half * 2 * len(pieces)),
        )(place, decode_hidden, *hidden, weight)

    def relay(own_term, got):
        return call(
            relay_kernel,
            "relay",
            [VMEM, VMEM],
            sds((total_rows, half), BF16),
            (),
            cost(total_rows * half, total_rows * half * 8),
        )(own_term, got)

    far_a = swap(project([(3, 0)], BF16)[0], "head", parts, 1)
    far_b = swap(project([(3, 1)], BF16)[0], "head", parts, 2)
    x_a = swap(project([(1, 0)], BF16)[0], "head", parts, 1)
    y_b = swap(project([(2, 1)], BF16)[0], "head", parts, 2)
    pass_a, pass_b = project([(2, 0), (1, 1)], F32)
    own_a, own_b = project([(0, 0), (0, 1)], F32)
    y_a = swap(relay(pass_a, far_a), "head", parts, 2)
    x_b = swap(relay(pass_b, far_b), "head", parts, 1)

    prefill_out, decode_out = call(
        finish_kernel,
        "finish",
        [VMEM] * 6,
        [sds((1, length, 2 * half), BF16), sds((rows_here, steps, 2 * half), BF16)],
        [pltpu.VMEM((length, 2 * half), BF16), pltpu.SemaphoreType.DMA((4,))],
        cost(6 * total_rows * half, 20 * total_rows * half),
        out_specs=[HBM, VMEM],
    )(own_a, own_b, x_a, y_a, x_b, y_b)
    return prefill_out, decode_out


def solution(mesh):
    return jax.shard_map(
        functools.partial(
            body, groups=mesh.shape["ctx"], reps=mesh.shape["rep"], parts=mesh.shape["head"]
        ),
        mesh=mesh,
        in_specs=(
            P("rep", "ctx", "head"),
            P("rep", "ctx", "head"),
            P("rep", "ctx", "head"),
            P("rep", "head", "ctx"),
            P("head", None),
            P(("ctx", "rep"), None, "head"),
            P(("ctx", "rep"), None, "head"),
            P(("ctx", "rep"), None, "head"),
            P(("ctx", "rep"), "head", None),
            P(("ctx", "rep")),
        ),
        out_specs=(P("rep", "ctx", "head"), P(("ctx", "rep"), None, "head")),
        check_vma=False,
    )
```

```python
import functools

import jax
import jax.numpy as jnp
from jax import lax
from jax.experimental import pallas as pl
from jax.experimental.pallas import tpu as pltpu
from jax.sharding import PartitionSpec as P

HEAD_DIM = 128
EPSILON = 1e-06
NEGATIVE = -1e30
HIGH = lax.Precision.HIGHEST
CHUNKS = 2
WEIGHT_PARTS = 4
EARLY_PARTS = 3
VMEM_BYTES = 8 * 2**20
F32 = jnp.float32
BF16 = jnp.bfloat16
NT = (((1,), (1,)), ((), ()))
TN = (((0,), (0,)), ((), ()))


def params():
    return pltpu.CompilerParams(vmem_limit_bytes=VMEM_BYTES)


def cost(flops, moved, exps=0):
    return pl.CostEstimate(flops=int(flops), bytes_accessed=int(moved), transcendentals=int(exps))


def normalize(array):
    return array * lax.rsqrt(jnp.mean(array * array, axis=-1, keepdims=True) + EPSILON)


def lower_ones(length):
    rows = lax.broadcasted_iota(jnp.int32, (length, length), 0)
    cols = lax.broadcasted_iota(jnp.int32, (length, length), 1)
    return rows >= cols


def decay_columns(rate, lower):
    return -lax.dot_general(lower.astype(F32), rate, NT, precision=HIGH, preferred_element_type=F32)


def decay_rows(rate, lower):
    return -lax.dot_general(rate, lower.astype(F32), NT, precision=HIGH, preferred_element_type=F32)


def identity(size):
    rows = lax.broadcasted_iota(jnp.int32, (size, size), 0)
    cols = lax.broadcasted_iota(jnp.int32, (size, size), 1)
    return rows, cols


def head_slice(index):
    return slice(index * HEAD_DIM, (index + 1) * HEAD_DIM)


def halves(array):
    top = array.astype(BF16)
    return top, (array - top.astype(F32)).astype(BF16)

VMEM = pl.BlockSpec(memory_space=pltpu.VMEM)
SMEM = pl.BlockSpec(memory_space=pltpu.SMEM)
ANY = pl.BlockSpec(memory_space=pl.ANY)
HBM = pl.BlockSpec(memory_space=pltpu.HBM)


def call(kernel, name, in_specs, out_shape, scratch=(), estimate=None, out_specs=None):
    if out_specs is None:
        out_specs = jax.tree.map(lambda _: VMEM, out_shape)
    return pl.pallas_call(
        kernel,
        in_specs=in_specs,
        out_specs=out_specs,
        out_shape=out_shape,
        scratch_shapes=list(scratch),
        compiler_params=params(),
        cost_estimate=estimate,
        name=name,
    )


def sds(shape, dtype):
    return jax.ShapeDtypeStruct(shape, dtype)


LOG_ROWS = 16


def log_rows(log):
    top = log.astype(BF16).astype(F32)
    mid = (log - top).astype(BF16).astype(F32)
    row = lax.broadcasted_iota(jnp.int32, (LOG_ROWS, HEAD_DIM), 0)
    rest = jnp.where(row == 2, log - top - mid, 0.0)
    return jnp.where(row == 0, top, jnp.where(row == 1, mid, rest)).astype(BF16)


def read_log(message_ref):
    rows = message_ref.shape[0]
    facts = message_ref[rows - LOG_ROWS :, :].astype(F32)
    return facts[0:1] + facts[1:2] + facts[2:3]


def state_rows(message_ref, index):
    return message_ref[index * HEAD_DIM : (index + 1) * HEAD_DIM, :]


def state_kernel(chunks, place_ref, *refs):
    k_hbm, v_hbm, rate_hbm, q_hbm, dq_hbm, dk_hbm, dv_hbm = refs[:7]
    own_ref, log_ref, col_ref, row_ref = refs[7:11]
    k_ref, v_ref, q_ref, dq_ref, dk_ref, dv_ref = refs[11:17]
    messages = refs[17 : 17 + len(chunks)]
    rate_ref, sems = refs[17 + len(chunks) :]
    heads = own_ref.shape[0]
    pairs = (
        (rate_hbm, rate_ref),
        (k_hbm.at[0], k_ref),
        (v_hbm.at[0], v_ref),
        (dq_hbm, dq_ref),
        (dk_hbm, dk_ref),
        (dv_hbm, dv_ref),
        (q_hbm, q_ref),
    )
    copies = [
        pltpu.make_async_copy(source, target, sems.at[i]) for i, (source, target) in enumerate(pairs)
    ]
    for copy in copies:
        copy.start()
    length = k_ref.shape[0]
    lower = lower_ones(length)
    copies[0].wait()
    rate = rate_ref[0]
    columns = decay_columns(rate, lower)
    col_ref[...] = columns
    row_ref[...] = decay_rows(rate, lower)
    total = columns[length - 1 :, :]
    factor = jnp.exp(total - columns)
    log_ref[...] = jnp.zeros_like(log_ref)
    log_ref[:, :heads] = total
    facts = log_rows(log_ref[...])
    copies[1].wait()
    copies[2].wait()
    for (first, size), message_ref in zip(chunks, messages):
        for i in range(size):
            h = first + i
            at = head_slice(h)
            weighted = k_ref[:, at].astype(F32) * factor[:, h : h + 1]
            top, rest = halves(weighted)
            both = lax.dot_general(
                jnp.concatenate([top, rest], axis=1), v_ref[:, at], TN, preferred_element_type=F32
            )
            state = both[:HEAD_DIM] + both[HEAD_DIM:]
            own_ref[h] = state
            message_ref[i * HEAD_DIM : (i + 1) * HEAD_DIM, :] = state.astype(BF16)
        message_ref[size * HEAD_DIM :, :] = facts
    for copy in copies[3:]:
        copy.wait()


def chain_kernel(phase, first, place_ref, own_ref, log_ref, got_ref, *rest):
    out_ref = rest[-1]
    size = (out_ref.shape[0] - LOG_ROWS) // HEAD_DIM
    right = place_ref[0] == phase
    log = log_ref[...]
    later = read_log(got_ref)
    own_factor = jnp.where(right, 1.0, jnp.exp(later))
    got_factor = jnp.where(right, jnp.exp(log), 1.0)
    for i in range(size):
        h = first + i
        value = (
            own_factor[:, h : h + 1] * own_ref[h]
            + got_factor[:, h : h + 1] * state_rows(got_ref, i).astype(F32)
        )
        out_ref[i * HEAD_DIM : (i + 1) * HEAD_DIM, :] = value.astype(BF16)
    out_ref[size * HEAD_DIM :, :] = log_rows(log + later)


def entering_state(group, got, index):
    state = state_rows(got[0], index)
    for phase in range(1, len(got)):
        state = jnp.where(group == phase + 1, state_rows(got[phase], index), state)
    return jnp.where(group == 0, jnp.zeros_like(state), state)


def weight_copies(places, weight_hbm, weights, sems):
    copies = []
    for i, (index, ref) in enumerate(zip(places, weights)):
        depth = ref.shape[0]
        copies.append(
            pltpu.make_async_copy(weight_hbm.at[pl.ds(index * depth, depth)], ref, sems.at[i])
        )
    for copy in copies:
        copy.start()
    return copies


def load_kernel(index, weight_hbm, *rest):
    weight_ref, token_ref, sems = rest[-3:]
    copies = weight_copies([index], weight_hbm, [weight_ref], sems)
    token_ref[...] = jnp.zeros_like(token_ref)
    for copy in copies:
        copy.wait()


def local_kernel(first, q_ref, k_ref, v_ref, col_ref, row_ref, weight_hbm, *rest):
    local_ref, token_ref = rest[:2]
    weights, sems = rest[2:-1], rest[-1]
    copies = weight_copies(range(len(weights)), weight_hbm, weights, sems)
    token_ref[...] = jnp.zeros_like(token_ref)
    lower = lower_ones(q_ref.shape[1])
    for i in range(local_ref.shape[1] // HEAD_DIM):
        h = first + i
        at = head_slice(h)
        scores = lax.dot_general(q_ref[0, :, at], k_ref[:, at], NT, preferred_element_type=F32)
        decay = jnp.exp(
            jnp.where(lower, col_ref[:, h : h + 1] - row_ref[h : h + 1, :], NEGATIVE)
        )
        narrow = (scores * decay).astype(BF16)
        local_ref[:, head_slice(i)] = jnp.dot(narrow, v_ref[:, at], preferred_element_type=F32)
    for copy in copies:
        copy.wait()


def hidden_kernel(phases, first, place_ref, q_ref, col_ref, local_ref, *rest):
    got, hidden_ref = rest[:phases], rest[-1]
    for i in range(hidden_ref.shape[1] // HEAD_DIM):
        h = first + i
        whole = head_slice(h)
        state = entering_state(place_ref[0], got, i)
        inter = jnp.dot(q_ref[0, :, whole], state, preferred_element_type=F32)
        attended = local_ref[:, whole] + inter * jnp.exp(col_ref[:, h : h + 1])
        hidden_ref[:, head_slice(i)] = normalize(attended).astype(BF16)


def final_kernel(chunks, phases, place_ref, own_ref, log_ref, *rest):
    out_ref = rest[-1]
    group = place_ref[0]
    keep = jnp.exp(log_ref[...])
    for c, (first, size) in enumerate(chunks):
        got = [rest[phase * len(chunks) + c] for phase in range(phases)]
        later = jnp.zeros((1, HEAD_DIM), F32)
        for phase in range(phases):
            later = jnp.where(group == phases - 1 - phase, read_log(got[phase]), later)
        later = jnp.exp(later)
        for i in range(size):
            h = first + i
            suffix = jnp.zeros((HEAD_DIM, HEAD_DIM), F32)
            for phase in range(phases):
                there = state_rows(got[phase], i).astype(F32)
                suffix = jnp.where(group == phases - 1 - phase, there, suffix)
            prefix = entering_state(group, got, i).astype(F32)
            here = own_ref[h] + keep[:, h : h + 1] * prefix
            out_ref[h] = suffix + later[:, h : h + 1] * here


def flat_rows(ref, rows_ref):
    rows, steps = ref.shape[0], ref.shape[1]
    for r in range(rows):
        rows_ref[r * steps : (r + 1) * steps, :] = ref[r].astype(F32)


def decode_kernel(place_ref, prompt_ref, q_ref, k_ref, v_ref, rate_ref, near_ref, far_ref, *rest):
    out_ref, q_rows, k_rows, v_rows, rate_rows = rest[-5:]
    rows_here, steps = q_ref.shape[0], q_ref.shape[1]
    d_rows = q_rows.shape[0]
    flat_rows(q_ref, q_rows)
    flat_rows(k_ref, k_rows)
    flat_rows(v_ref, v_rows)
    flat_rows(rate_ref, rate_rows)
    rows, cols = identity(d_rows)
    seen = (rows // steps == cols // steps) & (rows >= cols)
    ones = seen.astype(F32)
    rates = rate_rows[...]
    down = -jnp.dot(ones, rates, precision=HIGH, preferred_element_type=F32)
    across = -lax.dot_general(
        rates, ones, (((0,), (1,)), ((), ())), precision=HIGH, preferred_element_type=F32
    )
    grow = jnp.exp(down)
    row_of = lax.broadcasted_iota(jnp.int32, (d_rows, HEAD_DIM), 0) // steps
    prompt = jnp.zeros((d_rows, HEAD_DIM), jnp.int32)
    for r in range(rows_here):
        prompt = jnp.where(row_of == r, prompt_ref[r], prompt)
    mine = prompt == place_ref[1]
    for i in range(rates.shape[1]):
        at = head_slice(i)
        query = q_rows[:, at]
        narrow = query.astype(BF16)
        terms = []
        for ref in (near_ref, far_ref):
            top, low = halves(ref[i])
            both = jnp.dot(
                narrow, jnp.concatenate([top, low], axis=1), preferred_element_type=F32
            )
            terms.append(both[:, :HEAD_DIM] + both[:, HEAD_DIM:])
        base = jnp.where(mine, terms[0], terms[1])
        scores = lax.dot_general(
            query, k_rows[:, at], NT, precision=HIGH, preferred_element_type=F32
        )
        decay = jnp.exp(jnp.where(seen, down[:, i : i + 1] - across[i : i + 1, :], NEGATIVE))
        intra = jnp.dot(scores * decay, v_rows[:, at], precision=HIGH, preferred_element_type=F32)
        q_rows[:, at] = normalize(base * grow[:, i : i + 1] + intra)
    pad = out_ref.shape[0] - d_rows
    value = q_rows[...]
    if pad:
        value = jnp.concatenate([value, jnp.zeros((pad, value.shape[1]), F32)], axis=0)
    out_ref[...] = value.astype(BF16)


def times_weight(rows, weights, column, width):
    total = None
    for i, ref in enumerate(weights):
        depth = ref.shape[0]
        term = jnp.dot(
            rows[:, i * depth : (i + 1) * depth],
            ref[:, pl.ds(column, width)],
            preferred_element_type=F32,
        )
        total = term if total is None else total + term
    return total


def project_kernel(pieces, chunks, place_ref, *rest):
    hidden, weights = rest[:chunks], rest[chunks : chunks + WEIGHT_PARTS]
    outs = rest[-len(pieces) :]
    half = outs[0].shape[1]
    rows = jnp.concatenate([ref[...] for ref in hidden], axis=1)
    for (bits, side), out_ref in zip(pieces, outs):
        column = pl.multiple_of(((place_ref[2] ^ bits) * 2 + side) * half, HEAD_DIM)
        out_ref[...] = times_weight(rows, weights, column, half).astype(out_ref.dtype)


def decode_project_kernel(place_ref, rows_ref, *rest):
    weights, outs = rest[:WEIGHT_PARTS], rest[-4:]
    width = outs[0].shape[1]
    rows = rows_ref[...]
    for bits, out_ref in enumerate(outs):
        column = pl.multiple_of((place_ref[2] ^ bits) * width, HEAD_DIM)
        out_ref[...] = times_weight(rows, weights, column, width).astype(out_ref.dtype)


def decode_finish_kernel(own_ref, x_ref, y_ref, far_ref, out_ref):
    rows, steps = out_ref.shape[0], out_ref.shape[1]
    total = own_ref[...] + x_ref[...].astype(F32) + y_ref[...].astype(F32) + far_ref[...].astype(F32)
    for r in range(rows):
        out_ref[r] = total[r * steps : (r + 1) * steps].astype(BF16)


def relay_kernel(own_ref, got_ref, *rest):
    out_ref = rest[-1]
    out_ref[...] = (own_ref[...] + got_ref[...].astype(F32)).astype(BF16)


def finish_kernel(own_a, own_b, ax, ay, bx, by, prefill_hbm, out_ref, sems):
    width = own_a.shape[1]
    count = sems.shape[0]
    size = out_ref.shape[0] // count
    copies = []
    for c in range(count):
        at = slice(c * size, (c + 1) * size)
        for at_cols, own, x_ref, y_ref in ((0, own_a, ax, ay), (width, own_b, bx, by)):
            total = own[at] + x_ref[at].astype(F32) + y_ref[at].astype(F32)
            out_ref[at, at_cols : at_cols + width] = total.astype(BF16)
        copy = pltpu.make_async_copy(
            out_ref.at[pl.ds(c * size, size)], prefill_hbm.at[0, pl.ds(c * size, size)], sems.at[c]
        )
        copy.start()
        copies.append(copy)
    for copy in copies:
        copy.wait()


def swap(array, axis, size, bit):
    return lax.ppermute(array, axis, [(i, i ^ bit) for i in range(size)])


def body(
    prefill_query,
    prefill_key,
    prefill_value,
    prefill_rate,
    out_weight,
    decode_query,
    decode_key,
    decode_value,
    decode_rate,
    prompt_of_row,
    *,
    groups,
    reps,
    parts,
):
    length = prefill_query.shape[1]
    features = prefill_query.shape[2]
    heads = prefill_rate.shape[1]
    rows_here, steps = decode_query.shape[0], decode_query.shape[1]
    d_rows = rows_here * steps
    d_pad = -(-d_rows // 16) * 16
    place = jnp.stack([lax.axis_index("ctx"), lax.axis_index("rep"), lax.axis_index("head")])
    place = place.astype(jnp.int32)
    count = min(CHUNKS, heads)
    edges = [heads * c // count for c in range(count + 1)]
    chunks = [(a, b - a) for a, b in zip(edges[:-1], edges[1:])]
    phases = groups - 1
    state_elements = heads * HEAD_DIM * HEAD_DIM

    def in_hbm(array):
        return pltpu.with_memory_space_constraint(array, pltpu.HBM)

    def in_vmem(array):
        return pltpu.with_memory_space_constraint(array, pltpu.VMEM)

    def message_shape(size):
        return sds((size * HEAD_DIM + LOG_ROWS, HEAD_DIM), BF16)

    decode_shape = (rows_here, steps, features)
    made = call(
        functools.partial(state_kernel, chunks),
        "own_state",
        [SMEM] + [HBM] * 7,
        [
            pltpu.VMEM((heads, HEAD_DIM, HEAD_DIM), F32),
            pltpu.VMEM((1, HEAD_DIM), F32),
            pltpu.VMEM((length, heads), F32),
            pltpu.VMEM((heads, length), F32),
            pltpu.VMEM((length, features), BF16),
            pltpu.VMEM((length, features), BF16),
            pltpu.VMEM((1, length, features), BF16),
            pltpu.VMEM(decode_shape, BF16),
            pltpu.VMEM(decode_shape, BF16),
            pltpu.VMEM(decode_shape, BF16),
        ]
        + [message_shape(size) for _, size in chunks],
        [pltpu.VMEM((1, heads, length), F32), pltpu.SemaphoreType.DMA((7,))],
        cost(4 * length * features * HEAD_DIM, 34 * length * features),
    )(
        place,
        *[
            in_hbm(array)
            for array in (
                prefill_key,
                prefill_value,
                prefill_rate,
                prefill_query,
                decode_query,
                decode_key,
                decode_value,
            )
        ],
    )
    own, log_row, columns, rows, keys, values, queries, d_query, d_key, d_value = map(
        in_vmem, made[:10]
    )

    weight_hbm = in_hbm(out_weight)
    weight_part = pltpu.VMEM((features // WEIGHT_PARTS, out_weight.shape[1]), BF16)
    token = sds((8, HEAD_DIM), F32)
    local, local_token, *weights = call(
        functools.partial(local_kernel, 0),
        "local_attention",
        [VMEM] * 5 + [HBM],
        [pltpu.VMEM((length, features), F32), token] + [weight_part] * EARLY_PARTS,
        [pltpu.SemaphoreType.DMA((EARLY_PARTS,))],
        cost(4 * length * length * features, 12 * length * features, heads * length * length),
    )(queries, keys, values, columns, rows, weight_hbm)
    local = in_vmem(local)

    def load_weight(*after):
        if len(weights) == WEIGHT_PARTS:
            return []
        part, done = call(
            functools.partial(load_kernel, len(weights)),
            "load_weight",
            [HBM] + [ANY] * len(after),
            [weight_part, token],
            [pltpu.SemaphoreType.DMA((1,))],
            cost(1, features // WEIGHT_PARTS * out_weight.shape[1] * 2),
        )(weight_hbm, *after)
        weights.append(part)
        return [done]

    values_out = list(made[10:])
    received = []
    after = [local_token]
    for phase in range(phases):
        pairs = {(phase, phase + 1), (groups - 2 - phase, groups - 1 - phase)}
        pairs = sorted(pairs | {(b, a) for a, b in pairs})
        if phase > 0:
            values_out = []
            for c, (first, size) in enumerate(chunks):
                value = call(
                    functools.partial(chain_kernel, phase, first),
                    "chain",
                    [SMEM, VMEM, VMEM, VMEM] + [ANY] * len(after),
                    message_shape(size),
                    (),
                    cost(2 * size * HEAD_DIM * HEAD_DIM, 24 * size * HEAD_DIM * HEAD_DIM),
                )(place, own, log_row, received[-1][c], *after)
                values_out.append(value)
                after = []
        received.append([lax.ppermute(value, "ctx", pairs) for value in values_out])
    loaded = []
    while len(weights) < WEIGHT_PARTS:
        loaded = load_weight(values_out[-1], *loaded)
    weights = [in_vmem(part) for part in weights]

    after = loaded
    hidden = [
        call(
            functools.partial(hidden_kernel, phases, first),
            "hidden",
            [SMEM] + [VMEM] * (3 + phases) + [ANY] * len(after),
            sds((length, size * HEAD_DIM), BF16),
            (),
            cost(2 * length * size * HEAD_DIM * HEAD_DIM, 20 * length * size * HEAD_DIM),
        )(place, queries, columns, local, *[received[phase][c] for phase in range(phases)], *after)
        for c, (first, size) in enumerate(chunks)
    ]

    def final_states(*after):
        final = call(
            functools.partial(final_kernel, chunks, phases),
            "final_state",
            [SMEM, VMEM, VMEM] + [VMEM] * (phases * count) + [ANY] * len(after),
            sds((heads, HEAD_DIM, HEAD_DIM), F32),
            (),
            cost(4 * state_elements, state_elements * 4 * phases),
        )(place, own, log_row, *[got for phase in received for got in phase], *after)
        return final, swap(final, "rep", reps, 1)

    def decode_rows(final, other, *after):
        flat = pltpu.VMEM((d_rows, features), F32)
        return call(
            decode_kernel,
            "decode_rows",
            [SMEM, SMEM] + [VMEM] * 6 + [ANY] * len(after),
            sds((d_pad, features), BF16),
            [flat, flat, flat, pltpu.VMEM((d_rows, heads), F32)],
            cost(16 * d_rows * features * HEAD_DIM, state_elements),
        )(
            place,
            prompt_of_row,
            d_query,
            d_key,
            d_value,
            jnp.transpose(decode_rate, (0, 2, 1)),
            final,
            other,
            *after,
        )

    out_columns = out_weight.shape[1]
    if parts != 4 or (out_columns // parts) % 256 != 0 or length % 64 != 0:
        rows_all = jnp.concatenate([jnp.concatenate(hidden, axis=1), decode_rows(*final_states())], axis=0)
        terms = jnp.dot(rows_all, out_weight, preferred_element_type=F32)
        summed = lax.psum_scatter(terms, "head", scatter_dimension=1, tiled=True)
        prefill_out = summed[:length].astype(BF16)[None]
        decode_out = summed[length : length + d_rows].astype(BF16)
        return prefill_out, decode_out.reshape(rows_here, steps, -1)

    width = out_columns // parts
    half = width // 2

    def project(pieces, dtype, *after):
        return call(
            functools.partial(project_kernel, pieces, count),
            "project",
            [SMEM] + [VMEM] * (count + WEIGHT_PARTS) + [ANY] * len(after),
            [sds((length, half), dtype) for _ in pieces],
            (),
            cost(2 * length * features * half * len(pieces), features * half * 2 * len(pieces)),
        )(place, *hidden, *weights, *after)

    def relay(own_term, got, *after):
        return call(
            relay_kernel,
            "relay",
            [VMEM, VMEM] + [ANY] * len(after),
            sds((length, half), BF16),
            (),
            cost(length * half, length * half * 8),
        )(own_term, got, *after)

    far_a = swap(project([(3, 0)], BF16)[0], "head", parts, 1)
    to_y, = project([(3, 1)], BF16)
    far_b = swap(to_y, "head", parts, 2)
    x_a = swap(project([(1, 0)], BF16)[0], "head", parts, 1)
    y_b = swap(project([(2, 1)], BF16)[0], "head", parts, 2)
    pass_a, pass_b = project([(2, 0), (1, 1)], F32)
    own_a, own_b = project([(0, 0), (0, 1)], F32)
    sent_a, sent_b = relay(pass_a, far_a), relay(pass_b, far_b)
    y_a = swap(sent_a, "head", parts, 2)
    x_b = swap(sent_b, "head", parts, 1)

    d_hidden = decode_rows(*final_states(to_y), sent_a, sent_b)
    d_own, d_x, d_y, d_far = call(
        decode_project_kernel,
        "decode_project",
        [SMEM] + [VMEM] * (1 + WEIGHT_PARTS),
        [sds((d_pad, width), F32)] + [sds((d_pad, width), BF16)] * 3,
        (),
        cost(2 * d_pad * features * out_columns, features * out_columns // 8),
    )(place, d_hidden, *weights)
    decode_out = call(
        decode_finish_kernel,
        "decode_finish",
        [VMEM] * 4,
        sds((rows_here, steps, width), BF16),
        (),
        cost(4 * d_pad * width, 10 * d_pad * width),
    )(
        d_own,
        swap(d_x, "head", parts, 1),
        swap(d_y, "head", parts, 2),
        swap(d_far, "head", parts, 3),
    )

    prefill_out = call(
        finish_kernel,
        "finish",
        [VMEM] * 6,
        sds((1, length, width), BF16),
        [pltpu.VMEM((length, width), BF16), pltpu.SemaphoreType.DMA((4,))],
        cost(6 * length * half, 20 * length * half),
        out_specs=HBM,
    )(own_a, own_b, x_a, y_a, x_b, y_b)
    return prefill_out, decode_out


def solution(mesh):
    return jax.shard_map(
        functools.partial(
            body, groups=mesh.shape["ctx"], reps=mesh.shape["rep"], parts=mesh.shape["head"]
        ),
        mesh=mesh,
        in_specs=(
            P("rep", "ctx", "head"),
            P("rep", "ctx", "head"),
            P("rep", "ctx", "head"),
            P("rep", "head", "ctx"),
            P("head", None),
            P(("ctx", "rep"), None, "head"),
            P(("ctx", "rep"), None, "head"),
            P(("ctx", "rep"), None, "head"),
            P(("ctx", "rep"), "head", None),
            P(("ctx", "rep")),
        ),
        out_specs=(P("rep", "ctx", "head"), P(("ctx", "rep"), None, "head")),
        check_vma=False,
    )
```

```python
import functools

import jax
import jax.numpy as jnp
from jax import lax
from jax.experimental import pallas as pl
from jax.experimental.pallas import tpu as pltpu
from jax.sharding import PartitionSpec as P

HEAD_DIM = 128
EPSILON = 1e-06
NEGATIVE = -1e30
HIGH = lax.Precision.HIGHEST
CHUNKS = 2
WEIGHT_PARTS = 4
EARLY_PARTS = 3
VMEM_BYTES = 8 * 2**20
F32 = jnp.float32
BF16 = jnp.bfloat16
NT = (((1,), (1,)), ((), ()))
TN = (((0,), (0,)), ((), ()))


def params():
    return pltpu.CompilerParams(vmem_limit_bytes=VMEM_BYTES)


def cost(flops, moved, exps=0):
    return pl.CostEstimate(flops=int(flops), bytes_accessed=int(moved), transcendentals=int(exps))


def normalize(array):
    return array * lax.rsqrt(jnp.mean(array * array, axis=-1, keepdims=True) + EPSILON)


def lower_ones(length):
    rows = lax.broadcasted_iota(jnp.int32, (length, length), 0)
    cols = lax.broadcasted_iota(jnp.int32, (length, length), 1)
    return rows >= cols


def decay_columns(rate, lower):
    return -lax.dot_general(lower.astype(F32), rate, NT, precision=HIGH, preferred_element_type=F32)


def decay_rows(rate, lower):
    return -lax.dot_general(rate, lower.astype(F32), NT, precision=HIGH, preferred_element_type=F32)


def identity(size):
    rows = lax.broadcasted_iota(jnp.int32, (size, size), 0)
    cols = lax.broadcasted_iota(jnp.int32, (size, size), 1)
    return rows, cols


def head_slice(index):
    return slice(index * HEAD_DIM, (index + 1) * HEAD_DIM)


def halves(array):
    top = array.astype(BF16)
    return top, (array - top.astype(F32)).astype(BF16)

VMEM = pl.BlockSpec(memory_space=pltpu.VMEM)
SMEM = pl.BlockSpec(memory_space=pltpu.SMEM)
ANY = pl.BlockSpec(memory_space=pl.ANY)
HBM = pl.BlockSpec(memory_space=pltpu.HBM)


def call(kernel, name, in_specs, out_shape, scratch=(), estimate=None, out_specs=None):
    if out_specs is None:
        out_specs = jax.tree.map(lambda _: VMEM, out_shape)
    return pl.pallas_call(
        kernel,
        in_specs=in_specs,
        out_specs=out_specs,
        out_shape=out_shape,
        scratch_shapes=list(scratch),
        compiler_params=params(),
        cost_estimate=estimate,
        name=name,
    )


def sds(shape, dtype):
    return jax.ShapeDtypeStruct(shape, dtype)


LOG_ROWS = 16


def log_rows(log):
    top = log.astype(BF16).astype(F32)
    mid = (log - top).astype(BF16).astype(F32)
    row = lax.broadcasted_iota(jnp.int32, (LOG_ROWS, HEAD_DIM), 0)
    rest = jnp.where(row == 2, log - top - mid, 0.0)
    return jnp.where(row == 0, top, jnp.where(row == 1, mid, rest)).astype(BF16)


def read_log(message_ref):
    rows = message_ref.shape[0]
    facts = message_ref[rows - LOG_ROWS :, :].astype(F32)
    return facts[0:1] + facts[1:2] + facts[2:3]


def state_rows(message_ref, index):
    return message_ref[index * HEAD_DIM : (index + 1) * HEAD_DIM, :]


def own_states(first, k_ref, v_ref, columns, own_ref, message_ref):
    length = columns.shape[0]
    factor = jnp.exp(columns[length - 1 :, :] - columns)
    for i in range(own_ref.shape[0]):
        h = first + i
        at = head_slice(h)
        weighted = k_ref[:, at].astype(F32) * factor[:, h : h + 1]
        top, rest = halves(weighted)
        both = lax.dot_general(
            jnp.concatenate([top, rest], axis=1), v_ref[:, at], TN, preferred_element_type=F32
        )
        state = both[:HEAD_DIM] + both[HEAD_DIM:]
        own_ref[i] = state
        message_ref[i * HEAD_DIM : (i + 1) * HEAD_DIM, :] = state.astype(BF16)


def started(pairs, sems):
    copies = [
        pltpu.make_async_copy(source, target, sems.at[i]) for i, (source, target) in enumerate(pairs)
    ]
    for copy in copies:
        copy.start()
    return copies


def first_state_kernel(place_ref, k_hbm, v_hbm, rate_hbm, *refs):
    own_ref, log_ref, col_ref, rate_ref, k_ref, v_ref, message_ref, sems = refs
    copies = started(((rate_hbm, rate_ref), (k_hbm.at[0], k_ref), (v_hbm.at[0], v_ref)), sems)
    length = k_ref.shape[0]
    copies[0].wait()
    rate = rate_ref[0]
    columns = decay_columns(rate, lower_ones(length))
    col_ref[...] = columns
    log_ref[...] = jnp.zeros_like(log_ref)
    log_ref[:, : rate.shape[0]] = columns[length - 1 :, :]
    message_ref[message_ref.shape[0] - LOG_ROWS :, :] = log_rows(log_ref[...])
    copies[1].wait()
    copies[2].wait()
    own_states(0, k_ref, v_ref, columns, own_ref, message_ref)


def more_state_kernel(first, copied, k_ref, v_ref, col_ref, rate_ref, log_ref, *refs):
    sources, refs = refs[:copied], refs[copied:]
    own_ref, message_ref, row_ref = refs[:3]
    targets, sems = refs[3 : 3 + copied], refs[3 + copied]
    copies = started(tuple(zip(sources, targets)), sems) if copied else []
    row_ref[...] = decay_rows(rate_ref[0], lower_ones(k_ref.shape[0]))
    message_ref[message_ref.shape[0] - LOG_ROWS :, :] = log_rows(log_ref[...])
    own_states(first, k_ref, v_ref, col_ref[...], own_ref, message_ref)
    for copy in copies:
        copy.wait()


def chain_kernel(phase, first, place_ref, own_ref, log_ref, got_ref, *rest):
    out_ref = rest[-1]
    size = (out_ref.shape[0] - LOG_ROWS) // HEAD_DIM
    right = place_ref[0] == phase
    log = log_ref[...]
    later = read_log(got_ref)
    own_factor = jnp.where(right, 1.0, jnp.exp(later))
    got_factor = jnp.where(right, jnp.exp(log), 1.0)
    for i in range(size):
        h = first + i
        value = (
            own_factor[:, h : h + 1] * own_ref[i]
            + got_factor[:, h : h + 1] * state_rows(got_ref, i).astype(F32)
        )
        out_ref[i * HEAD_DIM : (i + 1) * HEAD_DIM, :] = value.astype(BF16)
    out_ref[size * HEAD_DIM :, :] = log_rows(log + later)


def entering_state(group, got, index):
    state = state_rows(got[0], index)
    for phase in range(1, len(got)):
        state = jnp.where(group == phase + 1, state_rows(got[phase], index), state)
    return jnp.where(group == 0, jnp.zeros_like(state), state)


def weight_copies(places, weight_hbm, weights, sems):
    copies = []
    for i, (index, ref) in enumerate(zip(places, weights)):
        depth = ref.shape[0]
        copies.append(
            pltpu.make_async_copy(weight_hbm.at[pl.ds(index * depth, depth)], ref, sems.at[i])
        )
    for copy in copies:
        copy.start()
    return copies


def load_kernel(index, weight_hbm, *rest):
    weight_ref, token_ref, sems = rest[-3:]
    copies = weight_copies([index], weight_hbm, [weight_ref], sems)
    token_ref[...] = jnp.zeros_like(token_ref)
    for copy in copies:
        copy.wait()


def local_kernel(first, q_ref, k_ref, v_ref, col_ref, row_ref, weight_hbm, *rest):
    local_ref, token_ref = rest[:2]
    weights, sems = rest[2:-1], rest[-1]
    copies = weight_copies(range(len(weights)), weight_hbm, weights, sems)
    token_ref[...] = jnp.zeros_like(token_ref)
    lower = lower_ones(q_ref.shape[1])
    for i in range(local_ref.shape[1] // HEAD_DIM):
        h = first + i
        at = head_slice(h)
        scores = lax.dot_general(q_ref[0, :, at], k_ref[:, at], NT, preferred_element_type=F32)
        decay = jnp.exp(
            jnp.where(lower, col_ref[:, h : h + 1] - row_ref[h : h + 1, :], NEGATIVE)
        )
        narrow = (scores * decay).astype(BF16)
        local_ref[:, head_slice(i)] = jnp.dot(narrow, v_ref[:, at], preferred_element_type=F32)
    for copy in copies:
        copy.wait()


def hidden_kernel(phases, first, place_ref, q_ref, col_ref, local_ref, *rest):
    got, hidden_ref = rest[:phases], rest[-1]
    for i in range(hidden_ref.shape[1] // HEAD_DIM):
        h = first + i
        whole = head_slice(h)
        state = entering_state(place_ref[0], got, i)
        inter = jnp.dot(q_ref[0, :, whole], state, preferred_element_type=F32)
        attended = local_ref[:, whole] + inter * jnp.exp(col_ref[:, h : h + 1])
        hidden_ref[:, head_slice(i)] = normalize(attended).astype(BF16)


def final_kernel(first, phases, place_ref, own_ref, log_ref, *rest):
    got, out_ref = rest[:phases], rest[-1]
    group = place_ref[0]
    keep = jnp.exp(log_ref[...])
    later = jnp.zeros((1, HEAD_DIM), F32)
    for phase in range(phases):
        later = jnp.where(group == phases - 1 - phase, read_log(got[phase]), later)
    later = jnp.exp(later)
    for i in range(out_ref.shape[0]):
        h = first + i
        suffix = jnp.zeros((HEAD_DIM, HEAD_DIM), F32)
        for phase in range(phases):
            there = state_rows(got[phase], i).astype(F32)
            suffix = jnp.where(group == phases - 1 - phase, there, suffix)
        prefix = entering_state(group, got, i).astype(F32)
        here = own_ref[i] + keep[:, h : h + 1] * prefix
        out_ref[i] = suffix + later[:, h : h + 1] * here


def flat_rows(ref, rows_ref):
    rows, steps = ref.shape[0], ref.shape[1]
    for r in range(rows):
        rows_ref[r * steps : (r + 1) * steps, :] = ref[r].astype(F32)


def decode_kernel(count, place_ref, prompt_ref, q_ref, k_ref, v_ref, rate_ref, *rest):
    near, far = rest[:count], rest[count : 2 * count]
    finals = [(c, i) for c, ref in enumerate(near) for i in range(ref.shape[0])]
    out_ref, q_rows, k_rows, v_rows, rate_rows = rest[-5:]
    rows_here, steps = q_ref.shape[0], q_ref.shape[1]
    d_rows = q_rows.shape[0]
    flat_rows(q_ref, q_rows)
    flat_rows(k_ref, k_rows)
    flat_rows(v_ref, v_rows)
    flat_rows(rate_ref, rate_rows)
    rows, cols = identity(d_rows)
    seen = (rows // steps == cols // steps) & (rows >= cols)
    ones = seen.astype(F32)
    rates = rate_rows[...]
    down = -jnp.dot(ones, rates, precision=HIGH, preferred_element_type=F32)
    across = -lax.dot_general(
        rates, ones, (((0,), (1,)), ((), ())), precision=HIGH, preferred_element_type=F32
    )
    grow = jnp.exp(down)
    row_of = lax.broadcasted_iota(jnp.int32, (d_rows, HEAD_DIM), 0) // steps
    prompt = jnp.zeros((d_rows, HEAD_DIM), jnp.int32)
    for r in range(rows_here):
        prompt = jnp.where(row_of == r, prompt_ref[r], prompt)
    mine = prompt == place_ref[1]
    for i in range(rates.shape[1]):
        at = head_slice(i)
        query = q_rows[:, at]
        narrow = query.astype(BF16)
        terms = []
        c, slot = finals[i]
        for ref in (near[c], far[c]):
            top, low = halves(ref[slot])
            both = jnp.dot(
                narrow, jnp.concatenate([top, low], axis=1), preferred_element_type=F32
            )
            terms.append(both[:, :HEAD_DIM] + both[:, HEAD_DIM:])
        base = jnp.where(mine, terms[0], terms[1])
        scores = lax.dot_general(
            query, k_rows[:, at], NT, precision=HIGH, preferred_element_type=F32
        )
        decay = jnp.exp(jnp.where(seen, down[:, i : i + 1] - across[i : i + 1, :], NEGATIVE))
        intra = jnp.dot(scores * decay, v_rows[:, at], precision=HIGH, preferred_element_type=F32)
        q_rows[:, at] = normalize(base * grow[:, i : i + 1] + intra)
    pad = out_ref.shape[0] - d_rows
    value = q_rows[...]
    if pad:
        value = jnp.concatenate([value, jnp.zeros((pad, value.shape[1]), F32)], axis=0)
    out_ref[...] = value.astype(BF16)


def times_weight(rows, weights, column, width):
    total = None
    for i, ref in enumerate(weights):
        depth = ref.shape[0]
        term = jnp.dot(
            rows[:, i * depth : (i + 1) * depth],
            ref[:, pl.ds(column, width)],
            preferred_element_type=F32,
        )
        total = term if total is None else total + term
    return total


def project_kernel(pieces, chunks, place_ref, *rest):
    hidden, weights = rest[:chunks], rest[chunks : chunks + WEIGHT_PARTS]
    outs = rest[-len(pieces) :]
    half = outs[0].shape[1]
    rows = jnp.concatenate([ref[...] for ref in hidden], axis=1)
    for (bits, side), out_ref in zip(pieces, outs):
        column = pl.multiple_of(((place_ref[2] ^ bits) * 2 + side) * half, HEAD_DIM)
        out_ref[...] = times_weight(rows, weights, column, half).astype(out_ref.dtype)


def decode_project_kernel(place_ref, rows_ref, *rest):
    weights, outs = rest[:WEIGHT_PARTS], rest[-4:]
    width = outs[0].shape[1]
    rows = rows_ref[...]
    for bits, out_ref in enumerate(outs):
        column = pl.multiple_of((place_ref[2] ^ bits) * width, HEAD_DIM)
        out_ref[...] = times_weight(rows, weights, column, width).astype(out_ref.dtype)


def relay_kernel(own_ref, got_ref, *rest):
    out_ref = rest[-1]
    out_ref[...] = (own_ref[...] + got_ref[...].astype(F32)).astype(BF16)


def finish_kernel(own_a, own_b, ax, ay, bx, by, d_own, d_x, d_y, d_far, *rest):
    prefill_hbm, decode_ref, out_ref, sems = rest
    width = own_a.shape[1]
    count = sems.shape[0]
    size = out_ref.shape[0] // count
    copies = []
    for c in range(count):
        at = slice(c * size, (c + 1) * size)
        for at_cols, own, x_ref, y_ref in ((0, own_a, ax, ay), (width, own_b, bx, by)):
            total = own[at] + x_ref[at].astype(F32) + y_ref[at].astype(F32)
            out_ref[at, at_cols : at_cols + width] = total.astype(BF16)
        copy = pltpu.make_async_copy(
            out_ref.at[pl.ds(c * size, size)], prefill_hbm.at[0, pl.ds(c * size, size)], sems.at[c]
        )
        copy.start()
        copies.append(copy)
    rows, steps = decode_ref.shape[0], decode_ref.shape[1]
    total = d_own[...] + d_x[...].astype(F32) + d_y[...].astype(F32) + d_far[...].astype(F32)
    for r in range(rows):
        decode_ref[r] = total[r * steps : (r + 1) * steps].astype(BF16)
    for copy in copies:
        copy.wait()


def swap(array, axis, size, bit):
    return lax.ppermute(array, axis, [(i, i ^ bit) for i in range(size)])


def body(
    prefill_query,
    prefill_key,
    prefill_value,
    prefill_rate,
    out_weight,
    decode_query,
    decode_key,
    decode_value,
    decode_rate,
    prompt_of_row,
    *,
    groups,
    reps,
    parts,
):
    length = prefill_query.shape[1]
    features = prefill_query.shape[2]
    heads = prefill_rate.shape[1]
    rows_here, steps = decode_query.shape[0], decode_query.shape[1]
    d_rows = rows_here * steps
    d_pad = -(-d_rows // 16) * 16
    place = jnp.stack([lax.axis_index("ctx"), lax.axis_index("rep"), lax.axis_index("head")])
    place = place.astype(jnp.int32)
    count = min(CHUNKS, heads)
    edges = [heads * c // count for c in range(count + 1)]
    chunks = [(a, b - a) for a, b in zip(edges[:-1], edges[1:])]
    phases = groups - 1
    state_elements = heads * HEAD_DIM * HEAD_DIM

    def in_hbm(array):
        return pltpu.with_memory_space_constraint(array, pltpu.HBM)

    def in_vmem(array):
        return pltpu.with_memory_space_constraint(array, pltpu.VMEM)

    def message_shape(size):
        return sds((size * HEAD_DIM + LOG_ROWS, HEAD_DIM), BF16)

    decode_shape = (rows_here, steps, features)
    made = call(
        first_state_kernel,
        "own_state",
        [SMEM] + [HBM] * 3,
        [
            pltpu.VMEM((chunks[0][1], HEAD_DIM, HEAD_DIM), F32),
            pltpu.VMEM((1, HEAD_DIM), F32),
            pltpu.VMEM((length, heads), F32),
            pltpu.VMEM((1, heads, length), F32),
            pltpu.VMEM((length, features), BF16),
            pltpu.VMEM((length, features), BF16),
            message_shape(chunks[0][1]),
        ],
        [pltpu.SemaphoreType.DMA((3,))],
        cost(4 * length * features * HEAD_DIM, 16 * length * features),
    )(place, in_hbm(prefill_key), in_hbm(prefill_value), in_hbm(prefill_rate))
    own, log_row, columns, rate, keys, values = map(in_vmem, made[:6])
    owns, values_out = [own], [made[6]]
    for c, (first, size) in enumerate(chunks[1:]):
        arrays = (prefill_query, decode_query, decode_key, decode_value) if c == 0 else ()
        made = call(
            functools.partial(more_state_kernel, first, len(arrays)),
            "more_state",
            [VMEM] * 5 + [HBM] * len(arrays),
            [
                pltpu.VMEM((size, HEAD_DIM, HEAD_DIM), F32),
                message_shape(size),
                pltpu.VMEM((heads, length), F32),
            ]
            + [pltpu.VMEM(array.shape, BF16) for array in arrays],
            [pltpu.SemaphoreType.DMA((max(len(arrays), 1),))],
            cost(4 * length * size * HEAD_DIM * HEAD_DIM, 8 * length * features),
        )(keys, values, columns, rate, log_row, *map(in_hbm, arrays))
        owns.append(in_vmem(made[0]))
        values_out.append(made[1])
        if c == 0:
            rows, queries, d_query, d_key, d_value = map(in_vmem, made[2:])

    weight_hbm = in_hbm(out_weight)
    weight_part = pltpu.VMEM((features // WEIGHT_PARTS, out_weight.shape[1]), BF16)
    token = sds((8, HEAD_DIM), F32)
    local, local_token, *weights = call(
        functools.partial(local_kernel, 0),
        "local_attention",
        [VMEM] * 5 + [HBM],
        [pltpu.VMEM((length, features), F32), token] + [weight_part] * EARLY_PARTS,
        [pltpu.SemaphoreType.DMA((EARLY_PARTS,))],
        cost(4 * length * length * features, 12 * length * features, heads * length * length),
    )(queries, keys, values, columns, rows, weight_hbm)
    local = in_vmem(local)

    def load_weight(*after):
        if len(weights) == WEIGHT_PARTS:
            return []
        part, done = call(
            functools.partial(load_kernel, len(weights)),
            "load_weight",
            [HBM] + [ANY] * len(after),
            [weight_part, token],
            [pltpu.SemaphoreType.DMA((1,))],
            cost(1, features // WEIGHT_PARTS * out_weight.shape[1] * 2),
        )(weight_hbm, *after)
        weights.append(part)
        return [done]

    received = []
    after = [local_token]
    for phase in range(phases):
        pairs = [(phase, phase + 1), (groups - 1 - phase, groups - 2 - phase)]
        if phase > 0:
            values_out = []
            for c, (first, size) in enumerate(chunks):
                value = call(
                    functools.partial(chain_kernel, phase, first),
                    "chain",
                    [SMEM, VMEM, VMEM, VMEM] + [ANY] * len(after),
                    message_shape(size),
                    (),
                    cost(2 * size * HEAD_DIM * HEAD_DIM, 24 * size * HEAD_DIM * HEAD_DIM),
                )(place, owns[c], log_row, received[-1][c], *after)
                values_out.append(value)
                after = []
        received.append([lax.ppermute(value, "ctx", pairs) for value in values_out])
    loaded = []
    while len(weights) < WEIGHT_PARTS:
        loaded = load_weight(values_out[-1], *loaded)
    weights = [in_vmem(part) for part in weights]

    after = loaded
    hidden = [
        call(
            functools.partial(hidden_kernel, phases, first),
            "hidden",
            [SMEM] + [VMEM] * (3 + phases) + [ANY] * len(after),
            sds((length, size * HEAD_DIM), BF16),
            (),
            cost(2 * length * size * HEAD_DIM * HEAD_DIM, 20 * length * size * HEAD_DIM),
        )(place, queries, columns, local, *[received[phase][c] for phase in range(phases)], *after)
        for c, (first, size) in enumerate(chunks)
    ]

    def final_states(*after):
        finals = []
        for c, (first, size) in enumerate(chunks):
            gate = after if c == count - 1 else ()
            finals.append(
                call(
                    functools.partial(final_kernel, first, phases),
                    "final_state",
                    [SMEM, VMEM, VMEM] + [VMEM] * phases + [ANY] * len(gate),
                    sds((size, HEAD_DIM, HEAD_DIM), F32),
                    (),
                    cost(4 * state_elements // count, state_elements * 4),
                )(place, owns[c], log_row, *[got[c] for got in received], *gate)
            )
        return finals, [swap(final, "rep", reps, 1) for final in finals]

    def decode_rows(finals, others, *after):
        flat = pltpu.VMEM((d_rows, features), F32)
        return call(
            functools.partial(decode_kernel, count),
            "decode_rows",
            [SMEM, SMEM] + [VMEM] * (4 + 2 * count) + [ANY] * len(after),
            sds((d_pad, features), BF16),
            [flat, flat, flat, pltpu.VMEM((d_rows, heads), F32)],
            cost(16 * d_rows * features * HEAD_DIM, state_elements),
        )(
            place,
            prompt_of_row,
            d_query,
            d_key,
            d_value,
            jnp.transpose(decode_rate, (0, 2, 1)),
            *finals,
            *others,
            *after,
        )

    out_columns = out_weight.shape[1]
    if parts != 4 or (out_columns // parts) % 256 != 0 or length % 64 != 0:
        rows_all = jnp.concatenate([jnp.concatenate(hidden, axis=1), decode_rows(*final_states())], axis=0)
        terms = jnp.dot(rows_all, out_weight, preferred_element_type=F32)
        summed = lax.psum_scatter(terms, "head", scatter_dimension=1, tiled=True)
        prefill_out = summed[:length].astype(BF16)[None]
        decode_out = summed[length : length + d_rows].astype(BF16)
        return prefill_out, decode_out.reshape(rows_here, steps, -1)

    width = out_columns // parts
    half = width // 2

    def project(pieces, dtype, *after):
        return call(
            functools.partial(project_kernel, pieces, count),
            "project",
            [SMEM] + [VMEM] * (count + WEIGHT_PARTS) + [ANY] * len(after),
            [sds((length, half), dtype) for _ in pieces],
            (),
            cost(2 * length * features * half * len(pieces), features * half * 2 * len(pieces)),
        )(place, *hidden, *weights, *after)

    def relay(own_term, got, *after):
        return call(
            relay_kernel,
            "relay",
            [VMEM, VMEM] + [ANY] * len(after),
            sds((length, half), BF16),
            (),
            cost(length * half, length * half * 8),
        )(own_term, got, *after)

    far_a = swap(project([(3, 0)], BF16)[0], "head", parts, 1)
    to_y, = project([(3, 1)], BF16)
    far_b = swap(to_y, "head", parts, 2)
    x_a = swap(project([(1, 0)], BF16)[0], "head", parts, 1)
    y_b = swap(project([(2, 1)], BF16)[0], "head", parts, 2)
    pass_a, pass_b = project([(2, 0), (1, 1)], F32)
    own_a, own_b = project([(0, 0), (0, 1)], F32)
    sent_a, sent_b = relay(pass_a, far_a), relay(pass_b, far_b)
    y_a = swap(sent_a, "head", parts, 2)
    x_b = swap(sent_b, "head", parts, 1)

    d_hidden = decode_rows(*final_states(to_y), sent_a, sent_b)
    d_own, d_x, d_y, d_far = call(
        decode_project_kernel,
        "decode_project",
        [SMEM] + [VMEM] * (1 + WEIGHT_PARTS),
        [sds((d_pad, width), F32)] + [sds((d_pad, width), BF16)] * 3,
        (),
        cost(2 * d_pad * features * out_columns, features * out_columns // 8),
    )(place, d_hidden, *weights)
    prefill_out, decode_out = call(
        finish_kernel,
        "finish",
        [VMEM] * 10,
        [sds((1, length, width), BF16), sds((rows_here, steps, width), BF16)],
        [pltpu.VMEM((length, width), BF16), pltpu.SemaphoreType.DMA((4,))],
        cost(6 * length * half, 20 * length * half),
        out_specs=[HBM, VMEM],
    )(
        own_a,
        own_b,
        x_a,
        y_a,
        x_b,
        y_b,
        d_own,
        swap(d_x, "head", parts, 1),
        swap(d_y, "head", parts, 2),
        swap(d_far, "head", parts, 3),
    )
    return prefill_out, decode_out


def solution(mesh):
    return jax.shard_map(
        functools.partial(
            body, groups=mesh.shape["ctx"], reps=mesh.shape["rep"], parts=mesh.shape["head"]
        ),
        mesh=mesh,
        in_specs=(
            P("rep", "ctx", "head"),
            P("rep", "ctx", "head"),
            P("rep", "ctx", "head"),
            P("rep", "head", "ctx"),
            P("head", None),
            P(("ctx", "rep"), None, "head"),
            P(("ctx", "rep"), None, "head"),
            P(("ctx", "rep"), None, "head"),
            P(("ctx", "rep"), "head", None),
            P(("ctx", "rep")),
        ),
        out_specs=(P("rep", "ctx", "head"), P(("ctx", "rep"), None, "head")),
        check_vma=False,
    )
```

```python
import functools

import jax
import jax.numpy as jnp
from jax import lax
from jax.experimental import pallas as pl
from jax.experimental.pallas import tpu as pltpu
from jax.sharding import PartitionSpec as P

HEAD_DIM = 128
EPSILON = 1e-06
NEGATIVE = -1e30
HIGH = lax.Precision.HIGHEST
CHUNKS = 2
WEIGHT_PARTS = 4
EARLY_PARTS = 3
VMEM_BYTES = 8 * 2**20
F32 = jnp.float32
BF16 = jnp.bfloat16
NT = (((1,), (1,)), ((), ()))
TN = (((0,), (0,)), ((), ()))


def params():
    return pltpu.CompilerParams(vmem_limit_bytes=VMEM_BYTES)


def cost(flops, moved, exps=0):
    return pl.CostEstimate(flops=int(flops), bytes_accessed=int(moved), transcendentals=int(exps))


def normalize(array):
    return array * lax.rsqrt(jnp.mean(array * array, axis=-1, keepdims=True) + EPSILON)


def lower_ones(length):
    rows = lax.broadcasted_iota(jnp.int32, (length, length), 0)
    cols = lax.broadcasted_iota(jnp.int32, (length, length), 1)
    return rows >= cols


def decay_columns(rate, lower):
    return -lax.dot_general(lower.astype(F32), rate, NT, precision=HIGH, preferred_element_type=F32)


def decay_rows(rate, lower):
    return -lax.dot_general(rate, lower.astype(F32), NT, precision=HIGH, preferred_element_type=F32)


def identity(size):
    rows = lax.broadcasted_iota(jnp.int32, (size, size), 0)
    cols = lax.broadcasted_iota(jnp.int32, (size, size), 1)
    return rows, cols


def head_slice(index):
    return slice(index * HEAD_DIM, (index + 1) * HEAD_DIM)


def halves(array):
    top = array.astype(BF16)
    return top, (array - top.astype(F32)).astype(BF16)

VMEM = pl.BlockSpec(memory_space=pltpu.VMEM)
SMEM = pl.BlockSpec(memory_space=pltpu.SMEM)
ANY = pl.BlockSpec(memory_space=pl.ANY)
HBM = pl.BlockSpec(memory_space=pltpu.HBM)


def call(kernel, name, in_specs, out_shape, scratch=(), estimate=None, out_specs=None):
    if out_specs is None:
        out_specs = jax.tree.map(lambda _: VMEM, out_shape)
    return pl.pallas_call(
        kernel,
        in_specs=in_specs,
        out_specs=out_specs,
        out_shape=out_shape,
        scratch_shapes=list(scratch),
        compiler_params=params(),
        cost_estimate=estimate,
        name=name,
    )


def sds(shape, dtype):
    return jax.ShapeDtypeStruct(shape, dtype)


LOG_ROWS = 16


def log_rows(log):
    top = log.astype(BF16).astype(F32)
    mid = (log - top).astype(BF16).astype(F32)
    row = lax.broadcasted_iota(jnp.int32, (LOG_ROWS, HEAD_DIM), 0)
    rest = jnp.where(row == 2, log - top - mid, 0.0)
    return jnp.where(row == 0, top, jnp.where(row == 1, mid, rest)).astype(BF16)


def read_log(message_ref):
    rows = message_ref.shape[0]
    facts = message_ref[rows - LOG_ROWS :, :].astype(F32)
    return facts[0:1] + facts[1:2] + facts[2:3]


def state_rows(message_ref, index):
    return message_ref[index * HEAD_DIM : (index + 1) * HEAD_DIM, :]


def own_states(first, k_ref, v_ref, columns, own_ref, message_ref):
    length = columns.shape[0]
    factor = jnp.exp(columns[length - 1 :, :] - columns)
    for i in range(own_ref.shape[0]):
        h = first + i
        at = head_slice(h)
        weighted = k_ref[:, at].astype(F32) * factor[:, h : h + 1]
        top, rest = halves(weighted)
        both = lax.dot_general(
            jnp.concatenate([top, rest], axis=1), v_ref[:, at], TN, preferred_element_type=F32
        )
        state = both[:HEAD_DIM] + both[HEAD_DIM:]
        own_ref[i] = state
        message_ref[i * HEAD_DIM : (i + 1) * HEAD_DIM, :] = state.astype(BF16)


def started(pairs, sems):
    copies = [
        pltpu.make_async_copy(source, target, sems.at[i]) for i, (source, target) in enumerate(pairs)
    ]
    for copy in copies:
        copy.start()
    return copies


def first_state_kernel(place_ref, k_hbm, v_hbm, rate_hbm, *refs):
    own_ref, log_ref, col_ref, rate_ref, k_ref, v_ref, message_ref, sems = refs
    copies = started(((rate_hbm, rate_ref), (k_hbm.at[0], k_ref), (v_hbm.at[0], v_ref)), sems)
    length = k_ref.shape[0]
    copies[0].wait()
    rate = rate_ref[0]
    columns = decay_columns(rate, lower_ones(length))
    col_ref[...] = columns
    log_ref[...] = jnp.zeros_like(log_ref)
    log_ref[:, : rate.shape[0]] = columns[length - 1 :, :]
    message_ref[message_ref.shape[0] - LOG_ROWS :, :] = log_rows(log_ref[...])
    copies[1].wait()
    copies[2].wait()
    own_states(0, k_ref, v_ref, columns, own_ref, message_ref)


def more_state_kernel(first, copied, k_ref, v_ref, col_ref, rate_ref, log_ref, *refs):
    sources, refs = refs[:copied], refs[copied:]
    own_ref, message_ref, row_ref = refs[:3]
    targets, sems = refs[3 : 3 + copied], refs[3 + copied]
    copies = started(tuple(zip(sources, targets)), sems) if copied else []
    row_ref[...] = decay_rows(rate_ref[0], lower_ones(k_ref.shape[0]))
    message_ref[message_ref.shape[0] - LOG_ROWS :, :] = log_rows(log_ref[...])
    own_states(first, k_ref, v_ref, col_ref[...], own_ref, message_ref)
    for copy in copies:
        copy.wait()


def chain_kernel(phase, first, place_ref, own_ref, log_ref, got_ref, *rest):
    out_ref = rest[-1]
    size = (out_ref.shape[0] - LOG_ROWS) // HEAD_DIM
    right = place_ref[0] == phase
    log = log_ref[...]
    later = read_log(got_ref)
    own_factor = jnp.where(right, 1.0, jnp.exp(later))
    got_factor = jnp.where(right, jnp.exp(log), 1.0)
    for i in range(size):
        h = first + i
        value = (
            own_factor[:, h : h + 1] * own_ref[i]
            + got_factor[:, h : h + 1] * state_rows(got_ref, i).astype(F32)
        )
        out_ref[i * HEAD_DIM : (i + 1) * HEAD_DIM, :] = value.astype(BF16)
    out_ref[size * HEAD_DIM :, :] = log_rows(log + later)


def entering_state(group, got, index):
    state = state_rows(got[0], index)
    for phase in range(1, len(got)):
        state = jnp.where(group == phase + 1, state_rows(got[phase], index), state)
    return jnp.where(group == 0, jnp.zeros_like(state), state)


def weight_copies(places, weight_hbm, weights, sems):
    copies = []
    for i, (index, ref) in enumerate(zip(places, weights)):
        depth = ref.shape[0]
        copies.append(
            pltpu.make_async_copy(weight_hbm.at[pl.ds(index * depth, depth)], ref, sems.at[i])
        )
    for copy in copies:
        copy.start()
    return copies


def load_kernel(index, weight_hbm, *rest):
    weight_ref, token_ref, sems = rest[-3:]
    copies = weight_copies([index], weight_hbm, [weight_ref], sems)
    token_ref[...] = jnp.zeros_like(token_ref)
    for copy in copies:
        copy.wait()


def local_kernel(first, q_ref, k_ref, v_ref, col_ref, row_ref, weight_hbm, *rest):
    local_ref, token_ref = rest[:2]
    weights, sems = rest[2:-1], rest[-1]
    copies = weight_copies(range(len(weights)), weight_hbm, weights, sems)
    token_ref[...] = jnp.zeros_like(token_ref)
    lower = lower_ones(q_ref.shape[1])
    for i in range(local_ref.shape[1] // HEAD_DIM):
        h = first + i
        at = head_slice(h)
        scores = lax.dot_general(q_ref[0, :, at], k_ref[:, at], NT, preferred_element_type=F32)
        decay = jnp.exp(
            jnp.where(lower, col_ref[:, h : h + 1] - row_ref[h : h + 1, :], NEGATIVE)
        )
        narrow = (scores * decay).astype(BF16)
        local_ref[:, head_slice(i)] = jnp.dot(narrow, v_ref[:, at], preferred_element_type=F32)
    for copy in copies:
        copy.wait()


def hidden_kernel(phases, first, place_ref, q_ref, col_ref, local_ref, *rest):
    got, hidden_ref = rest[:phases], rest[-1]
    for i in range(hidden_ref.shape[1] // HEAD_DIM):
        h = first + i
        whole = head_slice(h)
        state = entering_state(place_ref[0], got, i)
        inter = jnp.dot(q_ref[0, :, whole], state, preferred_element_type=F32)
        attended = local_ref[:, whole] + inter * jnp.exp(col_ref[:, h : h + 1])
        hidden_ref[:, head_slice(i)] = normalize(attended).astype(BF16)


def final_kernel(first, phases, place_ref, own_ref, log_ref, *rest):
    got, out_ref = rest[:phases], rest[-1]
    group = place_ref[0]
    keep = jnp.exp(log_ref[...])
    later = jnp.zeros((1, HEAD_DIM), F32)
    for phase in range(phases):
        later = jnp.where(group == phases - 1 - phase, read_log(got[phase]), later)
    later = jnp.exp(later)
    for i in range(out_ref.shape[0]):
        h = first + i
        suffix = jnp.zeros((HEAD_DIM, HEAD_DIM), F32)
        for phase in range(phases):
            there = state_rows(got[phase], i).astype(F32)
            suffix = jnp.where(group == phases - 1 - phase, there, suffix)
        prefix = entering_state(group, got, i).astype(F32)
        here = own_ref[i] + keep[:, h : h + 1] * prefix
        out_ref[i] = suffix + later[:, h : h + 1] * here


def flat_rows(ref, rows_ref):
    rows, steps = ref.shape[0], ref.shape[1]
    for r in range(rows):
        rows_ref[r * steps : (r + 1) * steps, :] = ref[r].astype(F32)


def decode_kernel(count, place_ref, prompt_ref, q_ref, k_ref, v_ref, rate_ref, *rest):
    near, far = rest[:count], rest[count : 2 * count]
    finals = [(c, i) for c, ref in enumerate(near) for i in range(ref.shape[0])]
    out_ref, q_rows, k_rows, v_rows, rate_rows = rest[-5:]
    rows_here, steps = q_ref.shape[0], q_ref.shape[1]
    d_rows = q_rows.shape[0]
    flat_rows(q_ref, q_rows)
    flat_rows(k_ref, k_rows)
    flat_rows(v_ref, v_rows)
    flat_rows(rate_ref, rate_rows)
    rows, cols = identity(d_rows)
    seen = (rows // steps == cols // steps) & (rows >= cols)
    ones = seen.astype(F32)
    rates = rate_rows[...]
    down = -jnp.dot(ones, rates, precision=HIGH, preferred_element_type=F32)
    across = -lax.dot_general(
        rates, ones, (((0,), (1,)), ((), ())), precision=HIGH, preferred_element_type=F32
    )
    grow = jnp.exp(down)
    row_of = lax.broadcasted_iota(jnp.int32, (d_rows, HEAD_DIM), 0) // steps
    prompt = jnp.zeros((d_rows, HEAD_DIM), jnp.int32)
    for r in range(rows_here):
        prompt = jnp.where(row_of == r, prompt_ref[r], prompt)
    mine = prompt == place_ref[1]
    for i in range(rates.shape[1]):
        at = head_slice(i)
        query = q_rows[:, at]
        narrow = query.astype(BF16)
        terms = []
        c, slot = finals[i]
        for ref in (near[c], far[c]):
            top, low = halves(ref[slot])
            both = jnp.dot(
                narrow, jnp.concatenate([top, low], axis=1), preferred_element_type=F32
            )
            terms.append(both[:, :HEAD_DIM] + both[:, HEAD_DIM:])
        base = jnp.where(mine, terms[0], terms[1])
        scores = lax.dot_general(
            query, k_rows[:, at], NT, precision=HIGH, preferred_element_type=F32
        )
        decay = jnp.exp(jnp.where(seen, down[:, i : i + 1] - across[i : i + 1, :], NEGATIVE))
        intra = jnp.dot(scores * decay, v_rows[:, at], precision=HIGH, preferred_element_type=F32)
        q_rows[:, at] = normalize(base * grow[:, i : i + 1] + intra)
    pad = out_ref.shape[0] - d_rows
    value = q_rows[...]
    if pad:
        value = jnp.concatenate([value, jnp.zeros((pad, value.shape[1]), F32)], axis=0)
    out_ref[...] = value.astype(BF16)


def times_weight(rows, weights, column, width):
    total = None
    for i, ref in enumerate(weights):
        depth = ref.shape[0]
        term = jnp.dot(
            rows[:, i * depth : (i + 1) * depth],
            ref[:, pl.ds(column, width)],
            preferred_element_type=F32,
        )
        total = term if total is None else total + term
    return total


def project_kernel(pieces, chunks, place_ref, *rest):
    hidden, weights = rest[:chunks], rest[chunks : chunks + WEIGHT_PARTS]
    outs = rest[-len(pieces) :]
    half = outs[0].shape[1]
    rows = jnp.concatenate([ref[...] for ref in hidden], axis=1)
    for (bits, side), out_ref in zip(pieces, outs):
        column = pl.multiple_of(((place_ref[2] ^ bits) * 2 + side) * half, HEAD_DIM)
        out_ref[...] = times_weight(rows, weights, column, half).astype(out_ref.dtype)


def decode_project_kernel(place_ref, rows_ref, *rest):
    weights, outs = rest[:WEIGHT_PARTS], rest[-4:]
    width = outs[0].shape[1]
    rows = rows_ref[...]
    for bits, out_ref in enumerate(outs):
        column = pl.multiple_of((place_ref[2] ^ bits) * width, HEAD_DIM)
        out_ref[...] = times_weight(rows, weights, column, width).astype(out_ref.dtype)


def relay_kernel(own_ref, got_ref, *rest):
    out_ref = rest[-1]
    out_ref[...] = (own_ref[...] + got_ref[...].astype(F32)).astype(BF16)


def finish_kernel(own_a, own_b, ax, ay, bx, by, d_own, d_x, d_y, d_far, *rest):
    prefill_hbm, decode_ref, out_ref, sems = rest
    width = own_a.shape[1]
    count = sems.shape[0]
    size = out_ref.shape[0] // count
    copies = []
    for c in range(count):
        at = slice(c * size, (c + 1) * size)
        for at_cols, own, x_ref, y_ref in ((0, own_a, ax, ay), (width, own_b, bx, by)):
            total = own[at] + x_ref[at].astype(F32) + y_ref[at].astype(F32)
            out_ref[at, at_cols : at_cols + width] = total.astype(BF16)
        copy = pltpu.make_async_copy(
            out_ref.at[pl.ds(c * size, size)], prefill_hbm.at[0, pl.ds(c * size, size)], sems.at[c]
        )
        copy.start()
        copies.append(copy)
    rows, steps = decode_ref.shape[0], decode_ref.shape[1]
    total = d_own[...] + d_x[...].astype(F32) + d_y[...].astype(F32) + d_far[...].astype(F32)
    for r in range(rows):
        decode_ref[r] = total[r * steps : (r + 1) * steps].astype(BF16)
    for copy in copies:
        copy.wait()


def swap(array, axis, size, bit):
    return lax.ppermute(array, axis, [(i, i ^ bit) for i in range(size)])


def body(
    prefill_query,
    prefill_key,
    prefill_value,
    prefill_rate,
    out_weight,
    decode_query,
    decode_key,
    decode_value,
    decode_rate,
    prompt_of_row,
    *,
    groups,
    reps,
    parts,
):
    length = prefill_query.shape[1]
    features = prefill_query.shape[2]
    heads = prefill_rate.shape[1]
    rows_here, steps = decode_query.shape[0], decode_query.shape[1]
    d_rows = rows_here * steps
    d_pad = -(-d_rows // 16) * 16
    place = jnp.stack([lax.axis_index("ctx"), lax.axis_index("rep"), lax.axis_index("head")])
    place = place.astype(jnp.int32)
    count = min(CHUNKS, heads)
    edges = [heads * c // count for c in range(count + 1)]
    chunks = [(a, b - a) for a, b in zip(edges[:-1], edges[1:])]
    phases = groups - 1
    state_elements = heads * HEAD_DIM * HEAD_DIM

    def in_hbm(array):
        return pltpu.with_memory_space_constraint(array, pltpu.HBM)

    def in_vmem(array):
        return pltpu.with_memory_space_constraint(array, pltpu.VMEM)

    def message_shape(size):
        return sds((size * HEAD_DIM + LOG_ROWS, HEAD_DIM), BF16)

    decode_shape = (rows_here, steps, features)
    made = call(
        first_state_kernel,
        "own_state",
        [SMEM] + [HBM] * 3,
        [
            pltpu.VMEM((chunks[0][1], HEAD_DIM, HEAD_DIM), F32),
            pltpu.VMEM((1, HEAD_DIM), F32),
            pltpu.VMEM((length, heads), F32),
            pltpu.VMEM((1, heads, length), F32),
            pltpu.VMEM((length, features), BF16),
            pltpu.VMEM((length, features), BF16),
            message_shape(chunks[0][1]),
        ],
        [pltpu.SemaphoreType.DMA((3,))],
        cost(4 * length * features * HEAD_DIM, 16 * length * features),
    )(place, in_hbm(prefill_key), in_hbm(prefill_value), in_hbm(prefill_rate))
    own, log_row, columns, rate, keys, values = map(in_vmem, made[:6])
    owns, values_out = [own], [made[6]]
    for c, (first, size) in enumerate(chunks[1:]):
        arrays = (prefill_query, decode_query, decode_key, decode_value) if c == 0 else ()
        made = call(
            functools.partial(more_state_kernel, first, len(arrays)),
            "more_state",
            [VMEM] * 5 + [HBM] * len(arrays),
            [
                pltpu.VMEM((size, HEAD_DIM, HEAD_DIM), F32),
                message_shape(size),
                pltpu.VMEM((heads, length), F32),
            ]
            + [pltpu.VMEM(array.shape, BF16) for array in arrays],
            [pltpu.SemaphoreType.DMA((max(len(arrays), 1),))],
            cost(4 * length * size * HEAD_DIM * HEAD_DIM, 8 * length * features),
        )(keys, values, columns, rate, log_row, *map(in_hbm, arrays))
        owns.append(in_vmem(made[0]))
        values_out.append(made[1])
        if c == 0:
            rows, queries, d_query, d_key, d_value = map(in_vmem, made[2:])

    weight_hbm = in_hbm(out_weight)
    weight_part = pltpu.VMEM((features // WEIGHT_PARTS, out_weight.shape[1]), BF16)
    token = sds((8, HEAD_DIM), F32)
    local, local_token, *weights = call(
        functools.partial(local_kernel, 0),
        "local_attention",
        [VMEM] * 5 + [HBM],
        [pltpu.VMEM((length, features), F32), token] + [weight_part] * EARLY_PARTS,
        [pltpu.SemaphoreType.DMA((EARLY_PARTS,))],
        cost(4 * length * length * features, 12 * length * features, heads * length * length),
    )(queries, keys, values, columns, rows, weight_hbm)
    local = in_vmem(local)

    def load_weight(*after):
        if len(weights) == WEIGHT_PARTS:
            return []
        part, done = call(
            functools.partial(load_kernel, len(weights)),
            "load_weight",
            [HBM] + [ANY] * len(after),
            [weight_part, token],
            [pltpu.SemaphoreType.DMA((1,))],
            cost(1, features // WEIGHT_PARTS * out_weight.shape[1] * 2),
        )(weight_hbm, *after)
        weights.append(part)
        return [done]

    received = []
    after = [local_token]
    for phase in range(phases):
        target = list(range(groups))
        for low in (phase, groups - 2 - phase):
            target[low], target[low + 1] = low + 1, low
        pairs = list(enumerate(target))
        if phase > 0:
            values_out = []
            for c, (first, size) in enumerate(chunks):
                value = call(
                    functools.partial(chain_kernel, phase, first),
                    "chain",
                    [SMEM, VMEM, VMEM, VMEM] + [ANY] * len(after),
                    message_shape(size),
                    (),
                    cost(2 * size * HEAD_DIM * HEAD_DIM, 24 * size * HEAD_DIM * HEAD_DIM),
                )(place, owns[c], log_row, received[-1][c], *after)
                values_out.append(value)
                after = []
        received.append([lax.ppermute(value, "ctx", pairs) for value in values_out])
    loaded = []
    while len(weights) < WEIGHT_PARTS:
        loaded = load_weight(values_out[-1], *loaded)
    weights = [in_vmem(part) for part in weights]

    after = loaded
    hidden = [
        call(
            functools.partial(hidden_kernel, phases, first),
            "hidden",
            [SMEM] + [VMEM] * (3 + phases) + [ANY] * len(after),
            sds((length, size * HEAD_DIM), BF16),
            (),
            cost(2 * length * size * HEAD_DIM * HEAD_DIM, 20 * length * size * HEAD_DIM),
        )(place, queries, columns, local, *[received[phase][c] for phase in range(phases)], *after)
        for c, (first, size) in enumerate(chunks)
    ]

    def final_states(*after):
        finals = []
        for c, (first, size) in enumerate(chunks):
            gate = after if c == count - 1 else ()
            finals.append(
                call(
                    functools.partial(final_kernel, first, phases),
                    "final_state",
                    [SMEM, VMEM, VMEM] + [VMEM] * phases + [ANY] * len(gate),
                    sds((size, HEAD_DIM, HEAD_DIM), F32),
                    (),
                    cost(4 * state_elements // count, state_elements * 4),
                )(place, owns[c], log_row, *[got[c] for got in received], *gate)
            )
        return finals, [swap(final, "rep", reps, 1) for final in finals]

    def decode_rows(finals, others, *after):
        flat = pltpu.VMEM((d_rows, features), F32)
        return call(
            functools.partial(decode_kernel, count),
            "decode_rows",
            [SMEM, SMEM] + [VMEM] * (4 + 2 * count) + [ANY] * len(after),
            sds((d_pad, features), BF16),
            [flat, flat, flat, pltpu.VMEM((d_rows, heads), F32)],
            cost(16 * d_rows * features * HEAD_DIM, state_elements),
        )(
            place,
            prompt_of_row,
            d_query,
            d_key,
            d_value,
            jnp.transpose(decode_rate, (0, 2, 1)),
            *finals,
            *others,
            *after,
        )

    out_columns = out_weight.shape[1]
    if parts != 4 or (out_columns // parts) % 256 != 0 or length % 64 != 0:
        rows_all = jnp.concatenate([jnp.concatenate(hidden, axis=1), decode_rows(*final_states())], axis=0)
        terms = jnp.dot(rows_all, out_weight, preferred_element_type=F32)
        summed = lax.psum_scatter(terms, "head", scatter_dimension=1, tiled=True)
        prefill_out = summed[:length].astype(BF16)[None]
        decode_out = summed[length : length + d_rows].astype(BF16)
        return prefill_out, decode_out.reshape(rows_here, steps, -1)

    width = out_columns // parts
    half = width // 2

    def project(pieces, dtype, *after):
        return call(
            functools.partial(project_kernel, pieces, count),
            "project",
            [SMEM] + [VMEM] * (count + WEIGHT_PARTS) + [ANY] * len(after),
            [sds((length, half), dtype) for _ in pieces],
            (),
            cost(2 * length * features * half * len(pieces), features * half * 2 * len(pieces)),
        )(place, *hidden, *weights, *after)

    def relay(own_term, got, *after):
        return call(
            relay_kernel,
            "relay",
            [VMEM, VMEM] + [ANY] * len(after),
            sds((length, half), BF16),
            (),
            cost(length * half, length * half * 8),
        )(own_term, got, *after)

    to_x, to_y = project([(3, 0), (3, 1)], BF16)
    far_a = swap(to_x, "head", parts, 1)
    far_b = swap(to_y, "head", parts, 2)
    x_a = swap(project([(1, 0)], BF16)[0], "head", parts, 1)
    y_b = swap(project([(2, 1)], BF16)[0], "head", parts, 2)
    pass_a, pass_b = project([(2, 0), (1, 1)], F32)
    own_a, own_b = project([(0, 0), (0, 1)], F32)
    sent_a, sent_b = relay(pass_a, far_a), relay(pass_b, far_b)
    y_a = swap(sent_a, "head", parts, 2)
    x_b = swap(sent_b, "head", parts, 1)

    d_hidden = decode_rows(*final_states(to_y), sent_a, sent_b)
    d_own, d_x, d_y, d_far = call(
        decode_project_kernel,
        "decode_project",
        [SMEM] + [VMEM] * (1 + WEIGHT_PARTS),
        [sds((d_pad, width), F32)] + [sds((d_pad, width), BF16)] * 3,
        (),
        cost(2 * d_pad * features * out_columns, features * out_columns // 8),
    )(place, d_hidden, *weights)
    prefill_out, decode_out = call(
        finish_kernel,
        "finish",
        [VMEM] * 10,
        [sds((1, length, width), BF16), sds((rows_here, steps, width), BF16)],
        [pltpu.VMEM((length, width), BF16), pltpu.SemaphoreType.DMA((4,))],
        cost(6 * length * half, 20 * length * half),
        out_specs=[HBM, VMEM],
    )(
        own_a,
        own_b,
        x_a,
        y_a,
        x_b,
        y_b,
        d_own,
        swap(d_x, "head", parts, 1),
        swap(d_y, "head", parts, 2),
        swap(d_far, "head", parts, 3),
    )
    return prefill_out, decode_out


def solution(mesh):
    return jax.shard_map(
        functools.partial(
            body, groups=mesh.shape["ctx"], reps=mesh.shape["rep"], parts=mesh.shape["head"]
        ),
        mesh=mesh,
        in_specs=(
            P("rep", "ctx", "head"),
            P("rep", "ctx", "head"),
            P("rep", "ctx", "head"),
            P("rep", "head", "ctx"),
            P("head", None),
            P(("ctx", "rep"), None, "head"),
            P(("ctx", "rep"), None, "head"),
            P(("ctx", "rep"), None, "head"),
            P(("ctx", "rep"), "head", None),
            P(("ctx", "rep")),
        ),
        out_specs=(P("rep", "ctx", "head"), P(("ctx", "rep"), None, "head")),
        check_vma=False,
    )
```

```python
import functools

import jax
import jax.numpy as jnp
from jax import lax
from jax.experimental import pallas as pl
from jax.experimental.pallas import tpu as pltpu
from jax.sharding import PartitionSpec as P

HEAD_DIM = 128
EPSILON = 1e-06
NEGATIVE = -1e30
HIGH = lax.Precision.HIGHEST
CHUNKS = 2
WEIGHT_PARTS = 4
EARLY_PARTS = 2
VMEM_BYTES = 8 * 2**20
F32 = jnp.float32
BF16 = jnp.bfloat16
NT = (((1,), (1,)), ((), ()))
TN = (((0,), (0,)), ((), ()))


def params():
    return pltpu.CompilerParams(vmem_limit_bytes=VMEM_BYTES)


def cost(flops, moved, exps=0):
    return pl.CostEstimate(flops=int(flops), bytes_accessed=int(moved), transcendentals=int(exps))


def normalize(array):
    return array * lax.rsqrt(jnp.mean(array * array, axis=-1, keepdims=True) + EPSILON)


def lower_ones(length):
    rows = lax.broadcasted_iota(jnp.int32, (length, length), 0)
    cols = lax.broadcasted_iota(jnp.int32, (length, length), 1)
    return rows >= cols


def decay_columns(rate, lower):
    return -lax.dot_general(lower.astype(F32), rate, NT, precision=HIGH, preferred_element_type=F32)


def decay_rows(rate, lower):
    return -lax.dot_general(rate, lower.astype(F32), NT, precision=HIGH, preferred_element_type=F32)


def identity(size):
    rows = lax.broadcasted_iota(jnp.int32, (size, size), 0)
    cols = lax.broadcasted_iota(jnp.int32, (size, size), 1)
    return rows, cols


def head_slice(index):
    return slice(index * HEAD_DIM, (index + 1) * HEAD_DIM)


def halves(array):
    top = array.astype(BF16)
    return top, (array - top.astype(F32)).astype(BF16)

VMEM = pl.BlockSpec(memory_space=pltpu.VMEM)
SMEM = pl.BlockSpec(memory_space=pltpu.SMEM)
ANY = pl.BlockSpec(memory_space=pl.ANY)
HBM = pl.BlockSpec(memory_space=pltpu.HBM)


def call(kernel, name, in_specs, out_shape, scratch=(), estimate=None, out_specs=None):
    if out_specs is None:
        out_specs = jax.tree.map(lambda _: VMEM, out_shape)
    return pl.pallas_call(
        kernel,
        in_specs=in_specs,
        out_specs=out_specs,
        out_shape=out_shape,
        scratch_shapes=list(scratch),
        compiler_params=params(),
        cost_estimate=estimate,
        name=name,
    )


def sds(shape, dtype):
    return jax.ShapeDtypeStruct(shape, dtype)


LOG_ROWS = 16


def log_rows(log):
    top = log.astype(BF16).astype(F32)
    mid = (log - top).astype(BF16).astype(F32)
    row = lax.broadcasted_iota(jnp.int32, (LOG_ROWS, HEAD_DIM), 0)
    rest = jnp.where(row == 2, log - top - mid, 0.0)
    return jnp.where(row == 0, top, jnp.where(row == 1, mid, rest)).astype(BF16)


def read_log(message_ref):
    rows = message_ref.shape[0]
    facts = message_ref[rows - LOG_ROWS :, :].astype(F32)
    return facts[0:1] + facts[1:2] + facts[2:3]


def state_rows(message_ref, index):
    return message_ref[index * HEAD_DIM : (index + 1) * HEAD_DIM, :]


def own_states(first, k_ref, v_ref, columns, own_ref, message_ref):
    length = columns.shape[0]
    factor = jnp.exp(columns[length - 1 :, :] - columns)
    for i in range(own_ref.shape[0]):
        h = first + i
        at = head_slice(h)
        weighted = k_ref[:, at].astype(F32) * factor[:, h : h + 1]
        top, rest = halves(weighted)
        both = lax.dot_general(
            jnp.concatenate([top, rest], axis=1), v_ref[:, at], TN, preferred_element_type=F32
        )
        state = both[:HEAD_DIM] + both[HEAD_DIM:]
        own_ref[i] = state
        message_ref[i * HEAD_DIM : (i + 1) * HEAD_DIM, :] = state.astype(BF16)


def started(pairs, sems):
    copies = [
        pltpu.make_async_copy(source, target, sems.at[i]) for i, (source, target) in enumerate(pairs)
    ]
    for copy in copies:
        copy.start()
    return copies


def first_state_kernel(place_ref, k_hbm, v_hbm, rate_hbm, *refs):
    own_ref, log_ref, col_ref, rate_ref, k_ref, v_ref, message_ref, sems = refs
    copies = started(((rate_hbm, rate_ref), (k_hbm.at[0], k_ref), (v_hbm.at[0], v_ref)), sems)
    length = k_ref.shape[0]
    copies[0].wait()
    rate = rate_ref[0]
    columns = decay_columns(rate, lower_ones(length))
    col_ref[...] = columns
    log_ref[...] = jnp.zeros_like(log_ref)
    log_ref[:, : rate.shape[0]] = columns[length - 1 :, :]
    message_ref[message_ref.shape[0] - LOG_ROWS :, :] = log_rows(log_ref[...])
    copies[1].wait()
    copies[2].wait()
    own_states(0, k_ref, v_ref, columns, own_ref, message_ref)


def more_state_kernel(first, k_ref, v_ref, col_ref, log_ref, *rest):
    own_ref, message_ref = rest[-2:]
    message_ref[message_ref.shape[0] - LOG_ROWS :, :] = log_rows(log_ref[...])
    own_states(first, k_ref, v_ref, col_ref[...], own_ref, message_ref)


def chain_kernel(phase, first, place_ref, own_ref, log_ref, got_ref, *rest):
    out_ref = rest[-1]
    size = (out_ref.shape[0] - LOG_ROWS) // HEAD_DIM
    right = place_ref[0] == phase
    log = log_ref[...]
    later = read_log(got_ref)
    own_factor = jnp.where(right, 1.0, jnp.exp(later))
    got_factor = jnp.where(right, jnp.exp(log), 1.0)
    for i in range(size):
        h = first + i
        value = (
            own_factor[:, h : h + 1] * own_ref[i]
            + got_factor[:, h : h + 1] * state_rows(got_ref, i).astype(F32)
        )
        out_ref[i * HEAD_DIM : (i + 1) * HEAD_DIM, :] = value.astype(BF16)
    out_ref[size * HEAD_DIM :, :] = log_rows(log + later)


def entering_state(group, got, index):
    state = state_rows(got[0], index)
    for phase in range(1, len(got)):
        state = jnp.where(group == phase + 1, state_rows(got[phase], index), state)
    return jnp.where(group == 0, jnp.zeros_like(state), state)


def weight_copies(places, weight_hbm, weights, sems):
    copies = []
    for i, (index, ref) in enumerate(zip(places, weights)):
        depth = ref.shape[0]
        copies.append(
            pltpu.make_async_copy(weight_hbm.at[pl.ds(index * depth, depth)], ref, sems.at[i])
        )
    for copy in copies:
        copy.start()
    return copies


def load_kernel(index, weight_hbm, *rest):
    weight_ref, token_ref, sems = rest[-3:]
    copies = weight_copies([index], weight_hbm, [weight_ref], sems)
    token_ref[...] = jnp.zeros_like(token_ref)
    for copy in copies:
        copy.wait()


def local_kernel(copied, k_ref, v_ref, col_ref, rate_ref, weight_hbm, *rest):
    sources, rest = rest[:copied], rest[copied:]
    targets, rest = rest[:copied], rest[copied:]
    local_ref, token_ref = rest[:2]
    weights, sems, more = rest[2:-2], rest[-2], rest[-1]
    loads = started(tuple(zip(sources, targets)), more)
    copies = weight_copies(range(len(weights)), weight_hbm, weights, sems)
    token_ref[...] = jnp.zeros_like(token_ref)
    q_ref = targets[0]
    lower = lower_ones(k_ref.shape[0])
    rows = decay_rows(rate_ref[0], lower)
    loads[0].wait()
    for h in range(local_ref.shape[1] // HEAD_DIM):
        at = head_slice(h)
        scores = lax.dot_general(q_ref[0, :, at], k_ref[:, at], NT, preferred_element_type=F32)
        decay = jnp.exp(jnp.where(lower, col_ref[:, h : h + 1] - rows[h : h + 1, :], NEGATIVE))
        narrow = (scores * decay).astype(BF16)
        local_ref[:, at] = jnp.dot(narrow, v_ref[:, at], preferred_element_type=F32)
    for copy in loads[1:] + copies:
        copy.wait()


def hidden_kernel(phases, first, place_ref, q_ref, col_ref, local_ref, *rest):
    got, hidden_ref = rest[:phases], rest[-1]
    for i in range(hidden_ref.shape[1] // HEAD_DIM):
        h = first + i
        whole = head_slice(h)
        state = entering_state(place_ref[0], got, i)
        inter = jnp.dot(q_ref[0, :, whole], state, preferred_element_type=F32)
        attended = local_ref[:, whole] + inter * jnp.exp(col_ref[:, h : h + 1])
        hidden_ref[:, head_slice(i)] = normalize(attended).astype(BF16)


def final_kernel(first, phases, place_ref, own_ref, log_ref, *rest):
    got, out_ref = rest[:phases], rest[-1]
    group = place_ref[0]
    keep = jnp.exp(log_ref[...])
    later = jnp.zeros((1, HEAD_DIM), F32)
    for phase in range(phases):
        later = jnp.where(group == phases - 1 - phase, read_log(got[phase]), later)
    later = jnp.exp(later)
    for i in range(out_ref.shape[0]):
        h = first + i
        suffix = jnp.zeros((HEAD_DIM, HEAD_DIM), F32)
        for phase in range(phases):
            there = state_rows(got[phase], i).astype(F32)
            suffix = jnp.where(group == phases - 1 - phase, there, suffix)
        prefix = entering_state(group, got, i).astype(F32)
        here = own_ref[i] + keep[:, h : h + 1] * prefix
        out_ref[i] = suffix + later[:, h : h + 1] * here


def flat_rows(ref, rows_ref):
    rows, steps = ref.shape[0], ref.shape[1]
    for r in range(rows):
        rows_ref[r * steps : (r + 1) * steps, :] = ref[r].astype(F32)


def decode_kernel(count, place_ref, prompt_ref, q_ref, k_ref, v_ref, rate_ref, *rest):
    near, far = rest[:count], rest[count : 2 * count]
    finals = [(c, i) for c, ref in enumerate(near) for i in range(ref.shape[0])]
    out_ref, q_rows, k_rows, v_rows, rate_rows = rest[-5:]
    rows_here, steps = q_ref.shape[0], q_ref.shape[1]
    d_rows = q_rows.shape[0]
    flat_rows(q_ref, q_rows)
    flat_rows(k_ref, k_rows)
    flat_rows(v_ref, v_rows)
    flat_rows(rate_ref, rate_rows)
    rows, cols = identity(d_rows)
    seen = (rows // steps == cols // steps) & (rows >= cols)
    ones = seen.astype(F32)
    rates = rate_rows[...]
    down = -jnp.dot(ones, rates, precision=HIGH, preferred_element_type=F32)
    across = -lax.dot_general(
        rates, ones, (((0,), (1,)), ((), ())), precision=HIGH, preferred_element_type=F32
    )
    grow = jnp.exp(down)
    row_of = lax.broadcasted_iota(jnp.int32, (d_rows, HEAD_DIM), 0) // steps
    prompt = jnp.zeros((d_rows, HEAD_DIM), jnp.int32)
    for r in range(rows_here):
        prompt = jnp.where(row_of == r, prompt_ref[r], prompt)
    mine = prompt == place_ref[1]
    for i in range(rates.shape[1]):
        at = head_slice(i)
        query = q_rows[:, at]
        narrow = query.astype(BF16)
        terms = []
        c, slot = finals[i]
        for ref in (near[c], far[c]):
            top, low = halves(ref[slot])
            both = jnp.dot(
                narrow, jnp.concatenate([top, low], axis=1), preferred_element_type=F32
            )
            terms.append(both[:, :HEAD_DIM] + both[:, HEAD_DIM:])
        base = jnp.where(mine, terms[0], terms[1])
        scores = lax.dot_general(
            query, k_rows[:, at], NT, precision=HIGH, preferred_element_type=F32
        )
        decay = jnp.exp(jnp.where(seen, down[:, i : i + 1] - across[i : i + 1, :], NEGATIVE))
        intra = jnp.dot(scores * decay, v_rows[:, at], precision=HIGH, preferred_element_type=F32)
        q_rows[:, at] = normalize(base * grow[:, i : i + 1] + intra)
    pad = out_ref.shape[0] - d_rows
    value = q_rows[...]
    if pad:
        value = jnp.concatenate([value, jnp.zeros((pad, value.shape[1]), F32)], axis=0)
    out_ref[...] = value.astype(BF16)


def times_weight(rows, weights, column, width):
    total = None
    for i, ref in enumerate(weights):
        depth = ref.shape[0]
        term = jnp.dot(
            rows[:, i * depth : (i + 1) * depth],
            ref[:, pl.ds(column, width)],
            preferred_element_type=F32,
        )
        total = term if total is None else total + term
    return total


def project_kernel(pieces, chunks, place_ref, *rest):
    hidden, weights = rest[:chunks], rest[chunks : chunks + WEIGHT_PARTS]
    outs = rest[-len(pieces) :]
    half = outs[0].shape[1]
    rows = jnp.concatenate([ref[...] for ref in hidden], axis=1)
    for (bits, side), out_ref in zip(pieces, outs):
        column = pl.multiple_of(((place_ref[2] ^ bits) * 2 + side) * half, HEAD_DIM)
        out_ref[...] = times_weight(rows, weights, column, half).astype(out_ref.dtype)


def decode_project_kernel(place_ref, rows_ref, *rest):
    weights, outs = rest[:WEIGHT_PARTS], rest[-4:]
    width = outs[0].shape[1]
    rows = rows_ref[...]
    for bits, out_ref in enumerate(outs):
        column = pl.multiple_of((place_ref[2] ^ bits) * width, HEAD_DIM)
        out_ref[...] = times_weight(rows, weights, column, width).astype(out_ref.dtype)


def relay_kernel(own_ref, got_ref, *rest):
    out_ref = rest[-1]
    out_ref[...] = (own_ref[...] + got_ref[...].astype(F32)).astype(BF16)


def finish_kernel(own_a, own_b, ax, ay, bx, by, d_own, d_x, d_y, d_far, *rest):
    prefill_hbm, decode_ref, out_ref, sems = rest
    width = own_a.shape[1]
    count = sems.shape[0]
    size = out_ref.shape[0] // count
    copies = []
    for c in range(count):
        at = slice(c * size, (c + 1) * size)
        for at_cols, own, x_ref, y_ref in ((0, own_a, ax, ay), (width, own_b, bx, by)):
            total = own[at] + x_ref[at].astype(F32) + y_ref[at].astype(F32)
            out_ref[at, at_cols : at_cols + width] = total.astype(BF16)
        copy = pltpu.make_async_copy(
            out_ref.at[pl.ds(c * size, size)], prefill_hbm.at[0, pl.ds(c * size, size)], sems.at[c]
        )
        copy.start()
        copies.append(copy)
    rows, steps = decode_ref.shape[0], decode_ref.shape[1]
    total = d_own[...] + d_x[...].astype(F32) + d_y[...].astype(F32) + d_far[...].astype(F32)
    for r in range(rows):
        decode_ref[r] = total[r * steps : (r + 1) * steps].astype(BF16)
    for copy in copies:
        copy.wait()


def swap(array, axis, size, bit):
    return lax.ppermute(array, axis, [(i, i ^ bit) for i in range(size)])


def body(
    prefill_query,
    prefill_key,
    prefill_value,
    prefill_rate,
    out_weight,
    decode_query,
    decode_key,
    decode_value,
    decode_rate,
    prompt_of_row,
    *,
    groups,
    reps,
    parts,
):
    length = prefill_query.shape[1]
    features = prefill_query.shape[2]
    heads = prefill_rate.shape[1]
    rows_here, steps = decode_query.shape[0], decode_query.shape[1]
    d_rows = rows_here * steps
    d_pad = -(-d_rows // 16) * 16
    place = jnp.stack([lax.axis_index("ctx"), lax.axis_index("rep"), lax.axis_index("head")])
    place = place.astype(jnp.int32)
    count = min(CHUNKS, heads)
    edges = [heads * c // count for c in range(count + 1)]
    chunks = [(a, b - a) for a, b in zip(edges[:-1], edges[1:])]
    phases = groups - 1
    state_elements = heads * HEAD_DIM * HEAD_DIM

    def in_hbm(array):
        return pltpu.with_memory_space_constraint(array, pltpu.HBM)

    def in_vmem(array):
        return pltpu.with_memory_space_constraint(array, pltpu.VMEM)

    def message_shape(size):
        return sds((size * HEAD_DIM + LOG_ROWS, HEAD_DIM), BF16)

    decode_shape = (rows_here, steps, features)
    made = call(
        first_state_kernel,
        "own_state",
        [SMEM] + [HBM] * 3,
        [
            pltpu.VMEM((chunks[0][1], HEAD_DIM, HEAD_DIM), F32),
            pltpu.VMEM((1, HEAD_DIM), F32),
            pltpu.VMEM((length, heads), F32),
            pltpu.VMEM((1, heads, length), F32),
            pltpu.VMEM((length, features), BF16),
            pltpu.VMEM((length, features), BF16),
            message_shape(chunks[0][1]),
        ],
        [pltpu.SemaphoreType.DMA((3,))],
        cost(4 * length * features * HEAD_DIM, 16 * length * features),
    )(place, in_hbm(prefill_key), in_hbm(prefill_value), in_hbm(prefill_rate))
    own, log_row, columns, rate, keys, values = map(in_vmem, made[:6])
    owns, values_out = [own], [made[6]]
    weight_hbm = in_hbm(out_weight)
    weight_part = pltpu.VMEM((features // WEIGHT_PARTS, out_weight.shape[1]), BF16)
    token = sds((8, HEAD_DIM), F32)
    arrays = (prefill_query, decode_query, decode_key, decode_value)
    queries, d_query, d_key, d_value, local, local_token, *weights = call(
        functools.partial(local_kernel, len(arrays)),
        "local_attention",
        [VMEM] * 4 + [HBM] * (1 + len(arrays)),
        [pltpu.VMEM(array.shape, BF16) for array in arrays]
        + [pltpu.VMEM((length, features), F32), token]
        + [weight_part] * EARLY_PARTS,
        [pltpu.SemaphoreType.DMA((EARLY_PARTS,)), pltpu.SemaphoreType.DMA((len(arrays),))],
        cost(4 * length * length * features, 12 * length * features, heads * length * length),
    )(keys, values, columns, rate, weight_hbm, *map(in_hbm, arrays))
    queries, d_query, d_key, d_value, local = map(
        in_vmem, (queries, d_query, d_key, d_value, local)
    )
    for first, size in chunks[1:]:
        made = call(
            functools.partial(more_state_kernel, first),
            "more_state",
            [VMEM] * 4 + [ANY],
            [pltpu.VMEM((size, HEAD_DIM, HEAD_DIM), F32), message_shape(size)],
            (),
            cost(4 * length * size * HEAD_DIM * HEAD_DIM, 8 * length * features),
        )(keys, values, columns, log_row, local_token)
        owns.append(in_vmem(made[0]))
        values_out.append(made[1])

    def load_weight(*after):
        if len(weights) == WEIGHT_PARTS:
            return []
        part, done = call(
            functools.partial(load_kernel, len(weights)),
            "load_weight",
            [HBM] + [ANY] * len(after),
            [weight_part, token],
            [pltpu.SemaphoreType.DMA((1,))],
            cost(1, features // WEIGHT_PARTS * out_weight.shape[1] * 2),
        )(weight_hbm, *after)
        weights.append(part)
        return [done]

    received = []
    after = values_out[-1:]
    for phase in range(phases):
        pairs = []
        for g in range(groups):
            for r in range(reps):
                if g in (phase, groups - 2 - phase):
                    other = (g + 1, r)
                elif g in (phase + 1, groups - 1 - phase):
                    other = (g - 1, r)
                else:
                    other = (g, r ^ 1)
                pairs.append((g * reps + r, other[0] * reps + other[1]))
        if phase > 0:
            values_out = []
            for c, (first, size) in enumerate(chunks):
                value = call(
                    functools.partial(chain_kernel, phase, first),
                    "chain",
                    [SMEM, VMEM, VMEM, VMEM] + [ANY] * len(after),
                    message_shape(size),
                    (),
                    cost(2 * size * HEAD_DIM * HEAD_DIM, 24 * size * HEAD_DIM * HEAD_DIM),
                )(place, owns[c], log_row, received[-1][c], *after)
                values_out.append(value)
                after = []
        received.append([lax.ppermute(value, ("ctx", "rep"), pairs) for value in values_out])
    loaded = []
    while len(weights) < WEIGHT_PARTS:
        loaded = load_weight(values_out[-1], *loaded)
    weights = [in_vmem(part) for part in weights]

    after = loaded
    hidden = [
        call(
            functools.partial(hidden_kernel, phases, first),
            "hidden",
            [SMEM] + [VMEM] * (3 + phases) + [ANY] * len(after),
            sds((length, size * HEAD_DIM), BF16),
            (),
            cost(2 * length * size * HEAD_DIM * HEAD_DIM, 20 * length * size * HEAD_DIM),
        )(place, queries, columns, local, *[received[phase][c] for phase in range(phases)], *after)
        for c, (first, size) in enumerate(chunks)
    ]

    def final_states(*after):
        finals = []
        for c, (first, size) in enumerate(chunks):
            gate = after if c == count - 1 else ()
            finals.append(
                call(
                    functools.partial(final_kernel, first, phases),
                    "final_state",
                    [SMEM, VMEM, VMEM] + [VMEM] * phases + [ANY] * len(gate),
                    sds((size, HEAD_DIM, HEAD_DIM), F32),
                    (),
                    cost(4 * state_elements // count, state_elements * 4),
                )(place, owns[c], log_row, *[got[c] for got in received], *gate)
            )
        return finals, [swap(final, "rep", reps, 1) for final in finals]

    def decode_rows(finals, others, *after):
        flat = pltpu.VMEM((d_rows, features), F32)
        return call(
            functools.partial(decode_kernel, count),
            "decode_rows",
            [SMEM, SMEM] + [VMEM] * (4 + 2 * count) + [ANY] * len(after),
            sds((d_pad, features), BF16),
            [flat, flat, flat, pltpu.VMEM((d_rows, heads), F32)],
            cost(16 * d_rows * features * HEAD_DIM, state_elements),
        )(
            place,
            prompt_of_row,
            d_query,
            d_key,
            d_value,
            jnp.transpose(decode_rate, (0, 2, 1)),
            *finals,
            *others,
            *after,
        )

    out_columns = out_weight.shape[1]
    if parts != 4 or (out_columns // parts) % 256 != 0 or length % 64 != 0:
        rows_all = jnp.concatenate([jnp.concatenate(hidden, axis=1), decode_rows(*final_states())], axis=0)
        terms = jnp.dot(rows_all, out_weight, preferred_element_type=F32)
        summed = lax.psum_scatter(terms, "head", scatter_dimension=1, tiled=True)
        prefill_out = summed[:length].astype(BF16)[None]
        decode_out = summed[length : length + d_rows].astype(BF16)
        return prefill_out, decode_out.reshape(rows_here, steps, -1)

    width = out_columns // parts
    half = width // 2

    def project(pieces, dtype, *after):
        return call(
            functools.partial(project_kernel, pieces, count),
            "project",
            [SMEM] + [VMEM] * (count + WEIGHT_PARTS) + [ANY] * len(after),
            [sds((length, half), dtype) for _ in pieces],
            (),
            cost(2 * length * features * half * len(pieces), features * half * 2 * len(pieces)),
        )(place, *hidden, *weights, *after)

    def relay(own_term, got, *after):
        return call(
            relay_kernel,
            "relay",
            [VMEM, VMEM] + [ANY] * len(after),
            sds((length, half), BF16),
            (),
            cost(length * half, length * half * 8),
        )(own_term, got, *after)

    to_x, to_y = project([(3, 0), (3, 1)], BF16)
    far_a = swap(to_x, "head", parts, 1)
    far_b = swap(to_y, "head", parts, 2)
    x_a = swap(project([(1, 0)], BF16)[0], "head", parts, 1)
    y_b = swap(project([(2, 1)], BF16)[0], "head", parts, 2)
    pass_a, pass_b = project([(2, 0), (1, 1)], F32)
    own_a, own_b = project([(0, 0), (0, 1)], F32)
    sent_a, sent_b = relay(pass_a, far_a), relay(pass_b, far_b)
    y_a = swap(sent_a, "head", parts, 2)
    x_b = swap(sent_b, "head", parts, 1)

    d_hidden = decode_rows(*final_states(to_y), sent_a, sent_b)
    d_own, d_x, d_y, d_far = call(
        decode_project_kernel,
        "decode_project",
        [SMEM] + [VMEM] * (1 + WEIGHT_PARTS),
        [sds((d_pad, width), F32)] + [sds((d_pad, width), BF16)] * 3,
        (),
        cost(2 * d_pad * features * out_columns, features * out_columns // 8),
    )(place, d_hidden, *weights)
    prefill_out, decode_out = call(
        finish_kernel,
        "finish",
        [VMEM] * 10,
        [sds((1, length, width), BF16), sds((rows_here, steps, width), BF16)],
        [pltpu.VMEM((length, width), BF16), pltpu.SemaphoreType.DMA((4,))],
        cost(6 * length * half, 20 * length * half),
        out_specs=[HBM, VMEM],
    )(
        own_a,
        own_b,
        x_a,
        y_a,
        x_b,
        y_b,
        d_own,
        swap(d_x, "head", parts, 1),
        swap(d_y, "head", parts, 2),
        swap(d_far, "head", parts, 3),
    )
    return prefill_out, decode_out


def solution(mesh):
    return jax.shard_map(
        functools.partial(
            body, groups=mesh.shape["ctx"], reps=mesh.shape["rep"], parts=mesh.shape["head"]
        ),
        mesh=mesh,
        in_specs=(
            P("rep", "ctx", "head"),
            P("rep", "ctx", "head"),
            P("rep", "ctx", "head"),
            P("rep", "head", "ctx"),
            P("head", None),
            P(("ctx", "rep"), None, "head"),
            P(("ctx", "rep"), None, "head"),
            P(("ctx", "rep"), None, "head"),
            P(("ctx", "rep"), "head", None),
            P(("ctx", "rep")),
        ),
        out_specs=(P("rep", "ctx", "head"), P(("ctx", "rep"), None, "head")),
        check_vma=False,
    )
```

```python
import functools

import jax
import jax.numpy as jnp
from jax import lax
from jax.experimental import pallas as pl
from jax.experimental.pallas import tpu as pltpu
from jax.sharding import PartitionSpec as P

HEAD_DIM = 128
EPSILON = 1e-06
NEGATIVE = -1e30
HIGH = lax.Precision.HIGHEST
CHUNKS = 2
WEIGHT_PARTS = 4
EARLY_PARTS = 2
VMEM_BYTES = 8 * 2**20
F32 = jnp.float32
BF16 = jnp.bfloat16
NT = (((1,), (1,)), ((), ()))
TN = (((0,), (0,)), ((), ()))


def params():
    return pltpu.CompilerParams(vmem_limit_bytes=VMEM_BYTES)


def cost(flops, moved, exps=0):
    return pl.CostEstimate(flops=int(flops), bytes_accessed=int(moved), transcendentals=int(exps))


def normalize(array):
    return array * lax.rsqrt(jnp.mean(array * array, axis=-1, keepdims=True) + EPSILON)


def lower_ones(length):
    rows = lax.broadcasted_iota(jnp.int32, (length, length), 0)
    cols = lax.broadcasted_iota(jnp.int32, (length, length), 1)
    return rows >= cols


def decay_columns(rate, lower):
    return -lax.dot_general(lower.astype(F32), rate, NT, precision=HIGH, preferred_element_type=F32)


def decay_rows(rate, lower):
    return -lax.dot_general(rate, lower.astype(F32), NT, precision=HIGH, preferred_element_type=F32)


def identity(size):
    rows = lax.broadcasted_iota(jnp.int32, (size, size), 0)
    cols = lax.broadcasted_iota(jnp.int32, (size, size), 1)
    return rows, cols


def head_slice(index):
    return slice(index * HEAD_DIM, (index + 1) * HEAD_DIM)


def halves(array):
    top = array.astype(BF16)
    return top, (array - top.astype(F32)).astype(BF16)

VMEM = pl.BlockSpec(memory_space=pltpu.VMEM)
SMEM = pl.BlockSpec(memory_space=pltpu.SMEM)
ANY = pl.BlockSpec(memory_space=pl.ANY)
HBM = pl.BlockSpec(memory_space=pltpu.HBM)


def call(kernel, name, in_specs, out_shape, scratch=(), estimate=None, out_specs=None):
    if out_specs is None:
        out_specs = jax.tree.map(lambda _: VMEM, out_shape)
    return pl.pallas_call(
        kernel,
        in_specs=in_specs,
        out_specs=out_specs,
        out_shape=out_shape,
        scratch_shapes=list(scratch),
        compiler_params=params(),
        cost_estimate=estimate,
        name=name,
    )


def sds(shape, dtype):
    return jax.ShapeDtypeStruct(shape, dtype)


LOG_ROWS = 16


def log_rows(log):
    top = log.astype(BF16).astype(F32)
    mid = (log - top).astype(BF16).astype(F32)
    row = lax.broadcasted_iota(jnp.int32, (LOG_ROWS, HEAD_DIM), 0)
    rest = jnp.where(row == 2, log - top - mid, 0.0)
    return jnp.where(row == 0, top, jnp.where(row == 1, mid, rest)).astype(BF16)


def read_log(message_ref):
    rows = message_ref.shape[0]
    facts = message_ref[rows - LOG_ROWS :, :].astype(F32)
    return facts[0:1] + facts[1:2] + facts[2:3]


def state_rows(message_ref, index):
    return message_ref[index * HEAD_DIM : (index + 1) * HEAD_DIM, :]


def own_states(first, k_ref, v_ref, columns, own_ref, message_ref):
    length = columns.shape[0]
    factor = jnp.exp(columns[length - 1 :, :] - columns)
    for i in range(own_ref.shape[0]):
        h = first + i
        at = head_slice(h)
        weighted = k_ref[:, at].astype(F32) * factor[:, h : h + 1]
        top, rest = halves(weighted)
        both = lax.dot_general(
            jnp.concatenate([top, rest], axis=1), v_ref[:, at], TN, preferred_element_type=F32
        )
        state = both[:HEAD_DIM] + both[HEAD_DIM:]
        own_ref[i] = state
        message_ref[i * HEAD_DIM : (i + 1) * HEAD_DIM, :] = state.astype(BF16)


def started(pairs, sems):
    copies = [
        pltpu.make_async_copy(source, target, sems.at[i]) for i, (source, target) in enumerate(pairs)
    ]
    for copy in copies:
        copy.start()
    return copies


def first_state_kernel(place_ref, k_hbm, v_hbm, rate_hbm, *refs):
    own_ref, log_ref, col_ref, rate_ref, k_ref, v_ref, message_ref, sems = refs
    copies = started(((rate_hbm, rate_ref), (k_hbm.at[0], k_ref), (v_hbm.at[0], v_ref)), sems)
    length = k_ref.shape[0]
    copies[0].wait()
    rate = rate_ref[0]
    columns = decay_columns(rate, lower_ones(length))
    col_ref[...] = columns
    log_ref[...] = jnp.zeros_like(log_ref)
    log_ref[:, : rate.shape[0]] = columns[length - 1 :, :]
    message_ref[message_ref.shape[0] - LOG_ROWS :, :] = log_rows(log_ref[...])
    copies[1].wait()
    copies[2].wait()
    own_states(0, k_ref, v_ref, columns, own_ref, message_ref)


def more_state_kernel(first, k_ref, v_ref, col_ref, log_ref, *rest):
    own_ref, message_ref = rest[-2:]
    message_ref[message_ref.shape[0] - LOG_ROWS :, :] = log_rows(log_ref[...])
    own_states(first, k_ref, v_ref, col_ref[...], own_ref, message_ref)


def chain_kernel(phase, first, place_ref, own_ref, log_ref, got_ref, *rest):
    out_ref = rest[-1]
    size = (out_ref.shape[0] - LOG_ROWS) // HEAD_DIM
    right = place_ref[0] == phase
    log = log_ref[...]
    later = read_log(got_ref)
    own_factor = jnp.where(right, 1.0, jnp.exp(later))
    got_factor = jnp.where(right, jnp.exp(log), 1.0)
    for i in range(size):
        h = first + i
        value = (
            own_factor[:, h : h + 1] * own_ref[i]
            + got_factor[:, h : h + 1] * state_rows(got_ref, i).astype(F32)
        )
        out_ref[i * HEAD_DIM : (i + 1) * HEAD_DIM, :] = value.astype(BF16)
    out_ref[size * HEAD_DIM :, :] = log_rows(log + later)


def entering_state(group, got, index):
    state = state_rows(got[0], index)
    for phase in range(1, len(got)):
        state = jnp.where(group == phase + 1, state_rows(got[phase], index), state)
    return jnp.where(group == 0, jnp.zeros_like(state), state)


def weight_copies(places, weight_hbm, weights, sems):
    copies = []
    for i, (index, ref) in enumerate(zip(places, weights)):
        depth = ref.shape[0]
        copies.append(
            pltpu.make_async_copy(weight_hbm.at[pl.ds(index * depth, depth)], ref, sems.at[i])
        )
    for copy in copies:
        copy.start()
    return copies


def load_kernel(index, weight_hbm, *rest):
    weight_ref, token_ref, sems = rest[-3:]
    copies = weight_copies([index], weight_hbm, [weight_ref], sems)
    token_ref[...] = jnp.zeros_like(token_ref)
    for copy in copies:
        copy.wait()


def local_kernel(copied, k_ref, v_ref, col_ref, rate_ref, weight_hbm, *rest):
    sources, rest = rest[:copied], rest[copied:]
    targets, rest = rest[:copied], rest[copied:]
    local_ref, token_ref = rest[:2]
    weights, sems, more = rest[2:-2], rest[-2], rest[-1]
    loads = started(tuple(zip(sources, targets)), more)
    copies = weight_copies(range(len(weights)), weight_hbm, weights, sems)
    token_ref[...] = jnp.zeros_like(token_ref)
    q_ref = targets[0]
    lower = lower_ones(k_ref.shape[0])
    rows = decay_rows(rate_ref[0], lower)
    loads[0].wait()
    for h in range(local_ref.shape[1] // HEAD_DIM):
        at = head_slice(h)
        scores = lax.dot_general(q_ref[0, :, at], k_ref[:, at], NT, preferred_element_type=F32)
        decay = jnp.exp(jnp.where(lower, col_ref[:, h : h + 1] - rows[h : h + 1, :], NEGATIVE))
        narrow = (scores * decay).astype(BF16)
        local_ref[:, at] = jnp.dot(narrow, v_ref[:, at], preferred_element_type=F32)
    for copy in loads[1:] + copies:
        copy.wait()


def hidden_kernel(phases, first, place_ref, q_ref, col_ref, local_ref, *rest):
    got, hidden_ref = rest[:phases], rest[-1]
    for i in range(hidden_ref.shape[1] // HEAD_DIM):
        h = first + i
        whole = head_slice(h)
        state = entering_state(place_ref[0], got, i)
        inter = jnp.dot(q_ref[0, :, whole], state, preferred_element_type=F32)
        attended = local_ref[:, whole] + inter * jnp.exp(col_ref[:, h : h + 1])
        hidden_ref[:, head_slice(i)] = normalize(attended).astype(BF16)


def final_kernel(first, phases, place_ref, own_ref, log_ref, *rest):
    got, out_ref = rest[:phases], rest[-1]
    group = place_ref[0]
    keep = jnp.exp(log_ref[...])
    later = jnp.zeros((1, HEAD_DIM), F32)
    for phase in range(phases):
        later = jnp.where(group == phases - 1 - phase, read_log(got[phase]), later)
    later = jnp.exp(later)
    for i in range(out_ref.shape[0]):
        h = first + i
        suffix = jnp.zeros((HEAD_DIM, HEAD_DIM), F32)
        for phase in range(phases):
            there = state_rows(got[phase], i).astype(F32)
            suffix = jnp.where(group == phases - 1 - phase, there, suffix)
        prefix = entering_state(group, got, i).astype(F32)
        here = own_ref[i] + keep[:, h : h + 1] * prefix
        out_ref[i] = suffix + later[:, h : h + 1] * here


def flat_rows(ref, rows_ref):
    rows, steps = ref.shape[0], ref.shape[1]
    for r in range(rows):
        rows_ref[r * steps : (r + 1) * steps, :] = ref[r].astype(F32)


def decode_kernel(count, place_ref, prompt_ref, q_ref, k_ref, v_ref, rate_ref, *rest):
    near, far = rest[:count], rest[count : 2 * count]
    finals = [(c, i) for c, ref in enumerate(near) for i in range(ref.shape[0])]
    out_ref, q_rows, k_rows, v_rows, rate_rows = rest[-5:]
    rows_here, steps = q_ref.shape[0], q_ref.shape[1]
    d_rows = q_rows.shape[0]
    flat_rows(q_ref, q_rows)
    flat_rows(k_ref, k_rows)
    flat_rows(v_ref, v_rows)
    flat_rows(rate_ref, rate_rows)
    rows, cols = identity(d_rows)
    seen = (rows // steps == cols // steps) & (rows >= cols)
    ones = seen.astype(F32)
    rates = rate_rows[...]
    down = -jnp.dot(ones, rates, precision=HIGH, preferred_element_type=F32)
    across = -lax.dot_general(
        rates, ones, (((0,), (1,)), ((), ())), precision=HIGH, preferred_element_type=F32
    )
    grow = jnp.exp(down)
    row_of = lax.broadcasted_iota(jnp.int32, (d_rows, HEAD_DIM), 0) // steps
    prompt = jnp.zeros((d_rows, HEAD_DIM), jnp.int32)
    for r in range(rows_here):
        prompt = jnp.where(row_of == r, prompt_ref[r], prompt)
    mine = prompt == place_ref[1]
    for i in range(rates.shape[1]):
        at = head_slice(i)
        query = q_rows[:, at]
        narrow = query.astype(BF16)
        terms = []
        c, slot = finals[i]
        for ref in (near[c], far[c]):
            top, low = halves(ref[slot])
            both = jnp.dot(
                narrow, jnp.concatenate([top, low], axis=1), preferred_element_type=F32
            )
            terms.append(both[:, :HEAD_DIM] + both[:, HEAD_DIM:])
        base = jnp.where(mine, terms[0], terms[1])
        scores = lax.dot_general(
            query, k_rows[:, at], NT, precision=HIGH, preferred_element_type=F32
        )
        decay = jnp.exp(jnp.where(seen, down[:, i : i + 1] - across[i : i + 1, :], NEGATIVE))
        intra = jnp.dot(scores * decay, v_rows[:, at], precision=HIGH, preferred_element_type=F32)
        q_rows[:, at] = normalize(base * grow[:, i : i + 1] + intra)
    pad = out_ref.shape[0] - d_rows
    value = q_rows[...]
    if pad:
        value = jnp.concatenate([value, jnp.zeros((pad, value.shape[1]), F32)], axis=0)
    out_ref[...] = value.astype(BF16)


def times_weight(rows, weights, column, width):
    total = None
    for i, ref in enumerate(weights):
        depth = ref.shape[0]
        term = jnp.dot(
            rows[:, i * depth : (i + 1) * depth],
            ref[:, pl.ds(column, width)],
            preferred_element_type=F32,
        )
        total = term if total is None else total + term
    return total


def project_kernel(pieces, width, chunks, added, place_ref, *rest):
    hidden, rest = rest[:chunks], rest[chunks:]
    addends, weights = rest[:added], rest[added : -len(pieces)]
    outs = rest[-len(pieces) :]
    rows = jnp.concatenate([ref[...] for ref in hidden], axis=1)
    for n, ((bits, first, columns), out_ref) in enumerate(zip(pieces, outs)):
        column = pl.multiple_of((place_ref[2] ^ bits) * width + first, HEAD_DIM)
        total = times_weight(rows, weights, column, columns)
        if added:
            total = total + addends[n][...]
        out_ref[...] = total.astype(out_ref.dtype)


def decode_project_kernel(place_ref, rows_ref, *rest):
    weights, outs = rest[:WEIGHT_PARTS], rest[-4:]
    width = outs[0].shape[1]
    rows = rows_ref[...]
    for bits, out_ref in enumerate(outs):
        column = pl.multiple_of((place_ref[2] ^ bits) * width, HEAD_DIM)
        terms = times_weight(rows, weights, column, width)
        out_ref[...] = terms[: out_ref.shape[0]].astype(out_ref.dtype)


def relay_kernel(own_ref, got_ref, *rest):
    out_ref = rest[-1]
    out_ref[...] = (own_ref[...] + got_ref[...].astype(F32)).astype(BF16)


def finish_kernel(own_a, own_b, ax, ay, bx, by, d_own, d_x, d_y, d_far, *rest):
    prefill_hbm, decode_ref, out_ref, sems = rest
    split = own_a.shape[1]
    count = sems.shape[0]
    size = out_ref.shape[0] // count
    copies = []
    for c in range(count):
        at = slice(c * size, (c + 1) * size)
        for first, own, x_ref, y_ref in ((0, own_a, ax, ay), (split, own_b, bx, by)):
            total = own[at] + x_ref[at].astype(F32) + y_ref[at].astype(F32)
            out_ref[at, first : first + own.shape[1]] = total.astype(BF16)
        copy = pltpu.make_async_copy(
            out_ref.at[pl.ds(c * size, size)], prefill_hbm.at[0, pl.ds(c * size, size)], sems.at[c]
        )
        copy.start()
        copies.append(copy)
    rows, steps = decode_ref.shape[0], decode_ref.shape[1]
    total = d_own[...] + d_x[...].astype(F32) + d_y[...].astype(F32) + d_far[...].astype(F32)
    for r in range(rows):
        decode_ref[r] = total[r * steps : (r + 1) * steps].astype(BF16)
    for copy in copies:
        copy.wait()


def swap(array, axis, size, bit):
    return lax.ppermute(array, axis, [(i, i ^ bit) for i in range(size)])


def body(
    prefill_query,
    prefill_key,
    prefill_value,
    prefill_rate,
    out_weight,
    decode_query,
    decode_key,
    decode_value,
    decode_rate,
    prompt_of_row,
    *,
    groups,
    reps,
    parts,
):
    length = prefill_query.shape[1]
    features = prefill_query.shape[2]
    heads = prefill_rate.shape[1]
    rows_here, steps = decode_query.shape[0], decode_query.shape[1]
    d_rows = rows_here * steps
    d_pad = -(-d_rows // 16) * 16
    place = jnp.stack([lax.axis_index("ctx"), lax.axis_index("rep"), lax.axis_index("head")])
    place = place.astype(jnp.int32)
    count = min(CHUNKS, heads)
    edges = [heads * c // count for c in range(count + 1)]
    chunks = [(a, b - a) for a, b in zip(edges[:-1], edges[1:])]
    phases = groups - 1
    state_elements = heads * HEAD_DIM * HEAD_DIM

    def in_hbm(array):
        return pltpu.with_memory_space_constraint(array, pltpu.HBM)

    def in_vmem(array):
        return pltpu.with_memory_space_constraint(array, pltpu.VMEM)

    def message_shape(size):
        return sds((size * HEAD_DIM + LOG_ROWS, HEAD_DIM), BF16)

    decode_shape = (rows_here, steps, features)
    made = call(
        first_state_kernel,
        "own_state",
        [SMEM] + [HBM] * 3,
        [
            pltpu.VMEM((chunks[0][1], HEAD_DIM, HEAD_DIM), F32),
            pltpu.VMEM((1, HEAD_DIM), F32),
            pltpu.VMEM((length, heads), F32),
            pltpu.VMEM((1, heads, length), F32),
            pltpu.VMEM((length, features), BF16),
            pltpu.VMEM((length, features), BF16),
            message_shape(chunks[0][1]),
        ],
        [pltpu.SemaphoreType.DMA((3,))],
        cost(4 * length * features * HEAD_DIM, 16 * length * features),
    )(place, in_hbm(prefill_key), in_hbm(prefill_value), in_hbm(prefill_rate))
    own, log_row, columns, rate, keys, values = map(in_vmem, made[:6])
    owns, values_out = [own], [made[6]]
    weight_hbm = in_hbm(out_weight)
    weight_part = pltpu.VMEM((features // WEIGHT_PARTS, out_weight.shape[1]), BF16)
    token = sds((8, HEAD_DIM), F32)
    arrays = (prefill_query, decode_query, decode_key, decode_value)
    queries, d_query, d_key, d_value, local, local_token, *weights = call(
        functools.partial(local_kernel, len(arrays)),
        "local_attention",
        [VMEM] * 4 + [HBM] * (1 + len(arrays)),
        [pltpu.VMEM(array.shape, BF16) for array in arrays]
        + [pltpu.VMEM((length, features), F32), token]
        + [weight_part] * EARLY_PARTS,
        [pltpu.SemaphoreType.DMA((EARLY_PARTS,)), pltpu.SemaphoreType.DMA((len(arrays),))],
        cost(4 * length * length * features, 12 * length * features, heads * length * length),
    )(keys, values, columns, rate, weight_hbm, *map(in_hbm, arrays))
    queries, d_query, d_key, d_value, local = map(
        in_vmem, (queries, d_query, d_key, d_value, local)
    )
    for first, size in chunks[1:]:
        made = call(
            functools.partial(more_state_kernel, first),
            "more_state",
            [VMEM] * 4 + [ANY],
            [pltpu.VMEM((size, HEAD_DIM, HEAD_DIM), F32), message_shape(size)],
            (),
            cost(4 * length * size * HEAD_DIM * HEAD_DIM, 8 * length * features),
        )(keys, values, columns, log_row, local_token)
        owns.append(in_vmem(made[0]))
        values_out.append(made[1])

    def load_weight(*after):
        if len(weights) == WEIGHT_PARTS:
            return []
        part, done = call(
            functools.partial(load_kernel, len(weights)),
            "load_weight",
            [HBM] + [ANY] * len(after),
            [weight_part, token],
            [pltpu.SemaphoreType.DMA((1,))],
            cost(1, 1),
        )(weight_hbm, *after)
        weights.append(part)
        return [done]

    received = []
    after = values_out[-1:]
    for phase in range(phases):
        pairs = []
        for g in range(groups):
            for r in range(reps):
                if g in (phase, groups - 2 - phase):
                    other = (g + 1, r)
                elif g in (phase + 1, groups - 1 - phase):
                    other = (g - 1, r)
                else:
                    other = (g, r ^ 1)
                pairs.append((g * reps + r, other[0] * reps + other[1]))
        if phase > 0:
            values_out = []
            for c, (first, size) in enumerate(chunks):
                value = call(
                    functools.partial(chain_kernel, phase, first),
                    "chain",
                    [SMEM, VMEM, VMEM, VMEM] + [ANY] * len(after),
                    message_shape(size),
                    (),
                    cost(2 * size * HEAD_DIM * HEAD_DIM, 24 * size * HEAD_DIM * HEAD_DIM),
                )(place, owns[c], log_row, received[-1][c], *after)
                values_out.append(value)
                after = load_weight(value) if c == 0 else []
        received.append([lax.ppermute(value, ("ctx", "rep"), pairs) for value in values_out])
    loaded = []
    while len(weights) < WEIGHT_PARTS:
        loaded = load_weight(values_out[-1], *loaded)
    weights = [in_vmem(part) for part in weights]

    after = loaded
    hidden = [
        call(
            functools.partial(hidden_kernel, phases, first),
            "hidden",
            [SMEM] + [VMEM] * (3 + phases) + [ANY] * len(after),
            sds((length, size * HEAD_DIM), BF16),
            (),
            cost(2 * length * size * HEAD_DIM * HEAD_DIM, 20 * length * size * HEAD_DIM),
        )(place, queries, columns, local, *[received[phase][c] for phase in range(phases)], *after)
        for c, (first, size) in enumerate(chunks)
    ]

    def final_states(*after):
        finals = []
        for c, (first, size) in enumerate(chunks):
            gate = after if c == count - 1 else ()
            finals.append(
                call(
                    functools.partial(final_kernel, first, phases),
                    "final_state",
                    [SMEM, VMEM, VMEM] + [VMEM] * phases + [ANY] * len(gate),
                    sds((size, HEAD_DIM, HEAD_DIM), F32),
                    (),
                    cost(4 * state_elements // count, state_elements * 4),
                )(place, owns[c], log_row, *[got[c] for got in received], *gate)
            )
        return finals, [swap(final, "rep", reps, 1) for final in finals]

    def decode_rows(finals, others, *after):
        flat = pltpu.VMEM((d_rows, features), F32)
        return call(
            functools.partial(decode_kernel, count),
            "decode_rows",
            [SMEM, SMEM] + [VMEM] * (4 + 2 * count) + [ANY] * len(after),
            sds((d_pad, features), BF16),
            [flat, flat, flat, pltpu.VMEM((d_rows, heads), F32)],
            cost(16 * d_rows * features * HEAD_DIM, state_elements),
        )(
            place,
            prompt_of_row,
            d_query,
            d_key,
            d_value,
            jnp.transpose(decode_rate, (0, 2, 1)),
            *finals,
            *others,
            *after,
        )

    out_columns = out_weight.shape[1]
    if parts != 4 or (out_columns // parts) % 256 != 0 or length % 64 != 0:
        rows_all = jnp.concatenate([jnp.concatenate(hidden, axis=1), decode_rows(*final_states())], axis=0)
        terms = jnp.dot(rows_all, out_weight, preferred_element_type=F32)
        summed = lax.psum_scatter(terms, "head", scatter_dimension=1, tiled=True)
        prefill_out = summed[:length].astype(BF16)[None]
        decode_out = summed[length : length + d_rows].astype(BF16)
        return prefill_out, decode_out.reshape(rows_here, steps, -1)

    width = out_columns // parts
    split = (width * 5 // 12) // HEAD_DIM * HEAD_DIM
    side_x, side_y = (0, split), (split, width - split)

    def project(pieces, dtype, inputs=None, parts_used=None, addends=()):
        inputs = hidden if inputs is None else inputs
        used = weights if parts_used is None else weights[parts_used]
        moved = sum(columns for _, _, columns in pieces)
        depth = sum(array.shape[1] for array in inputs)
        return call(
            functools.partial(project_kernel, pieces, width, len(inputs), len(addends)),
            "project",
            [SMEM] + [VMEM] * (len(inputs) + len(addends) + len(used)),
            [sds((length, columns), dtype) for _, _, columns in pieces],
            (),
            cost(2 * length * depth * moved, depth * moved * 2),
        )(place, *inputs, *addends, *used)

    def relay(own_term, got):
        return call(
            relay_kernel,
            "relay",
            [VMEM, VMEM],
            sds(own_term.shape, BF16),
            (),
            cost(own_term.size, own_term.size * 8),
        )(own_term, got)

    far = [(3, *side_x), (3, *side_y)]
    if count == 2 and chunks[0][1] * HEAD_DIM * 2 == features and WEIGHT_PARTS % 2 == 0:
        early = slice(0, WEIGHT_PARTS // 2)
        late = slice(WEIGHT_PARTS // 2, WEIGHT_PARTS)
        begun = project(far, F32, hidden[:1], early)
        to_x, to_y = project(far, BF16, hidden[1:], late, begun)
    else:
        to_x, to_y = project(far, BF16)
    far_a = swap(to_x, "head", parts, 1)
    far_b = swap(to_y, "head", parts, 2)
    x_a = swap(project([(1, *side_x)], BF16)[0], "head", parts, 1)
    y_b = swap(project([(2, *side_y)], BF16)[0], "head", parts, 2)
    pass_a, pass_b = project([(2, *side_x), (1, *side_y)], F32)
    own_a, own_b = project([(0, *side_x), (0, *side_y)], F32)
    sent_a, sent_b = relay(pass_a, far_a), relay(pass_b, far_b)
    y_a = swap(sent_a, "head", parts, 2)
    x_b = swap(sent_b, "head", parts, 1)

    d_hidden = decode_rows(*final_states(to_y), sent_a, sent_b)
    d_own, d_x, d_y, d_far = call(
        decode_project_kernel,
        "decode_project",
        [SMEM] + [VMEM] * (1 + WEIGHT_PARTS),
        [sds((d_rows, width), F32)] + [sds((d_rows, width), BF16)] * 3,
        (),
        cost(2 * d_pad * features * out_columns, features * out_columns // 8),
    )(place, d_hidden, *weights)
    prefill_out, decode_out = call(
        finish_kernel,
        "finish",
        [VMEM] * 10,
        [sds((1, length, width), BF16), sds((rows_here, steps, width), BF16)],
        [pltpu.VMEM((length, width), BF16), pltpu.SemaphoreType.DMA((4,))],
        cost(3 * length * width, 10 * length * width),
        out_specs=[HBM, VMEM],
    )(
        own_a,
        own_b,
        x_a,
        y_a,
        x_b,
        y_b,
        d_own,
        swap(d_x, "head", parts, 1),
        swap(d_y, "head", parts, 2),
        swap(d_far, "head", parts, 3),
    )
    return prefill_out, decode_out


def solution(mesh):
    return jax.shard_map(
        functools.partial(
            body, groups=mesh.shape["ctx"], reps=mesh.shape["rep"], parts=mesh.shape["head"]
        ),
        mesh=mesh,
        in_specs=(
            P("rep", "ctx", "head"),
            P("rep", "ctx", "head"),
            P("rep", "ctx", "head"),
            P("rep", "head", "ctx"),
            P("head", None),
            P(("ctx", "rep"), None, "head"),
            P(("ctx", "rep"), None, "head"),
            P(("ctx", "rep"), None, "head"),
            P(("ctx", "rep"), "head", None),
            P(("ctx", "rep")),
        ),
        out_specs=(P("rep", "ctx", "head"), P(("ctx", "rep"), None, "head")),
        check_vma=False,
    )
```

```python
import functools

import jax
import jax.numpy as jnp
from jax import lax
from jax.experimental import pallas as pl
from jax.experimental.pallas import tpu as pltpu
from jax.sharding import PartitionSpec as P

HEAD_DIM = 128
EPSILON = 1e-06
NEGATIVE = -1e30
HIGH = lax.Precision.HIGHEST
CHUNKS = 2
WEIGHT_PARTS = 8
EARLY_PARTS = 3
LATER_PARTS = (2, 2, 1)
VMEM_BYTES = 8 * 2**20
F32 = jnp.float32
BF16 = jnp.bfloat16
NT = (((1,), (1,)), ((), ()))
TN = (((0,), (0,)), ((), ()))


def params():
    return pltpu.CompilerParams(vmem_limit_bytes=VMEM_BYTES)


def cost(flops, moved, exps=0):
    return pl.CostEstimate(flops=int(flops), bytes_accessed=int(moved), transcendentals=int(exps))


def normalize(array):
    return array * lax.rsqrt(jnp.mean(array * array, axis=-1, keepdims=True) + EPSILON)


def lower_ones(length):
    rows = lax.broadcasted_iota(jnp.int32, (length, length), 0)
    cols = lax.broadcasted_iota(jnp.int32, (length, length), 1)
    return rows >= cols


def decay_columns(rate, lower):
    return -lax.dot_general(lower.astype(F32), rate, NT, precision=HIGH, preferred_element_type=F32)


def decay_rows(rate, lower):
    return -lax.dot_general(rate, lower.astype(F32), NT, precision=HIGH, preferred_element_type=F32)


def identity(size):
    rows = lax.broadcasted_iota(jnp.int32, (size, size), 0)
    cols = lax.broadcasted_iota(jnp.int32, (size, size), 1)
    return rows, cols


def head_slice(index):
    return slice(index * HEAD_DIM, (index + 1) * HEAD_DIM)


def halves(array):
    top = array.astype(BF16)
    return top, (array - top.astype(F32)).astype(BF16)

VMEM = pl.BlockSpec(memory_space=pltpu.VMEM)
SMEM = pl.BlockSpec(memory_space=pltpu.SMEM)
ANY = pl.BlockSpec(memory_space=pl.ANY)
HBM = pl.BlockSpec(memory_space=pltpu.HBM)


def call(kernel, name, in_specs, out_shape, scratch=(), estimate=None, out_specs=None):
    if out_specs is None:
        out_specs = jax.tree.map(lambda _: VMEM, out_shape)
    return pl.pallas_call(
        kernel,
        in_specs=in_specs,
        out_specs=out_specs,
        out_shape=out_shape,
        scratch_shapes=list(scratch),
        compiler_params=params(),
        cost_estimate=estimate,
        name=name,
    )


def sds(shape, dtype):
    return jax.ShapeDtypeStruct(shape, dtype)


LOG_ROWS = 16


def log_rows(log):
    top = log.astype(BF16).astype(F32)
    mid = (log - top).astype(BF16).astype(F32)
    row = lax.broadcasted_iota(jnp.int32, (LOG_ROWS, HEAD_DIM), 0)
    rest = jnp.where(row == 2, log - top - mid, 0.0)
    return jnp.where(row == 0, top, jnp.where(row == 1, mid, rest)).astype(BF16)


def read_log(message_ref):
    rows = message_ref.shape[0]
    facts = message_ref[rows - LOG_ROWS :, :].astype(F32)
    return facts[0:1] + facts[1:2] + facts[2:3]


def state_rows(message_ref, index):
    return message_ref[index * HEAD_DIM : (index + 1) * HEAD_DIM, :]


def own_states(first, k_ref, v_ref, columns, own_ref, message_ref):
    length = columns.shape[0]
    factor = jnp.exp(columns[length - 1 :, :] - columns)
    for i in range(own_ref.shape[0]):
        h = first + i
        at = head_slice(h)
        weighted = k_ref[:, at].astype(F32) * factor[:, h : h + 1]
        top, rest = halves(weighted)
        both = lax.dot_general(
            jnp.concatenate([top, rest], axis=1), v_ref[:, at], TN, preferred_element_type=F32
        )
        state = both[:HEAD_DIM] + both[HEAD_DIM:]
        own_ref[i] = state
        message_ref[i * HEAD_DIM : (i + 1) * HEAD_DIM, :] = state.astype(BF16)


def started(pairs, sems):
    copies = [
        pltpu.make_async_copy(source, target, sems.at[i]) for i, (source, target) in enumerate(pairs)
    ]
    for copy in copies:
        copy.start()
    return copies


def first_state_kernel(place_ref, k_hbm, v_hbm, rate_hbm, *refs):
    own_ref, log_ref, col_ref, rate_ref, k_ref, v_ref, message_ref, sems = refs
    copies = started(((rate_hbm, rate_ref), (k_hbm.at[0], k_ref), (v_hbm.at[0], v_ref)), sems)
    length = k_ref.shape[0]
    copies[0].wait()
    rate = rate_ref[0]
    columns = decay_columns(rate, lower_ones(length))
    col_ref[...] = columns
    log_ref[...] = jnp.zeros_like(log_ref)
    log_ref[:, : rate.shape[0]] = columns[length - 1 :, :]
    message_ref[message_ref.shape[0] - LOG_ROWS :, :] = log_rows(log_ref[...])
    copies[1].wait()
    copies[2].wait()
    own_states(0, k_ref, v_ref, columns, own_ref, message_ref)


def more_state_kernel(first, k_ref, v_ref, col_ref, log_ref, *rest):
    own_ref, message_ref = rest[-2:]
    message_ref[message_ref.shape[0] - LOG_ROWS :, :] = log_rows(log_ref[...])
    own_states(first, k_ref, v_ref, col_ref[...], own_ref, message_ref)


def chain_kernel(phase, first, place_ref, own_ref, log_ref, got_ref, *rest):
    out_ref = rest[-1]
    size = (out_ref.shape[0] - LOG_ROWS) // HEAD_DIM
    right = place_ref[0] == phase
    log = log_ref[...]
    later = read_log(got_ref)
    own_factor = jnp.where(right, 1.0, jnp.exp(later))
    got_factor = jnp.where(right, jnp.exp(log), 1.0)
    for i in range(size):
        h = first + i
        value = (
            own_factor[:, h : h + 1] * own_ref[i]
            + got_factor[:, h : h + 1] * state_rows(got_ref, i).astype(F32)
        )
        out_ref[i * HEAD_DIM : (i + 1) * HEAD_DIM, :] = value.astype(BF16)
    out_ref[size * HEAD_DIM :, :] = log_rows(log + later)


def entering_state(group, got, index):
    state = state_rows(got[0], index)
    for phase in range(1, len(got)):
        state = jnp.where(group == phase + 1, state_rows(got[phase], index), state)
    return jnp.where(group == 0, jnp.zeros_like(state), state)


def weight_copies(places, weight_hbm, weights, sems):
    copies = []
    for i, (index, ref) in enumerate(zip(places, weights)):
        depth = ref.shape[0]
        copies.append(
            pltpu.make_async_copy(weight_hbm.at[pl.ds(index * depth, depth)], ref, sems.at[i])
        )
    for copy in copies:
        copy.start()
    return copies


def load_kernel(places, weight_hbm, *rest):
    token_ref, sems = rest[-2:]
    weights = rest[-2 - len(places) : -2]
    copies = weight_copies(places, weight_hbm, weights, sems)
    token_ref[...] = jnp.zeros_like(token_ref)
    for copy in copies:
        copy.wait()


def local_kernel(copied, k_ref, v_ref, col_ref, rate_ref, weight_hbm, *rest):
    sources, rest = rest[:copied], rest[copied:]
    targets, rest = rest[:copied], rest[copied:]
    local_ref, token_ref = rest[:2]
    weights, sems, more = rest[2:-2], rest[-2], rest[-1]
    loads = started(tuple(zip(sources, targets)), more)
    copies = weight_copies(range(len(weights)), weight_hbm, weights, sems)
    token_ref[...] = jnp.zeros_like(token_ref)
    q_ref = targets[0]
    lower = lower_ones(k_ref.shape[0])
    rows = decay_rows(rate_ref[0], lower)
    loads[0].wait()
    for h in range(local_ref.shape[1] // HEAD_DIM):
        at = head_slice(h)
        scores = lax.dot_general(q_ref[0, :, at], k_ref[:, at], NT, preferred_element_type=F32)
        decay = jnp.exp(jnp.where(lower, col_ref[:, h : h + 1] - rows[h : h + 1, :], NEGATIVE))
        narrow = (scores * decay).astype(BF16)
        local_ref[:, at] = jnp.dot(narrow, v_ref[:, at], preferred_element_type=F32)
    for copy in loads[1:] + copies:
        copy.wait()


def hidden_kernel(phases, first, place_ref, q_ref, col_ref, local_ref, *rest):
    got, hidden_ref = rest[:phases], rest[-1]
    for i in range(hidden_ref.shape[1] // HEAD_DIM):
        h = first + i
        whole = head_slice(h)
        state = entering_state(place_ref[0], got, i)
        inter = jnp.dot(q_ref[0, :, whole], state, preferred_element_type=F32)
        attended = local_ref[:, whole] + inter * jnp.exp(col_ref[:, h : h + 1])
        hidden_ref[:, head_slice(i)] = normalize(attended).astype(BF16)


def final_kernel(first, phases, place_ref, own_ref, log_ref, *rest):
    got, out_ref = rest[:phases], rest[-1]
    keep = jnp.exp(log_ref[...])

    def write(group):
        prefix = got[group - 1] if group > 0 else None
        suffix = got[phases - 1 - group] if group < phases else None
        later = None if suffix is None else jnp.exp(read_log(suffix))
        for i in range(out_ref.shape[0]):
            h = first + i
            value = own_ref[i]
            if prefix is not None:
                value = value + keep[:, h : h + 1] * state_rows(prefix, i).astype(F32)
            if suffix is not None:
                value = later[:, h : h + 1] * value + state_rows(suffix, i).astype(F32)
            out_ref[i] = value

    for group in range(phases + 1):
        pl.when(place_ref[0] == group)(functools.partial(write, group))


def flat_rows(ref, rows_ref):
    rows, steps = ref.shape[0], ref.shape[1]
    for r in range(rows):
        rows_ref[r * steps : (r + 1) * steps, :] = ref[r].astype(F32)


def decode_kernel(count, place_ref, prompt_ref, q_ref, k_ref, v_ref, rate_ref, *rest):
    near, far = rest[:count], rest[count : 2 * count]
    finals = [(c, i) for c, ref in enumerate(near) for i in range(ref.shape[0])]
    out_ref, q_rows, k_rows, v_rows, rate_rows = rest[-5:]
    rows_here, steps = q_ref.shape[0], q_ref.shape[1]
    d_rows = q_rows.shape[0]
    flat_rows(q_ref, q_rows)
    flat_rows(k_ref, k_rows)
    flat_rows(v_ref, v_rows)
    flat_rows(rate_ref, rate_rows)
    rows, cols = identity(d_rows)
    seen = (rows // steps == cols // steps) & (rows >= cols)
    ones = seen.astype(F32)
    rates = rate_rows[...]
    down = -jnp.dot(ones, rates, precision=HIGH, preferred_element_type=F32)
    across = -lax.dot_general(
        rates, ones, (((0,), (1,)), ((), ())), precision=HIGH, preferred_element_type=F32
    )
    grow = jnp.exp(down)
    row_of = lax.broadcasted_iota(jnp.int32, (d_rows, HEAD_DIM), 0) // steps
    prompt = jnp.zeros((d_rows, HEAD_DIM), jnp.int32)
    for r in range(rows_here):
        prompt = jnp.where(row_of == r, prompt_ref[r], prompt)
    mine = prompt == place_ref[1]
    for i in range(rates.shape[1]):
        at = head_slice(i)
        query = q_rows[:, at]
        narrow = query.astype(BF16)
        terms = []
        c, slot = finals[i]
        for ref in (near[c], far[c]):
            top, low = halves(ref[slot])
            both = jnp.dot(
                narrow, jnp.concatenate([top, low], axis=1), preferred_element_type=F32
            )
            terms.append(both[:, :HEAD_DIM] + both[:, HEAD_DIM:])
        base = jnp.where(mine, terms[0], terms[1])
        scores = lax.dot_general(
            query, k_rows[:, at], NT, precision=HIGH, preferred_element_type=F32
        )
        decay = jnp.exp(jnp.where(seen, down[:, i : i + 1] - across[i : i + 1, :], NEGATIVE))
        intra = jnp.dot(scores * decay, v_rows[:, at], precision=HIGH, preferred_element_type=F32)
        q_rows[:, at] = normalize(base * grow[:, i : i + 1] + intra)
    pad = out_ref.shape[0] - d_rows
    value = q_rows[...]
    if pad:
        value = jnp.concatenate([value, jnp.zeros((pad, value.shape[1]), F32)], axis=0)
    out_ref[...] = value.astype(BF16)


def times_weight(rows, weights, column, width):
    total = None
    for i, ref in enumerate(weights):
        depth = ref.shape[0]
        term = jnp.dot(
            rows[:, i * depth : (i + 1) * depth],
            ref[:, pl.ds(column, width)],
            preferred_element_type=F32,
        )
        total = term if total is None else total + term
    return total


def project_kernel(pieces, width, chunks, added, used, place_ref, *rest):
    hidden, rest = rest[:chunks], rest[chunks:]
    addends, weights = rest[:added], rest[added : added + used]
    outs = rest[-len(pieces) :]
    rows = jnp.concatenate([ref[...] for ref in hidden], axis=1)
    for n, ((bits, first, columns), out_ref) in enumerate(zip(pieces, outs)):
        column = pl.multiple_of((place_ref[2] ^ bits) * width + first, HEAD_DIM)
        total = times_weight(rows, weights, column, columns)
        if added:
            total = total + addends[n][...]
        out_ref[...] = total.astype(out_ref.dtype)


def decode_project_kernel(place_ref, rows_ref, *rest):
    weights, (keep_ref, send_ref) = rest[:WEIGHT_PARTS], rest[-2:]
    width = keep_ref.shape[1] // 2
    rows = rows_ref[...]
    for out_ref, sides in ((keep_ref, (0, 2)), (send_ref, (1, 3))):
        for n, bits in enumerate(sides):
            column = pl.multiple_of((place_ref[2] ^ bits) * width, HEAD_DIM)
            terms = times_weight(rows, weights, column, width)
            out_ref[:, n * width : (n + 1) * width] = terms[: out_ref.shape[0]].astype(out_ref.dtype)


def decode_relay_kernel(keep_ref, got_ref, own_ref, send_ref):
    width = own_ref.shape[1]
    total = keep_ref[...] + got_ref[...].astype(F32)
    own_ref[...] = total[:, :width]
    send_ref[...] = total[:, width:].astype(BF16)


def relay_kernel(own_ref, got_ref, *rest):
    out_ref = rest[-1]
    out_ref[...] = (own_ref[...] + got_ref[...].astype(F32)).astype(BF16)


def finish_kernel(own_a, own_b, ax, ay, bx, by, d_own, d_got, *rest):
    prefill_hbm, decode_ref, out_ref, sems = rest
    split = own_a.shape[1]
    count = sems.shape[0]
    size = out_ref.shape[0] // count
    copies = []
    for c in range(count):
        at = slice(c * size, (c + 1) * size)
        for first, own, x_ref, y_ref in ((0, own_a, ax, ay), (split, own_b, bx, by)):
            total = own[at] + x_ref[at].astype(F32) + y_ref[at].astype(F32)
            out_ref[at, first : first + own.shape[1]] = total.astype(BF16)
        copy = pltpu.make_async_copy(
            out_ref.at[pl.ds(c * size, size)], prefill_hbm.at[0, pl.ds(c * size, size)], sems.at[c]
        )
        copy.start()
        copies.append(copy)
    rows, steps = decode_ref.shape[0], decode_ref.shape[1]
    total = d_own[...] + d_got[...].astype(F32)
    for r in range(rows):
        decode_ref[r] = total[r * steps : (r + 1) * steps].astype(BF16)
    for copy in copies:
        copy.wait()


def swap(array, axis, size, bit):
    return lax.ppermute(array, axis, [(i, i ^ bit) for i in range(size)])


def body(
    prefill_query,
    prefill_key,
    prefill_value,
    prefill_rate,
    out_weight,
    decode_query,
    decode_key,
    decode_value,
    decode_rate,
    prompt_of_row,
    *,
    groups,
    reps,
    parts,
):
    length = prefill_query.shape[1]
    features = prefill_query.shape[2]
    heads = prefill_rate.shape[1]
    rows_here, steps = decode_query.shape[0], decode_query.shape[1]
    d_rows = rows_here * steps
    d_pad = -(-d_rows // 16) * 16
    place = jnp.stack([lax.axis_index("ctx"), lax.axis_index("rep"), lax.axis_index("head")])
    place = place.astype(jnp.int32)
    count = min(CHUNKS, heads)
    edges = [heads * c // count for c in range(count + 1)]
    chunks = [(a, b - a) for a, b in zip(edges[:-1], edges[1:])]
    phases = groups - 1
    state_elements = heads * HEAD_DIM * HEAD_DIM

    def in_hbm(array):
        return pltpu.with_memory_space_constraint(array, pltpu.HBM)

    def in_vmem(array):
        return pltpu.with_memory_space_constraint(array, pltpu.VMEM)

    def message_shape(size):
        return sds((size * HEAD_DIM + LOG_ROWS, HEAD_DIM), BF16)

    decode_shape = (rows_here, steps, features)
    made = call(
        first_state_kernel,
        "own_state",
        [SMEM] + [HBM] * 3,
        [
            pltpu.VMEM((chunks[0][1], HEAD_DIM, HEAD_DIM), F32),
            pltpu.VMEM((1, HEAD_DIM), F32),
            pltpu.VMEM((length, heads), F32),
            pltpu.VMEM((1, heads, length), F32),
            pltpu.VMEM((length, features), BF16),
            pltpu.VMEM((length, features), BF16),
            message_shape(chunks[0][1]),
        ],
        [pltpu.SemaphoreType.DMA((3,))],
        cost(4 * length * features * HEAD_DIM, 16 * length * features),
    )(place, in_hbm(prefill_key), in_hbm(prefill_value), in_hbm(prefill_rate))
    own, log_row, columns, rate, keys, values = map(in_vmem, made[:6])
    owns, values_out = [own], [made[6]]
    weight_hbm = in_hbm(out_weight)
    weight_part = pltpu.VMEM((features // WEIGHT_PARTS, out_weight.shape[1]), BF16)
    token = sds((8, HEAD_DIM), F32)
    arrays = (prefill_query, decode_query, decode_key, decode_value)
    queries, d_query, d_key, d_value, local, local_token, *weights = call(
        functools.partial(local_kernel, len(arrays)),
        "local_attention",
        [VMEM] * 4 + [HBM] * (1 + len(arrays)),
        [pltpu.VMEM(array.shape, BF16) for array in arrays]
        + [pltpu.VMEM((length, features), F32), token]
        + [weight_part] * EARLY_PARTS,
        [pltpu.SemaphoreType.DMA((EARLY_PARTS,)), pltpu.SemaphoreType.DMA((len(arrays),))],
        cost(4 * length * length * features, 12 * length * features, heads * length * length),
    )(keys, values, columns, rate, weight_hbm, *map(in_hbm, arrays))
    queries, d_query, d_key, d_value, local = map(
        in_vmem, (queries, d_query, d_key, d_value, local)
    )
    for first, size in chunks[1:]:
        made = call(
            functools.partial(more_state_kernel, first),
            "more_state",
            [VMEM] * 4 + [ANY],
            [pltpu.VMEM((size, HEAD_DIM, HEAD_DIM), F32), message_shape(size)],
            (),
            cost(4 * length * size * HEAD_DIM * HEAD_DIM, 8 * length * features),
        )(keys, values, columns, log_row, local_token)
        owns.append(in_vmem(made[0]))
        values_out.append(made[1])

    todo = list(LATER_PARTS)

    def load_weight(*after):
        if not todo:
            return []
        places = range(len(weights), len(weights) + todo.pop(0))
        *loaded, done = call(
            functools.partial(load_kernel, places),
            "load_weight",
            [HBM] + [ANY] * len(after),
            [weight_part] * len(places) + [token],
            [pltpu.SemaphoreType.DMA((len(places),))],
            cost(1, 1),
        )(weight_hbm, *after)
        weights.extend(loaded)
        return [done]

    received = []
    after = values_out[-1:]
    for phase in range(phases):
        pairs = []
        for g in range(groups):
            for r in range(reps):
                if g in (phase, groups - 2 - phase):
                    other = (g + 1, r)
                elif g in (phase + 1, groups - 1 - phase):
                    other = (g - 1, r)
                else:
                    other = (g, r ^ 1)
                pairs.append((g * reps + r, other[0] * reps + other[1]))
        if phase > 0:
            values_out = []
            for c, (first, size) in enumerate(chunks):
                value = call(
                    functools.partial(chain_kernel, phase, first),
                    "chain",
                    [SMEM, VMEM, VMEM, VMEM] + [ANY] * len(after),
                    message_shape(size),
                    (),
                    cost(2 * size * HEAD_DIM * HEAD_DIM, 24 * size * HEAD_DIM * HEAD_DIM),
                )(place, owns[c], log_row, received[-1][c], *after)
                values_out.append(value)
                after = load_weight(value) if c == 0 else []
        received.append([lax.ppermute(value, ("ctx", "rep"), pairs) for value in values_out])
    loaded = []
    while todo:
        loaded = load_weight(values_out[-1], *loaded)
    weights = [in_vmem(part) for part in weights]

    after = loaded
    hidden = [
        call(
            functools.partial(hidden_kernel, phases, first),
            "hidden",
            [SMEM] + [VMEM] * (3 + phases) + [ANY] * len(after),
            sds((length, size * HEAD_DIM), BF16),
            (),
            cost(2 * length * size * HEAD_DIM * HEAD_DIM, 20 * length * size * HEAD_DIM),
        )(place, queries, columns, local, *[received[phase][c] for phase in range(phases)], *after)
        for c, (first, size) in enumerate(chunks)
    ]

    def final_states(*after):
        finals = []
        for c, (first, size) in enumerate(chunks):
            gate = after[c : c + 1]
            finals.append(
                call(
                    functools.partial(final_kernel, first, phases),
                    "final_state",
                    [SMEM, VMEM, VMEM] + [VMEM] * phases + [ANY] * len(gate),
                    sds((size, HEAD_DIM, HEAD_DIM), F32),
                    (),
                    cost(1, 1),
                )(place, owns[c], log_row, *[got[c] for got in received], *gate)
            )
        return finals, [swap(final, "rep", reps, 1) for final in finals]

    def decode_rows(finals, others, *after):
        flat = pltpu.VMEM((d_rows, features), F32)
        return call(
            functools.partial(decode_kernel, count),
            "decode_rows",
            [SMEM, SMEM] + [VMEM] * (4 + 2 * count) + [ANY] * len(after),
            sds((d_pad, features), BF16),
            [flat, flat, flat, pltpu.VMEM((d_rows, heads), F32)],
            cost(1, 1),
        )(
            place,
            prompt_of_row,
            d_query,
            d_key,
            d_value,
            jnp.transpose(decode_rate, (0, 2, 1)),
            *finals,
            *others,
            *after,
        )

    out_columns = out_weight.shape[1]
    if parts != 4 or (out_columns // parts) % 256 != 0 or length % 64 != 0:
        rows_all = jnp.concatenate([jnp.concatenate(hidden, axis=1), decode_rows(*final_states())], axis=0)
        terms = jnp.dot(rows_all, out_weight, preferred_element_type=F32)
        summed = lax.psum_scatter(terms, "head", scatter_dimension=1, tiled=True)
        prefill_out = summed[:length].astype(BF16)[None]
        decode_out = summed[length : length + d_rows].astype(BF16)
        return prefill_out, decode_out.reshape(rows_here, steps, -1)

    width = out_columns // parts
    split = (width * 5 // 12) // HEAD_DIM * HEAD_DIM
    side_x, side_y = (0, split), (split, width - split)

    def project(pieces, dtype, inputs=None, parts_used=None, addends=(), after=()):
        inputs = hidden if inputs is None else inputs
        used = weights if parts_used is None else weights[parts_used]
        moved = sum(columns for _, _, columns in pieces)
        depth = sum(array.shape[1] for array in inputs)
        return call(
            functools.partial(project_kernel, pieces, width, len(inputs), len(addends), len(used)),
            "project",
            [SMEM] + [VMEM] * (len(inputs) + len(addends) + len(used)) + [ANY] * len(after),
            [sds((length, columns), dtype) for _, _, columns in pieces],
            (),
            cost(1, 1),
        )(place, *inputs, *addends, *used, *after)

    def relay(own_term, got, *after):
        return call(
            relay_kernel,
            "relay",
            [VMEM, VMEM] + [ANY] * len(after),
            sds(own_term.shape, BF16),
            (),
            cost(1, 1),
        )(own_term, got, *after)

    far = [(3, *side_x), (3, *side_y)]
    if count == 2 and chunks[0][1] * HEAD_DIM * 2 == features and WEIGHT_PARTS % 2 == 0:
        early = slice(0, WEIGHT_PARTS // 2)
        late = slice(WEIGHT_PARTS // 2, WEIGHT_PARTS)
        begun = project(far, F32, hidden[:1], early)
        to_x, to_y = project(far, BF16, hidden[1:], late, begun)
    else:
        begun = hidden[:1]
        to_x, to_y = project(far, BF16)
    finals, others = final_states(*begun[:1], to_y)
    far_a = swap(to_x, "head", parts, 1)
    far_b = swap(to_y, "head", parts, 2)
    near_x, = project([(1, *side_x)], BF16)
    near_y, = project([(2, *side_y)], BF16)
    x_a = swap(near_x, "head", parts, 1)
    y_b = swap(near_y, "head", parts, 2)
    pass_a, pass_b = project([(2, *side_x), (1, *side_y)], F32, after=(near_x, near_y))
    d_hidden = decode_rows(finals, others, pass_a)
    d_keep, d_send = call(
        decode_project_kernel,
        "decode_project",
        [SMEM] + [VMEM] * (1 + WEIGHT_PARTS),
        [sds((d_rows, 2 * width), F32), sds((d_rows, 2 * width), BF16)],
        (),
        cost(1, 1),
    )(place, d_hidden, *weights)
    d_got = swap(d_send, "head", parts, 1)
    own_a, own_b = project([(0, *side_x), (0, *side_y)], F32, after=(d_got,))
    d_own, d_pass = call(
        decode_relay_kernel,
        "decode_relay",
        [VMEM] * 2,
        [sds((d_rows, width), F32), sds((d_rows, width), BF16)],
        (),
        cost(1, 1),
    )(d_keep, d_got)

    sent_a, sent_b = relay(pass_a, far_a), relay(pass_b, far_b, x_a, d_send)
    y_a = swap(sent_a, "head", parts, 2)
    x_b = swap(sent_b, "head", parts, 1)

    prefill_out, decode_out = call(
        finish_kernel,
        "finish",
        [VMEM] * 8,
        [sds((1, length, width), BF16), sds((rows_here, steps, width), BF16)],
        [pltpu.VMEM((length, width), BF16), pltpu.SemaphoreType.DMA((4,))],
        cost(3 * length * width, 10 * length * width),
        out_specs=[HBM, VMEM],
    )(
        own_a,
        own_b,
        x_a,
        y_a,
        x_b,
        y_b,
        d_own,
        swap(d_pass, "head", parts, 2),
    )
    return prefill_out, decode_out


def solution(mesh):
    return jax.shard_map(
        functools.partial(
            body, groups=mesh.shape["ctx"], reps=mesh.shape["rep"], parts=mesh.shape["head"]
        ),
        mesh=mesh,
        in_specs=(
            P("rep", "ctx", "head"),
            P("rep", "ctx", "head"),
            P("rep", "ctx", "head"),
            P("rep", "head", "ctx"),
            P("head", None),
            P(("ctx", "rep"), None, "head"),
            P(("ctx", "rep"), None, "head"),
            P(("ctx", "rep"), None, "head"),
            P(("ctx", "rep"), "head", None),
            P(("ctx", "rep")),
        ),
        out_specs=(P("rep", "ctx", "head"), P(("ctx", "rep"), None, "head")),
        check_vma=False,
    )
```

```python
import functools

import jax
import jax.numpy as jnp
from jax import lax
from jax.experimental import pallas as pl
from jax.experimental.pallas import tpu as pltpu
from jax.sharding import PartitionSpec as P

HEAD_DIM = 128
EPSILON = 1e-06
NEGATIVE = -1e30
HIGH = lax.Precision.HIGHEST
CHUNKS = 2
WEIGHT_PARTS = 8
EARLY_PARTS = 3
LATER_PARTS = (2, 3)
VMEM_BYTES = 8 * 2**20
F32 = jnp.float32
BF16 = jnp.bfloat16
NT = (((1,), (1,)), ((), ()))
TN = (((0,), (0,)), ((), ()))


def params():
    return pltpu.CompilerParams(vmem_limit_bytes=VMEM_BYTES)


def cost(flops, moved, exps=0):
    return pl.CostEstimate(flops=int(flops), bytes_accessed=int(moved), transcendentals=int(exps))


def normalize(array):
    return array * lax.rsqrt(jnp.mean(array * array, axis=-1, keepdims=True) + EPSILON)


def lower_ones(length):
    rows = lax.broadcasted_iota(jnp.int32, (length, length), 0)
    cols = lax.broadcasted_iota(jnp.int32, (length, length), 1)
    return rows >= cols


def decay_columns(rate, lower):
    return -lax.dot_general(lower.astype(F32), rate, NT, precision=HIGH, preferred_element_type=F32)


def decay_rows(rate, lower):
    return -lax.dot_general(rate, lower.astype(F32), NT, precision=HIGH, preferred_element_type=F32)


def identity(size):
    rows = lax.broadcasted_iota(jnp.int32, (size, size), 0)
    cols = lax.broadcasted_iota(jnp.int32, (size, size), 1)
    return rows, cols


def head_slice(index):
    return slice(index * HEAD_DIM, (index + 1) * HEAD_DIM)


def halves(array):
    top = array.astype(BF16)
    return top, (array - top.astype(F32)).astype(BF16)

VMEM = pl.BlockSpec(memory_space=pltpu.VMEM)
SMEM = pl.BlockSpec(memory_space=pltpu.SMEM)
ANY = pl.BlockSpec(memory_space=pl.ANY)
HBM = pl.BlockSpec(memory_space=pltpu.HBM)


def call(kernel, name, in_specs, out_shape, scratch=(), estimate=None, out_specs=None):
    if out_specs is None:
        out_specs = jax.tree.map(lambda _: VMEM, out_shape)
    return pl.pallas_call(
        kernel,
        in_specs=in_specs,
        out_specs=out_specs,
        out_shape=out_shape,
        scratch_shapes=list(scratch),
        compiler_params=params(),
        cost_estimate=estimate,
        name=name,
    )


def sds(shape, dtype):
    return jax.ShapeDtypeStruct(shape, dtype)


LOG_ROWS = 16


def log_rows(log):
    top = log.astype(BF16).astype(F32)
    mid = (log - top).astype(BF16).astype(F32)
    row = lax.broadcasted_iota(jnp.int32, (LOG_ROWS, HEAD_DIM), 0)
    rest = jnp.where(row == 2, log - top - mid, 0.0)
    return jnp.where(row == 0, top, jnp.where(row == 1, mid, rest)).astype(BF16)


def read_log(message_ref):
    rows = message_ref.shape[0]
    facts = message_ref[rows - LOG_ROWS :, :].astype(F32)
    return facts[0:1] + facts[1:2] + facts[2:3]


def state_rows(message_ref, index):
    return message_ref[index * HEAD_DIM : (index + 1) * HEAD_DIM, :]


def own_states(first, k_ref, v_ref, columns, own_ref, message_ref):
    length = columns.shape[0]
    factor = jnp.exp(columns[length - 1 :, :] - columns)
    for i in range(own_ref.shape[0]):
        h = first + i
        at = head_slice(h)
        weighted = k_ref[:, at].astype(F32) * factor[:, h : h + 1]
        top, rest = halves(weighted)
        both = lax.dot_general(
            jnp.concatenate([top, rest], axis=1), v_ref[:, at], TN, preferred_element_type=F32
        )
        state = both[:HEAD_DIM] + both[HEAD_DIM:]
        own_ref[i] = state
        message_ref[i * HEAD_DIM : (i + 1) * HEAD_DIM, :] = state.astype(BF16)


def started(pairs, sems):
    copies = [
        pltpu.make_async_copy(source, target, sems.at[i]) for i, (source, target) in enumerate(pairs)
    ]
    for copy in copies:
        copy.start()
    return copies


def first_state_kernel(place_ref, k_hbm, v_hbm, rate_hbm, *refs):
    own_ref, log_ref, col_ref, rate_ref, k_ref, v_ref, message_ref, sems = refs
    copies = started(((rate_hbm, rate_ref), (k_hbm.at[0], k_ref), (v_hbm.at[0], v_ref)), sems)
    length = k_ref.shape[0]
    copies[0].wait()
    rate = rate_ref[0]
    columns = decay_columns(rate, lower_ones(length))
    col_ref[...] = columns
    log_ref[...] = jnp.zeros_like(log_ref)
    log_ref[:, : rate.shape[0]] = columns[length - 1 :, :]
    message_ref[message_ref.shape[0] - LOG_ROWS :, :] = log_rows(log_ref[...])
    copies[1].wait()
    copies[2].wait()
    own_states(0, k_ref, v_ref, columns, own_ref, message_ref)


def more_state_kernel(first, k_ref, v_ref, col_ref, log_ref, *rest):
    own_ref, message_ref = rest[-2:]
    message_ref[message_ref.shape[0] - LOG_ROWS :, :] = log_rows(log_ref[...])
    own_states(first, k_ref, v_ref, col_ref[...], own_ref, message_ref)


def chain_kernel(phase, first, place_ref, own_ref, log_ref, got_ref, *rest):
    out_ref = rest[-1]
    size = (out_ref.shape[0] - LOG_ROWS) // HEAD_DIM
    right = place_ref[0] == phase
    log = log_ref[...]
    later = read_log(got_ref)
    own_factor = jnp.where(right, 1.0, jnp.exp(later))
    got_factor = jnp.where(right, jnp.exp(log), 1.0)
    for i in range(size):
        h = first + i
        value = (
            own_factor[:, h : h + 1] * own_ref[i]
            + got_factor[:, h : h + 1] * state_rows(got_ref, i).astype(F32)
        )
        out_ref[i * HEAD_DIM : (i + 1) * HEAD_DIM, :] = value.astype(BF16)
    out_ref[size * HEAD_DIM :, :] = log_rows(log + later)


def entering_state(group, got, index):
    state = state_rows(got[0], index)
    for phase in range(1, len(got)):
        state = jnp.where(group == phase + 1, state_rows(got[phase], index), state)
    return jnp.where(group == 0, jnp.zeros_like(state), state)


def weight_copies(places, weight_hbm, weights, sems):
    copies = []
    for i, (index, ref) in enumerate(zip(places, weights)):
        depth = ref.shape[0]
        copies.append(
            pltpu.make_async_copy(weight_hbm.at[pl.ds(index * depth, depth)], ref, sems.at[i])
        )
    for copy in copies:
        copy.start()
    return copies


def load_kernel(places, weight_hbm, *rest):
    token_ref, sems = rest[-2:]
    weights = rest[-2 - len(places) : -2]
    copies = weight_copies(places, weight_hbm, weights, sems)
    token_ref[...] = jnp.zeros_like(token_ref)
    for copy in copies:
        copy.wait()


def local_kernel(copied, k_ref, v_ref, col_ref, rate_ref, weight_hbm, *rest):
    sources, rest = rest[:copied], rest[copied:]
    targets, rest = rest[:copied], rest[copied:]
    local_ref, token_ref = rest[:2]
    weights, sems, more = rest[2:-2], rest[-2], rest[-1]
    loads = started(tuple(zip(sources, targets)), more)
    copies = weight_copies(range(len(weights)), weight_hbm, weights, sems)
    token_ref[...] = jnp.zeros_like(token_ref)
    q_ref = targets[0]
    lower = lower_ones(k_ref.shape[0])
    rows = decay_rows(rate_ref[0], lower)
    loads[0].wait()
    for h in range(local_ref.shape[1] // HEAD_DIM):
        at = head_slice(h)
        scores = lax.dot_general(q_ref[0, :, at], k_ref[:, at], NT, preferred_element_type=F32)
        decay = jnp.exp(jnp.where(lower, col_ref[:, h : h + 1] - rows[h : h + 1, :], NEGATIVE))
        narrow = (scores * decay).astype(BF16)
        local_ref[:, at] = jnp.dot(narrow, v_ref[:, at], preferred_element_type=F32)
    for copy in loads[1:] + copies:
        copy.wait()


def hidden_kernel(phases, first, place_ref, q_ref, col_ref, local_ref, *rest):
    got, hidden_ref = rest[:phases], rest[-1]
    for i in range(hidden_ref.shape[1] // HEAD_DIM):
        h = first + i
        whole = head_slice(h)
        state = entering_state(place_ref[0], got, i)
        inter = jnp.dot(q_ref[0, :, whole], state, preferred_element_type=F32)
        attended = local_ref[:, whole] + inter * jnp.exp(col_ref[:, h : h + 1])
        hidden_ref[:, head_slice(i)] = normalize(attended).astype(BF16)


def final_kernel(first, phases, place_ref, own_ref, log_ref, *rest):
    got, out_ref = rest[:phases], rest[-1]
    keep = jnp.exp(log_ref[...])

    def write(group):
        prefix = got[group - 1] if group > 0 else None
        suffix = got[phases - 1 - group] if group < phases else None
        later = None if suffix is None else jnp.exp(read_log(suffix))
        for i in range(out_ref.shape[0]):
            h = first + i
            value = own_ref[i]
            if prefix is not None:
                value = value + keep[:, h : h + 1] * state_rows(prefix, i).astype(F32)
            if suffix is not None:
                value = later[:, h : h + 1] * value + state_rows(suffix, i).astype(F32)
            out_ref[i] = value

    for group in range(phases + 1):
        pl.when(place_ref[0] == group)(functools.partial(write, group))


def flat_rows(ref, rows_ref):
    rows, steps = ref.shape[0], ref.shape[1]
    for r in range(rows):
        rows_ref[r * steps : (r + 1) * steps, :] = ref[r].astype(F32)


def decode_kernel(count, place_ref, prompt_ref, q_ref, k_ref, v_ref, rate_ref, *rest):
    near, far = rest[:count], rest[count : 2 * count]
    finals = [(c, i) for c, ref in enumerate(near) for i in range(ref.shape[0])]
    out_ref, q_rows, k_rows, v_rows, rate_rows = rest[-5:]
    rows_here, steps = q_ref.shape[0], q_ref.shape[1]
    d_rows = q_rows.shape[0]
    flat_rows(q_ref, q_rows)
    flat_rows(k_ref, k_rows)
    flat_rows(v_ref, v_rows)
    flat_rows(rate_ref, rate_rows)
    rows, cols = identity(d_rows)
    seen = (rows // steps == cols // steps) & (rows >= cols)
    ones = seen.astype(F32)
    rates = rate_rows[...]
    down = -jnp.dot(ones, rates, precision=HIGH, preferred_element_type=F32)
    across = -lax.dot_general(
        rates, ones, (((0,), (1,)), ((), ())), precision=HIGH, preferred_element_type=F32
    )
    grow = jnp.exp(down)
    row_of = lax.broadcasted_iota(jnp.int32, (d_rows, HEAD_DIM), 0) // steps
    prompt = jnp.zeros((d_rows, HEAD_DIM), jnp.int32)
    for r in range(rows_here):
        prompt = jnp.where(row_of == r, prompt_ref[r], prompt)
    mine = prompt == place_ref[1]
    for i in range(rates.shape[1]):
        at = head_slice(i)
        query = q_rows[:, at]
        narrow = query.astype(BF16)
        terms = []
        c, slot = finals[i]
        for ref in (near[c], far[c]):
            top, low = halves(ref[slot])
            both = jnp.dot(
                narrow, jnp.concatenate([top, low], axis=1), preferred_element_type=F32
            )
            terms.append(both[:, :HEAD_DIM] + both[:, HEAD_DIM:])
        base = jnp.where(mine, terms[0], terms[1])
        scores = lax.dot_general(
            query, k_rows[:, at], NT, precision=HIGH, preferred_element_type=F32
        )
        decay = jnp.exp(jnp.where(seen, down[:, i : i + 1] - across[i : i + 1, :], NEGATIVE))
        intra = jnp.dot(scores * decay, v_rows[:, at], precision=HIGH, preferred_element_type=F32)
        q_rows[:, at] = normalize(base * grow[:, i : i + 1] + intra)
    pad = out_ref.shape[0] - d_rows
    value = q_rows[...]
    if pad:
        value = jnp.concatenate([value, jnp.zeros((pad, value.shape[1]), F32)], axis=0)
    out_ref[...] = value.astype(BF16)


def times_weight(rows, weights, column, width):
    total = None
    for i, ref in enumerate(weights):
        depth = ref.shape[0]
        term = jnp.dot(
            rows[:, i * depth : (i + 1) * depth],
            ref[:, pl.ds(column, width)],
            preferred_element_type=F32,
        )
        total = term if total is None else total + term
    return total


def project_kernel(pieces, width, chunks, added, place_ref, *rest):
    hidden, rest = rest[:chunks], rest[chunks:]
    addends, weights = rest[:added], rest[added : -len(pieces)]
    outs = rest[-len(pieces) :]
    rows = jnp.concatenate([ref[...] for ref in hidden], axis=1)
    for n, ((bits, first, columns), out_ref) in enumerate(zip(pieces, outs)):
        column = pl.multiple_of((place_ref[2] ^ bits) * width + first, HEAD_DIM)
        total = times_weight(rows, weights, column, columns)
        if added:
            total = total + addends[n][...]
        out_ref[...] = total.astype(out_ref.dtype)


def decode_project_kernel(place_ref, rows_ref, *rest):
    weights, outs = rest[:WEIGHT_PARTS], rest[-4:]
    width = outs[0].shape[1]
    rows = rows_ref[...]
    for bits, out_ref in enumerate(outs):
        column = pl.multiple_of((place_ref[2] ^ bits) * width, HEAD_DIM)
        terms = times_weight(rows, weights, column, width)
        out_ref[...] = terms[: out_ref.shape[0]].astype(out_ref.dtype)


def relay_kernel(own_ref, got_ref, *rest):
    out_ref = rest[-1]
    out_ref[...] = (own_ref[...] + got_ref[...].astype(F32)).astype(BF16)


def finish_kernel(own_a, own_b, ax, ay, bx, by, d_own, d_x, d_y, d_far, *rest):
    prefill_hbm, decode_ref, out_ref, sems = rest
    split = own_a.shape[1]
    count = sems.shape[0]
    size = out_ref.shape[0] // count
    copies = []
    for c in range(count):
        at = slice(c * size, (c + 1) * size)
        for first, own, x_ref, y_ref in ((0, own_a, ax, ay), (split, own_b, bx, by)):
            total = own[at] + x_ref[at].astype(F32) + y_ref[at].astype(F32)
            out_ref[at, first : first + own.shape[1]] = total.astype(BF16)
        copy = pltpu.make_async_copy(
            out_ref.at[pl.ds(c * size, size)], prefill_hbm.at[0, pl.ds(c * size, size)], sems.at[c]
        )
        copy.start()
        copies.append(copy)
    rows, steps = decode_ref.shape[0], decode_ref.shape[1]
    total = d_own[...] + d_x[...].astype(F32) + d_y[...].astype(F32) + d_far[...].astype(F32)
    for r in range(rows):
        decode_ref[r] = total[r * steps : (r + 1) * steps].astype(BF16)
    for copy in copies:
        copy.wait()


def swap(array, axis, size, bit):
    return lax.ppermute(array, axis, [(i, i ^ bit) for i in range(size)])


def body(
    prefill_query,
    prefill_key,
    prefill_value,
    prefill_rate,
    out_weight,
    decode_query,
    decode_key,
    decode_value,
    decode_rate,
    prompt_of_row,
    *,
    groups,
    reps,
    parts,
):
    length = prefill_query.shape[1]
    features = prefill_query.shape[2]
    heads = prefill_rate.shape[1]
    rows_here, steps = decode_query.shape[0], decode_query.shape[1]
    d_rows = rows_here * steps
    d_pad = -(-d_rows // 16) * 16
    place = jnp.stack([lax.axis_index("ctx"), lax.axis_index("rep"), lax.axis_index("head")])
    place = place.astype(jnp.int32)
    count = min(CHUNKS, heads)
    edges = [heads * c // count for c in range(count + 1)]
    chunks = [(a, b - a) for a, b in zip(edges[:-1], edges[1:])]
    phases = groups - 1
    state_elements = heads * HEAD_DIM * HEAD_DIM

    def in_hbm(array):
        return pltpu.with_memory_space_constraint(array, pltpu.HBM)

    def in_vmem(array):
        return pltpu.with_memory_space_constraint(array, pltpu.VMEM)

    def message_shape(size):
        return sds((size * HEAD_DIM + LOG_ROWS, HEAD_DIM), BF16)

    decode_shape = (rows_here, steps, features)
    made = call(
        first_state_kernel,
        "own_state",
        [SMEM] + [HBM] * 3,
        [
            pltpu.VMEM((chunks[0][1], HEAD_DIM, HEAD_DIM), F32),
            pltpu.VMEM((1, HEAD_DIM), F32),
            pltpu.VMEM((length, heads), F32),
            pltpu.VMEM((1, heads, length), F32),
            pltpu.VMEM((length, features), BF16),
            pltpu.VMEM((length, features), BF16),
            message_shape(chunks[0][1]),
        ],
        [pltpu.SemaphoreType.DMA((3,))],
        cost(4 * length * features * HEAD_DIM, 16 * length * features),
    )(place, in_hbm(prefill_key), in_hbm(prefill_value), in_hbm(prefill_rate))
    own, log_row, columns, rate, keys, values = map(in_vmem, made[:6])
    owns, values_out = [own], [made[6]]
    weight_hbm = in_hbm(out_weight)
    weight_part = pltpu.VMEM((features // WEIGHT_PARTS, out_weight.shape[1]), BF16)
    token = sds((8, HEAD_DIM), F32)
    arrays = (prefill_query, decode_query, decode_key, decode_value)
    queries, d_query, d_key, d_value, local, local_token, *weights = call(
        functools.partial(local_kernel, len(arrays)),
        "local_attention",
        [VMEM] * 4 + [HBM] * (1 + len(arrays)),
        [pltpu.VMEM(array.shape, BF16) for array in arrays]
        + [pltpu.VMEM((length, features), F32), token]
        + [weight_part] * EARLY_PARTS,
        [pltpu.SemaphoreType.DMA((EARLY_PARTS,)), pltpu.SemaphoreType.DMA((len(arrays),))],
        cost(4 * length * length * features, 12 * length * features, heads * length * length),
    )(keys, values, columns, rate, weight_hbm, *map(in_hbm, arrays))
    queries, d_query, d_key, d_value, local = map(
        in_vmem, (queries, d_query, d_key, d_value, local)
    )
    for first, size in chunks[1:]:
        made = call(
            functools.partial(more_state_kernel, first),
            "more_state",
            [VMEM] * 4 + [ANY],
            [pltpu.VMEM((size, HEAD_DIM, HEAD_DIM), F32), message_shape(size)],
            (),
            cost(4 * length * size * HEAD_DIM * HEAD_DIM, 8 * length * features),
        )(keys, values, columns, log_row, local_token)
        owns.append(in_vmem(made[0]))
        values_out.append(made[1])

    todo = list(LATER_PARTS)

    def load_weight(*after):
        if not todo:
            return []
        places = range(len(weights), len(weights) + todo.pop(0))
        *loaded, done = call(
            functools.partial(load_kernel, places),
            "load_weight",
            [HBM] + [ANY] * len(after),
            [weight_part] * len(places) + [token],
            [pltpu.SemaphoreType.DMA((len(places),))],
            cost(1, 1),
        )(weight_hbm, *after)
        weights.extend(loaded)
        return [done]

    received = []
    after = values_out[-1:]
    for phase in range(phases):
        pairs = []
        for g in range(groups):
            for r in range(reps):
                if g in (phase, groups - 2 - phase):
                    other = (g + 1, r)
                elif g in (phase + 1, groups - 1 - phase):
                    other = (g - 1, r)
                else:
                    other = (g, r ^ 1)
                pairs.append((g * reps + r, other[0] * reps + other[1]))
        if phase > 0:
            values_out = []
            for c, (first, size) in enumerate(chunks):
                value = call(
                    functools.partial(chain_kernel, phase, first),
                    "chain",
                    [SMEM, VMEM, VMEM, VMEM] + [ANY] * len(after),
                    message_shape(size),
                    (),
                    cost(2 * size * HEAD_DIM * HEAD_DIM, 24 * size * HEAD_DIM * HEAD_DIM),
                )(place, owns[c], log_row, received[-1][c], *after)
                values_out.append(value)
                after = load_weight(value) if c == 0 else []
        received.append([lax.ppermute(value, ("ctx", "rep"), pairs) for value in values_out])
    loaded = []
    while todo:
        loaded = load_weight(values_out[-1], *loaded)
    weights = [in_vmem(part) for part in weights]

    def make_hidden(c, *after):
        first, size = chunks[c]
        return call(
            functools.partial(hidden_kernel, phases, first),
            "hidden",
            [SMEM] + [VMEM] * (3 + phases) + [ANY] * len(after),
            sds((length, size * HEAD_DIM), BF16),
            (),
            cost(2 * length * size * HEAD_DIM * HEAD_DIM, 20 * length * size * HEAD_DIM),
        )(place, queries, columns, local, *[received[phase][c] for phase in range(phases)], *after)

    def make_final(c, *after):
        first, size = chunks[c]
        final = call(
            functools.partial(final_kernel, first, phases),
            "final_state",
            [SMEM, VMEM, VMEM] + [VMEM] * phases + [ANY] * len(after),
            sds((size, HEAD_DIM, HEAD_DIM), F32),
            (),
            cost(4 * state_elements // count, state_elements * 4),
        )(place, owns[c], log_row, *[got[c] for got in received], *after)
        return final, swap(final, "rep", reps, 1)

    hidden, finals = [make_hidden(0, *loaded)], []
    for c in range(1, count):
        finals.append(make_final(c - 1, hidden[-1]))
        hidden.append(make_hidden(c, finals[-1][0]))

    def decode_rows(finals, others, *after):
        flat = pltpu.VMEM((d_rows, features), F32)
        return call(
            functools.partial(decode_kernel, count),
            "decode_rows",
            [SMEM, SMEM] + [VMEM] * (4 + 2 * count) + [ANY] * len(after),
            sds((d_pad, features), BF16),
            [flat, flat, flat, pltpu.VMEM((d_rows, heads), F32)],
            cost(16 * d_rows * features * HEAD_DIM, state_elements),
        )(
            place,
            prompt_of_row,
            d_query,
            d_key,
            d_value,
            jnp.transpose(decode_rate, (0, 2, 1)),
            *finals,
            *others,
            *after,
        )

    out_columns = out_weight.shape[1]
    if parts != 4 or (out_columns // parts) % 256 != 0 or length % 64 != 0:
        rows_all = jnp.concatenate([jnp.concatenate(hidden, axis=1), decode_rows(*zip(*finals, make_final(count - 1)))], axis=0)
        terms = jnp.dot(rows_all, out_weight, preferred_element_type=F32)
        summed = lax.psum_scatter(terms, "head", scatter_dimension=1, tiled=True)
        prefill_out = summed[:length].astype(BF16)[None]
        decode_out = summed[length : length + d_rows].astype(BF16)
        return prefill_out, decode_out.reshape(rows_here, steps, -1)

    width = out_columns // parts
    split = (width * 5 // 12) // HEAD_DIM * HEAD_DIM
    side_x, side_y = (0, split), (split, width - split)

    def project(pieces, dtype, inputs=None, parts_used=None, addends=()):
        inputs = hidden if inputs is None else inputs
        used = weights if parts_used is None else weights[parts_used]
        moved = sum(columns for _, _, columns in pieces)
        depth = sum(array.shape[1] for array in inputs)
        return call(
            functools.partial(project_kernel, pieces, width, len(inputs), len(addends)),
            "project",
            [SMEM] + [VMEM] * (len(inputs) + len(addends) + len(used)),
            [sds((length, columns), dtype) for _, _, columns in pieces],
            (),
            cost(2 * length * depth * moved, depth * moved * 2),
        )(place, *inputs, *addends, *used)

    def relay(own_term, got):
        return call(
            relay_kernel,
            "relay",
            [VMEM, VMEM],
            sds(own_term.shape, BF16),
            (),
            cost(own_term.size, own_term.size * 8),
        )(own_term, got)

    far = [(3, *side_x), (3, *side_y)]
    if count == 2 and chunks[0][1] * HEAD_DIM * 2 == features and WEIGHT_PARTS % 2 == 0:
        early = slice(0, WEIGHT_PARTS // 2)
        late = slice(WEIGHT_PARTS // 2, WEIGHT_PARTS)
        begun = project(far, F32, hidden[:1], early)
        to_x, to_y = project(far, BF16, hidden[1:], late, begun)
    else:
        to_x, to_y = project(far, BF16)
    far_a = swap(to_x, "head", parts, 1)
    far_b = swap(to_y, "head", parts, 2)
    x_a = swap(project([(1, *side_x)], BF16)[0], "head", parts, 1)
    y_b = swap(project([(2, *side_y)], BF16)[0], "head", parts, 2)
    pass_a, pass_b = project([(2, *side_x), (1, *side_y)], F32)
    own_a, own_b = project([(0, *side_x), (0, *side_y)], F32)
    sent_a, sent_b = relay(pass_a, far_a), relay(pass_b, far_b)
    y_a = swap(sent_a, "head", parts, 2)
    x_b = swap(sent_b, "head", parts, 1)

    finals.append(make_final(count - 1, to_y))
    d_hidden = decode_rows(*zip(*finals), sent_a, sent_b)
    d_own, d_x, d_y, d_far = call(
        decode_project_kernel,
        "decode_project",
        [SMEM] + [VMEM] * (1 + WEIGHT_PARTS),
        [sds((d_rows, width), F32)] + [sds((d_rows, width), BF16)] * 3,
        (),
        cost(2 * d_pad * features * out_columns, features * out_columns // 8),
    )(place, d_hidden, *weights)
    prefill_out, decode_out = call(
        finish_kernel,
        "finish",
        [VMEM] * 10,
        [sds((1, length, width), BF16), sds((rows_here, steps, width), BF16)],
        [pltpu.VMEM((length, width), BF16), pltpu.SemaphoreType.DMA((4,))],
        cost(3 * length * width, 10 * length * width),
        out_specs=[HBM, VMEM],
    )(
        own_a,
        own_b,
        x_a,
        y_a,
        x_b,
        y_b,
        d_own,
        swap(d_x, "head", parts, 1),
        swap(d_y, "head", parts, 2),
        swap(d_far, "head", parts, 3),
    )
    return prefill_out, decode_out


def solution(mesh):
    return jax.shard_map(
        functools.partial(
            body, groups=mesh.shape["ctx"], reps=mesh.shape["rep"], parts=mesh.shape["head"]
        ),
        mesh=mesh,
        in_specs=(
            P("rep", "ctx", "head"),
            P("rep", "ctx", "head"),
            P("rep", "ctx", "head"),
            P("rep", "head", "ctx"),
            P("head", None),
            P(("ctx", "rep"), None, "head"),
            P(("ctx", "rep"), None, "head"),
            P(("ctx", "rep"), None, "head"),
            P(("ctx", "rep"), "head", None),
            P(("ctx", "rep")),
        ),
        out_specs=(P("rep", "ctx", "head"), P(("ctx", "rep"), None, "head")),
        check_vma=False,
    )
```

```python
import functools

import jax
import jax.numpy as jnp
from jax import lax
from jax.experimental import pallas as pl
from jax.experimental.pallas import tpu as pltpu
from jax.sharding import PartitionSpec as P

HEAD_DIM = 128
EPSILON = 1e-06
NEGATIVE = -1e30
HIGH = lax.Precision.HIGHEST
CHUNKS = 2
WEIGHT_PARTS = 8
EARLY_PARTS = 3
LATER_PARTS = (2, 3)
VMEM_BYTES = 8 * 2**20
F32 = jnp.float32
BF16 = jnp.bfloat16
NT = (((1,), (1,)), ((), ()))
TN = (((0,), (0,)), ((), ()))


def params():
    return pltpu.CompilerParams(vmem_limit_bytes=VMEM_BYTES)


def cost(flops, moved, exps=0):
    return pl.CostEstimate(flops=int(flops), bytes_accessed=int(moved), transcendentals=int(exps))


def normalize(array):
    return array * lax.rsqrt(jnp.mean(array * array, axis=-1, keepdims=True) + EPSILON)


def lower_ones(length):
    rows = lax.broadcasted_iota(jnp.int32, (length, length), 0)
    cols = lax.broadcasted_iota(jnp.int32, (length, length), 1)
    return rows >= cols


def decay_columns(rate, lower):
    return -lax.dot_general(lower.astype(F32), rate, NT, precision=HIGH, preferred_element_type=F32)


def decay_rows(rate, lower):
    return -lax.dot_general(rate, lower.astype(F32), NT, precision=HIGH, preferred_element_type=F32)


def identity(size):
    rows = lax.broadcasted_iota(jnp.int32, (size, size), 0)
    cols = lax.broadcasted_iota(jnp.int32, (size, size), 1)
    return rows, cols


def head_slice(index):
    return slice(index * HEAD_DIM, (index + 1) * HEAD_DIM)


def halves(array):
    top = array.astype(BF16)
    return top, (array - top.astype(F32)).astype(BF16)

VMEM = pl.BlockSpec(memory_space=pltpu.VMEM)
SMEM = pl.BlockSpec(memory_space=pltpu.SMEM)
ANY = pl.BlockSpec(memory_space=pl.ANY)
HBM = pl.BlockSpec(memory_space=pltpu.HBM)


def call(kernel, name, in_specs, out_shape, scratch=(), estimate=None, out_specs=None):
    if out_specs is None:
        out_specs = jax.tree.map(lambda _: VMEM, out_shape)
    return pl.pallas_call(
        kernel,
        in_specs=in_specs,
        out_specs=out_specs,
        out_shape=out_shape,
        scratch_shapes=list(scratch),
        compiler_params=params(),
        cost_estimate=estimate,
        name=name,
    )


def sds(shape, dtype):
    return jax.ShapeDtypeStruct(shape, dtype)


LOG_ROWS = 16


def log_rows(log):
    top = log.astype(BF16).astype(F32)
    mid = (log - top).astype(BF16).astype(F32)
    row = lax.broadcasted_iota(jnp.int32, (LOG_ROWS, HEAD_DIM), 0)
    rest = jnp.where(row == 2, log - top - mid, 0.0)
    return jnp.where(row == 0, top, jnp.where(row == 1, mid, rest)).astype(BF16)


def read_log(message_ref):
    rows = message_ref.shape[0]
    facts = message_ref[rows - LOG_ROWS :, :].astype(F32)
    return facts[0:1] + facts[1:2] + facts[2:3]


def state_rows(message_ref, index):
    return message_ref[index * HEAD_DIM : (index + 1) * HEAD_DIM, :]


def own_states(first, k_ref, v_ref, columns, own_ref, message_ref):
    length = columns.shape[0]
    factor = jnp.exp(columns[length - 1 :, :] - columns)
    for i in range(own_ref.shape[0]):
        h = first + i
        at = head_slice(h)
        weighted = k_ref[:, at].astype(F32) * factor[:, h : h + 1]
        top, rest = halves(weighted)
        both = lax.dot_general(
            jnp.concatenate([top, rest], axis=1), v_ref[:, at], TN, preferred_element_type=F32
        )
        state = both[:HEAD_DIM] + both[HEAD_DIM:]
        own_ref[i] = state
        message_ref[i * HEAD_DIM : (i + 1) * HEAD_DIM, :] = state.astype(BF16)


def started(pairs, sems):
    copies = [
        pltpu.make_async_copy(source, target, sems.at[i]) for i, (source, target) in enumerate(pairs)
    ]
    for copy in copies:
        copy.start()
    return copies


def first_state_kernel(place_ref, k_hbm, v_hbm, rate_hbm, *refs):
    own_ref, log_ref, col_ref, rate_ref, k_ref, v_ref, message_ref, sems = refs
    copies = started(((rate_hbm, rate_ref), (k_hbm.at[0], k_ref), (v_hbm.at[0], v_ref)), sems)
    length = k_ref.shape[0]
    copies[0].wait()
    rate = rate_ref[0]
    columns = decay_columns(rate, lower_ones(length))
    col_ref[...] = columns
    log_ref[...] = jnp.zeros_like(log_ref)
    log_ref[:, : rate.shape[0]] = columns[length - 1 :, :]
    message_ref[message_ref.shape[0] - LOG_ROWS :, :] = log_rows(log_ref[...])
    copies[1].wait()
    copies[2].wait()
    own_states(0, k_ref, v_ref, columns, own_ref, message_ref)


def more_state_kernel(first, k_ref, v_ref, col_ref, log_ref, *rest):
    own_ref, message_ref = rest[-2:]
    message_ref[message_ref.shape[0] - LOG_ROWS :, :] = log_rows(log_ref[...])
    own_states(first, k_ref, v_ref, col_ref[...], own_ref, message_ref)


def chain_kernel(phase, first, place_ref, own_ref, log_ref, got_ref, *rest):
    out_ref = rest[-1]
    size = (out_ref.shape[0] - LOG_ROWS) // HEAD_DIM
    right = place_ref[0] == phase
    log = log_ref[...]
    later = read_log(got_ref)
    own_factor = jnp.where(right, 1.0, jnp.exp(later))
    got_factor = jnp.where(right, jnp.exp(log), 1.0)
    for i in range(size):
        h = first + i
        value = (
            own_factor[:, h : h + 1] * own_ref[i]
            + got_factor[:, h : h + 1] * state_rows(got_ref, i).astype(F32)
        )
        out_ref[i * HEAD_DIM : (i + 1) * HEAD_DIM, :] = value.astype(BF16)
    out_ref[size * HEAD_DIM :, :] = log_rows(log + later)


def entering_state(group, got, index):
    state = state_rows(got[0], index)
    for phase in range(1, len(got)):
        state = jnp.where(group == phase + 1, state_rows(got[phase], index), state)
    return jnp.where(group == 0, jnp.zeros_like(state), state)


def weight_copies(places, weight_hbm, weights, sems):
    copies = []
    for i, (index, ref) in enumerate(zip(places, weights)):
        depth = ref.shape[0]
        copies.append(
            pltpu.make_async_copy(weight_hbm.at[pl.ds(index * depth, depth)], ref, sems.at[i])
        )
    for copy in copies:
        copy.start()
    return copies


def load_kernel(places, weight_hbm, *rest):
    token_ref, sems = rest[-2:]
    weights = rest[-2 - len(places) : -2]
    copies = weight_copies(places, weight_hbm, weights, sems)
    token_ref[...] = jnp.zeros_like(token_ref)
    for copy in copies:
        copy.wait()


def local_kernel(copied, k_ref, v_ref, col_ref, rate_ref, weight_hbm, *rest):
    sources, rest = rest[:copied], rest[copied:]
    targets, rest = rest[:copied], rest[copied:]
    local_ref, token_ref = rest[:2]
    weights, sems, more = rest[2:-2], rest[-2], rest[-1]
    loads = started(tuple(zip(sources, targets)), more)
    copies = weight_copies(range(len(weights)), weight_hbm, weights, sems)
    token_ref[...] = jnp.zeros_like(token_ref)
    q_ref = targets[0]
    lower = lower_ones(k_ref.shape[0])
    rows = decay_rows(rate_ref[0], lower)
    loads[0].wait()
    for h in range(local_ref.shape[1] // HEAD_DIM):
        at = head_slice(h)
        scores = lax.dot_general(q_ref[0, :, at], k_ref[:, at], NT, preferred_element_type=F32)
        decay = jnp.exp(jnp.where(lower, col_ref[:, h : h + 1] - rows[h : h + 1, :], NEGATIVE))
        narrow = (scores * decay).astype(BF16)
        local_ref[:, at] = jnp.dot(narrow, v_ref[:, at], preferred_element_type=F32)
    for copy in loads[1:] + copies:
        copy.wait()


def hidden_kernel(phases, first, place_ref, q_ref, col_ref, local_ref, *rest):
    got, hidden_ref = rest[:phases], rest[-1]
    for i in range(hidden_ref.shape[1] // HEAD_DIM):
        h = first + i
        whole = head_slice(h)
        state = entering_state(place_ref[0], got, i)
        inter = jnp.dot(q_ref[0, :, whole], state, preferred_element_type=F32)
        attended = local_ref[:, whole] + inter * jnp.exp(col_ref[:, h : h + 1])
        hidden_ref[:, head_slice(i)] = normalize(attended).astype(BF16)


def final_kernel(first, phases, place_ref, own_ref, log_ref, *rest):
    got, out_ref = rest[:phases], rest[-1]
    keep = jnp.exp(log_ref[...])

    def write(group):
        prefix = got[group - 1] if group > 0 else None
        suffix = got[phases - 1 - group] if group < phases else None
        later = None if suffix is None else jnp.exp(read_log(suffix))
        for i in range(out_ref.shape[0]):
            h = first + i
            value = own_ref[i]
            if prefix is not None:
                value = value + keep[:, h : h + 1] * state_rows(prefix, i).astype(F32)
            if suffix is not None:
                value = later[:, h : h + 1] * value + state_rows(suffix, i).astype(F32)
            out_ref[i] = value

    for group in range(phases + 1):
        pl.when(place_ref[0] == group)(functools.partial(write, group))


def flat_rows(ref, rows_ref):
    rows, steps = ref.shape[0], ref.shape[1]
    for r in range(rows):
        rows_ref[r * steps : (r + 1) * steps, :] = ref[r].astype(F32)


def decode_kernel(count, place_ref, prompt_ref, q_ref, k_ref, v_ref, rate_ref, *rest):
    near, far = rest[:count], rest[count : 2 * count]
    finals = [(c, i) for c, ref in enumerate(near) for i in range(ref.shape[0])]
    out_ref, q_rows, k_rows, v_rows, rate_rows = rest[-5:]
    rows_here, steps = q_ref.shape[0], q_ref.shape[1]
    d_rows = q_rows.shape[0]
    flat_rows(q_ref, q_rows)
    flat_rows(k_ref, k_rows)
    flat_rows(v_ref, v_rows)
    flat_rows(rate_ref, rate_rows)
    rows, cols = identity(d_rows)
    seen = (rows // steps == cols // steps) & (rows >= cols)
    ones = seen.astype(F32)
    rates = rate_rows[...]
    down = -jnp.dot(ones, rates, precision=HIGH, preferred_element_type=F32)
    across = -lax.dot_general(
        rates, ones, (((0,), (1,)), ((), ())), precision=HIGH, preferred_element_type=F32
    )
    grow = jnp.exp(down)
    row_of = lax.broadcasted_iota(jnp.int32, (d_rows, HEAD_DIM), 0) // steps
    prompt = jnp.zeros((d_rows, HEAD_DIM), jnp.int32)
    for r in range(rows_here):
        prompt = jnp.where(row_of == r, prompt_ref[r], prompt)
    mine = prompt == place_ref[1]
    for i in range(rates.shape[1]):
        at = head_slice(i)
        query = q_rows[:, at]
        narrow = query.astype(BF16)
        terms = []
        c, slot = finals[i]
        for ref in (near[c], far[c]):
            top, low = halves(ref[slot])
            both = jnp.dot(
                narrow, jnp.concatenate([top, low], axis=1), preferred_element_type=F32
            )
            terms.append(both[:, :HEAD_DIM] + both[:, HEAD_DIM:])
        base = jnp.where(mine, terms[0], terms[1])
        scores = lax.dot_general(
            query, k_rows[:, at], NT, precision=HIGH, preferred_element_type=F32
        )
        decay = jnp.exp(jnp.where(seen, down[:, i : i + 1] - across[i : i + 1, :], NEGATIVE))
        intra = jnp.dot(scores * decay, v_rows[:, at], precision=HIGH, preferred_element_type=F32)
        q_rows[:, at] = normalize(base * grow[:, i : i + 1] + intra)
    pad = out_ref.shape[0] - d_rows
    value = q_rows[...]
    if pad:
        value = jnp.concatenate([value, jnp.zeros((pad, value.shape[1]), F32)], axis=0)
    out_ref[...] = value.astype(BF16)


def times_weight(rows, weights, column, width):
    total = None
    for i, ref in enumerate(weights):
        depth = ref.shape[0]
        term = jnp.dot(
            rows[:, i * depth : (i + 1) * depth],
            ref[:, pl.ds(column, width)],
            preferred_element_type=F32,
        )
        total = term if total is None else total + term
    return total


def project_kernel(pieces, width, chunks, added, place_ref, *rest):
    hidden, rest = rest[:chunks], rest[chunks:]
    addends, weights = rest[:added], rest[added : -len(pieces)]
    outs = rest[-len(pieces) :]
    rows = jnp.concatenate([ref[...] for ref in hidden], axis=1)
    for n, ((bits, first, columns), out_ref) in enumerate(zip(pieces, outs)):
        column = pl.multiple_of((place_ref[2] ^ bits) * width + first, HEAD_DIM)
        total = times_weight(rows, weights, column, columns)
        if added:
            total = total + addends[n][...]
        out_ref[...] = total.astype(out_ref.dtype)


def decode_project_kernel(place_ref, rows_ref, *rest):
    weights, outs = rest[:WEIGHT_PARTS], rest[-4:]
    width = outs[0].shape[1]
    rows = rows_ref[...]
    for bits, out_ref in enumerate(outs):
        column = pl.multiple_of((place_ref[2] ^ bits) * width, HEAD_DIM)
        terms = times_weight(rows, weights, column, width)
        out_ref[...] = terms[: out_ref.shape[0]].astype(out_ref.dtype)


def relay_kernel(own_ref, got_ref, *rest):
    out_ref = rest[-1]
    out_ref[...] = (own_ref[...] + got_ref[...].astype(F32)).astype(BF16)


def finish_kernel(own_a, own_b, ax, ay, bx, by, d_own, d_x, d_y, d_far, *rest):
    prefill_hbm, decode_ref, out_ref, sems = rest
    split = own_a.shape[1]
    count = sems.shape[0]
    size = out_ref.shape[0] // count
    copies = []
    for c in range(count):
        at = slice(c * size, (c + 1) * size)
        for first, own, x_ref, y_ref in ((0, own_a, ax, ay), (split, own_b, bx, by)):
            total = own[at] + x_ref[at].astype(F32) + y_ref[at].astype(F32)
            out_ref[at, first : first + own.shape[1]] = total.astype(BF16)
        copy = pltpu.make_async_copy(
            out_ref.at[pl.ds(c * size, size)], prefill_hbm.at[0, pl.ds(c * size, size)], sems.at[c]
        )
        copy.start()
        copies.append(copy)
    rows, steps = decode_ref.shape[0], decode_ref.shape[1]
    total = d_own[...] + d_x[...].astype(F32) + d_y[...].astype(F32) + d_far[...].astype(F32)
    for r in range(rows):
        decode_ref[r] = total[r * steps : (r + 1) * steps].astype(BF16)
    for copy in copies:
        copy.wait()


def swap(array, axis, size, bit):
    return lax.ppermute(array, axis, [(i, i ^ bit) for i in range(size)])


def body(
    prefill_query,
    prefill_key,
    prefill_value,
    prefill_rate,
    out_weight,
    decode_query,
    decode_key,
    decode_value,
    decode_rate,
    prompt_of_row,
    *,
    groups,
    reps,
    parts,
):
    length = prefill_query.shape[1]
    features = prefill_query.shape[2]
    heads = prefill_rate.shape[1]
    rows_here, steps = decode_query.shape[0], decode_query.shape[1]
    d_rows = rows_here * steps
    d_pad = -(-d_rows // 16) * 16
    place = jnp.stack([lax.axis_index("ctx"), lax.axis_index("rep"), lax.axis_index("head")])
    place = place.astype(jnp.int32)
    count = min(CHUNKS, heads)
    edges = [heads * c // count for c in range(count + 1)]
    chunks = [(a, b - a) for a, b in zip(edges[:-1], edges[1:])]
    phases = groups - 1
    state_elements = heads * HEAD_DIM * HEAD_DIM

    def in_hbm(array):
        return pltpu.with_memory_space_constraint(array, pltpu.HBM)

    def in_vmem(array):
        return pltpu.with_memory_space_constraint(array, pltpu.VMEM)

    def message_shape(size):
        return sds((size * HEAD_DIM + LOG_ROWS, HEAD_DIM), BF16)

    decode_shape = (rows_here, steps, features)
    made = call(
        first_state_kernel,
        "own_state",
        [SMEM] + [HBM] * 3,
        [
            pltpu.VMEM((chunks[0][1], HEAD_DIM, HEAD_DIM), F32),
            pltpu.VMEM((1, HEAD_DIM), F32),
            pltpu.VMEM((length, heads), F32),
            pltpu.VMEM((1, heads, length), F32),
            pltpu.VMEM((length, features), BF16),
            pltpu.VMEM((length, features), BF16),
            message_shape(chunks[0][1]),
        ],
        [pltpu.SemaphoreType.DMA((3,))],
        cost(4 * length * features * HEAD_DIM, 16 * length * features),
    )(place, in_hbm(prefill_key), in_hbm(prefill_value), in_hbm(prefill_rate))
    own, log_row, columns, rate, keys, values = map(in_vmem, made[:6])
    owns, values_out = [own], [made[6]]
    weight_hbm = in_hbm(out_weight)
    weight_part = pltpu.VMEM((features // WEIGHT_PARTS, out_weight.shape[1]), BF16)
    token = sds((8, HEAD_DIM), F32)
    arrays = (prefill_query, decode_query, decode_key, decode_value)
    queries, d_query, d_key, d_value, local, local_token, *weights = call(
        functools.partial(local_kernel, len(arrays)),
        "local_attention",
        [VMEM] * 4 + [HBM] * (1 + len(arrays)),
        [pltpu.VMEM(array.shape, BF16) for array in arrays]
        + [pltpu.VMEM((length, features), F32), token]
        + [weight_part] * EARLY_PARTS,
        [pltpu.SemaphoreType.DMA((EARLY_PARTS,)), pltpu.SemaphoreType.DMA((len(arrays),))],
        cost(4 * length * length * features, 12 * length * features, heads * length * length),
    )(keys, values, columns, rate, weight_hbm, *map(in_hbm, arrays))
    queries, d_query, d_key, d_value, local = map(
        in_vmem, (queries, d_query, d_key, d_value, local)
    )
    for first, size in chunks[1:]:
        made = call(
            functools.partial(more_state_kernel, first),
            "more_state",
            [VMEM] * 4 + [ANY],
            [pltpu.VMEM((size, HEAD_DIM, HEAD_DIM), F32), message_shape(size)],
            (),
            cost(4 * length * size * HEAD_DIM * HEAD_DIM, 8 * length * features),
        )(keys, values, columns, log_row, local_token)
        owns.append(in_vmem(made[0]))
        values_out.append(made[1])

    todo = list(LATER_PARTS)

    def load_weight(*after):
        if not todo:
            return []
        places = range(len(weights), len(weights) + todo.pop(0))
        *loaded, done = call(
            functools.partial(load_kernel, places),
            "load_weight",
            [HBM] + [ANY] * len(after),
            [weight_part] * len(places) + [token],
            [pltpu.SemaphoreType.DMA((len(places),))],
            cost(1, 1),
        )(weight_hbm, *after)
        weights.extend(loaded)
        return [done]

    received = []
    after = values_out[-1:]
    for phase in range(phases):
        pairs = []
        for g in range(groups):
            for r in range(reps):
                if g in (phase, groups - 2 - phase):
                    other = (g + 1, r)
                elif g in (phase + 1, groups - 1 - phase):
                    other = (g - 1, r)
                else:
                    other = (g, r ^ 1)
                pairs.append((g * reps + r, other[0] * reps + other[1]))
        if phase > 0:
            values_out = []
            for c, (first, size) in enumerate(chunks):
                value = call(
                    functools.partial(chain_kernel, phase, first),
                    "chain",
                    [SMEM, VMEM, VMEM, VMEM] + [ANY] * len(after),
                    message_shape(size),
                    (),
                    cost(2 * size * HEAD_DIM * HEAD_DIM, 24 * size * HEAD_DIM * HEAD_DIM),
                )(place, owns[c], log_row, received[-1][c], *after)
                values_out.append(value)
                after = load_weight(value) if c == 0 else []
        received.append([lax.ppermute(value, ("ctx", "rep"), pairs) for value in values_out])
    loaded = []
    while todo:
        loaded = load_weight(values_out[-1], *loaded)
    weights = [in_vmem(part) for part in weights]

    def make_hidden(c, *after):
        first, size = chunks[c]
        return call(
            functools.partial(hidden_kernel, phases, first),
            "hidden",
            [SMEM] + [VMEM] * (3 + phases) + [ANY] * len(after),
            sds((length, size * HEAD_DIM), BF16),
            (),
            cost(2 * length * size * HEAD_DIM * HEAD_DIM, 20 * length * size * HEAD_DIM),
        )(place, queries, columns, local, *[received[phase][c] for phase in range(phases)], *after)

    def make_final(c, *after):
        first, size = chunks[c]
        final = call(
            functools.partial(final_kernel, first, phases),
            "final_state",
            [SMEM, VMEM, VMEM] + [VMEM] * phases + [ANY] * len(after),
            sds((size, HEAD_DIM, HEAD_DIM), F32),
            (),
            cost(4 * state_elements // count, state_elements * 4),
        )(place, owns[c], log_row, *[got[c] for got in received], *after)
        return final, swap(final, "rep", reps, 1)

    hidden, finals = [make_hidden(0, *loaded)], []
    for c in range(1, count):
        finals.append(make_final(c - 1, hidden[-1]))
        hidden.append(make_hidden(c, finals[-1][0]))

    def decode_rows(finals, others, *after):
        flat = pltpu.VMEM((d_rows, features), F32)
        return call(
            functools.partial(decode_kernel, count),
            "decode_rows",
            [SMEM, SMEM] + [VMEM] * (4 + 2 * count) + [ANY] * len(after),
            sds((d_pad, features), BF16),
            [flat, flat, flat, pltpu.VMEM((d_rows, heads), F32)],
            cost(16 * d_rows * features * HEAD_DIM, state_elements),
        )(
            place,
            prompt_of_row,
            d_query,
            d_key,
            d_value,
            jnp.transpose(decode_rate, (0, 2, 1)),
            *finals,
            *others,
            *after,
        )

    out_columns = out_weight.shape[1]
    if parts != 4 or (out_columns // parts) % 256 != 0 or length % 64 != 0:
        rows_all = jnp.concatenate([jnp.concatenate(hidden, axis=1), decode_rows(*zip(*finals, make_final(count - 1)))], axis=0)
        terms = jnp.dot(rows_all, out_weight, preferred_element_type=F32)
        summed = lax.psum_scatter(terms, "head", scatter_dimension=1, tiled=True)
        prefill_out = summed[:length].astype(BF16)[None]
        decode_out = summed[length : length + d_rows].astype(BF16)
        return prefill_out, decode_out.reshape(rows_here, steps, -1)

    width = out_columns // parts
    split = (width * 5 // 12) // HEAD_DIM * HEAD_DIM
    side_x, side_y = (0, split), (split, width - split)

    def project(pieces, dtype, inputs=None, parts_used=None, addends=()):
        dtypes = dtype if isinstance(dtype, tuple) else (dtype,) * len(pieces)
        inputs = hidden if inputs is None else inputs
        used = weights if parts_used is None else weights[parts_used]
        moved = sum(columns for _, _, columns in pieces)
        depth = sum(array.shape[1] for array in inputs)
        return call(
            functools.partial(project_kernel, pieces, width, len(inputs), len(addends)),
            "project",
            [SMEM] + [VMEM] * (len(inputs) + len(addends) + len(used)),
            [sds((length, columns), kind) for (_, _, columns), kind in zip(pieces, dtypes)],
            (),
            cost(2 * length * depth * moved, depth * moved * 2),
        )(place, *inputs, *addends, *used)

    def relay(own_term, got):
        return call(
            relay_kernel,
            "relay",
            [VMEM, VMEM],
            sds(own_term.shape, BF16),
            (),
            cost(own_term.size, own_term.size * 8),
        )(own_term, got)

    far = [(3, *side_x), (3, *side_y)]
    if count == 2 and chunks[0][1] * HEAD_DIM * 2 == features and WEIGHT_PARTS % 2 == 0:
        early = slice(0, WEIGHT_PARTS // 2)
        late = slice(WEIGHT_PARTS // 2, WEIGHT_PARTS)
        begun = project(far, F32, hidden[:1], early)
        to_x, to_y = project(far, BF16, hidden[1:], late, begun)
    else:
        to_x, to_y = project(far, BF16)
    far_a = swap(to_x, "head", parts, 1)
    far_b = swap(to_y, "head", parts, 2)
    near_x, own_a, own_b = project([(1, *side_x), (0, *side_x), (0, *side_y)], (BF16, F32, F32))
    x_a = swap(near_x, "head", parts, 1)
    y_b = swap(project([(2, *side_y)], BF16)[0], "head", parts, 2)
    pass_a, pass_b = project([(2, *side_x), (1, *side_y)], F32)
    sent_a, sent_b = relay(pass_a, far_a), relay(pass_b, far_b)
    y_a = swap(sent_a, "head", parts, 2)
    x_b = swap(sent_b, "head", parts, 1)

    finals.append(make_final(count - 1, to_y))
    d_hidden = decode_rows(*zip(*finals), sent_a, sent_b)
    d_own, d_x, d_y, d_far = call(
        decode_project_kernel,
        "decode_project",
        [SMEM] + [VMEM] * (1 + WEIGHT_PARTS),
        [sds((d_rows, width), F32)] + [sds((d_rows, width), BF16)] * 3,
        (),
        cost(2 * d_pad * features * out_columns, features * out_columns // 8),
    )(place, d_hidden, *weights)
    prefill_out, decode_out = call(
        finish_kernel,
        "finish",
        [VMEM] * 10,
        [sds((1, length, width), BF16), sds((rows_here, steps, width), BF16)],
        [pltpu.VMEM((length, width), BF16), pltpu.SemaphoreType.DMA((4,))],
        cost(3 * length * width, 10 * length * width),
        out_specs=[HBM, VMEM],
    )(
        own_a,
        own_b,
        x_a,
        y_a,
        x_b,
        y_b,
        d_own,
        swap(d_x, "head", parts, 1),
        swap(d_y, "head", parts, 2),
        swap(d_far, "head", parts, 3),
    )
    return prefill_out, decode_out


def solution(mesh):
    return jax.shard_map(
        functools.partial(
            body, groups=mesh.shape["ctx"], reps=mesh.shape["rep"], parts=mesh.shape["head"]
        ),
        mesh=mesh,
        in_specs=(
            P("rep", "ctx", "head"),
            P("rep", "ctx", "head"),
            P("rep", "ctx", "head"),
            P("rep", "head", "ctx"),
            P("head", None),
            P(("ctx", "rep"), None, "head"),
            P(("ctx", "rep"), None, "head"),
            P(("ctx", "rep"), None, "head"),
            P(("ctx", "rep"), "head", None),
            P(("ctx", "rep")),
        ),
        out_specs=(P("rep", "ctx", "head"), P(("ctx", "rep"), None, "head")),
        check_vma=False,
    )
```

```python
import functools

import jax
import jax.numpy as jnp
from jax import lax
from jax.experimental import pallas as pl
from jax.experimental.pallas import tpu as pltpu
from jax.sharding import PartitionSpec as P

HEAD_DIM = 128
EPSILON = 1e-06
NEGATIVE = -1e30
HIGH = lax.Precision.HIGHEST
CHUNKS = 2
WEIGHT_PARTS = 8
EARLY_PARTS = 3
LATER_PARTS = (2, 3)
VMEM_BYTES = 8 * 2**20
F32 = jnp.float32
BF16 = jnp.bfloat16
NT = (((1,), (1,)), ((), ()))
TN = (((0,), (0,)), ((), ()))


def params():
    return pltpu.CompilerParams(vmem_limit_bytes=VMEM_BYTES)


def cost(flops, moved, exps=0):
    return pl.CostEstimate(flops=int(flops), bytes_accessed=int(moved), transcendentals=int(exps))


def normalize(array):
    return array * lax.rsqrt(jnp.mean(array * array, axis=-1, keepdims=True) + EPSILON)


def lower_ones(length):
    rows = lax.broadcasted_iota(jnp.int32, (length, length), 0)
    cols = lax.broadcasted_iota(jnp.int32, (length, length), 1)
    return rows >= cols


def decay_columns(rate, lower):
    return -lax.dot_general(lower.astype(F32), rate, NT, precision=HIGH, preferred_element_type=F32)


def decay_rows(rate, lower):
    return -lax.dot_general(rate, lower.astype(F32), NT, precision=HIGH, preferred_element_type=F32)


def identity(size):
    rows = lax.broadcasted_iota(jnp.int32, (size, size), 0)
    cols = lax.broadcasted_iota(jnp.int32, (size, size), 1)
    return rows, cols


def head_slice(index):
    return slice(index * HEAD_DIM, (index + 1) * HEAD_DIM)


def halves(array):
    top = array.astype(BF16)
    return top, (array - top.astype(F32)).astype(BF16)

VMEM = pl.BlockSpec(memory_space=pltpu.VMEM)
SMEM = pl.BlockSpec(memory_space=pltpu.SMEM)
ANY = pl.BlockSpec(memory_space=pl.ANY)
HBM = pl.BlockSpec(memory_space=pltpu.HBM)


def call(kernel, name, in_specs, out_shape, scratch=(), estimate=None, out_specs=None):
    if out_specs is None:
        out_specs = jax.tree.map(lambda _: VMEM, out_shape)
    return pl.pallas_call(
        kernel,
        in_specs=in_specs,
        out_specs=out_specs,
        out_shape=out_shape,
        scratch_shapes=list(scratch),
        compiler_params=params(),
        cost_estimate=estimate,
        name=name,
    )


def sds(shape, dtype):
    return jax.ShapeDtypeStruct(shape, dtype)


LOG_ROWS = 16


def log_rows(log):
    top = log.astype(BF16).astype(F32)
    mid = (log - top).astype(BF16).astype(F32)
    row = lax.broadcasted_iota(jnp.int32, (LOG_ROWS, HEAD_DIM), 0)
    rest = jnp.where(row == 2, log - top - mid, 0.0)
    return jnp.where(row == 0, top, jnp.where(row == 1, mid, rest)).astype(BF16)


def read_log(message_ref):
    rows = message_ref.shape[0]
    facts = message_ref[rows - LOG_ROWS :, :].astype(F32)
    return facts[0:1] + facts[1:2] + facts[2:3]


def state_rows(message_ref, index):
    return message_ref[index * HEAD_DIM : (index + 1) * HEAD_DIM, :]


def own_states(first, k_ref, v_ref, columns, own_ref, message_ref):
    length = columns.shape[0]
    factor = jnp.exp(columns[length - 1 :, :] - columns)
    for i in range(own_ref.shape[0]):
        h = first + i
        at = head_slice(h)
        weighted = k_ref[:, at].astype(F32) * factor[:, h : h + 1]
        top, rest = halves(weighted)
        both = lax.dot_general(
            jnp.concatenate([top, rest], axis=1), v_ref[:, at], TN, preferred_element_type=F32
        )
        state = both[:HEAD_DIM] + both[HEAD_DIM:]
        own_ref[i] = state
        message_ref[i * HEAD_DIM : (i + 1) * HEAD_DIM, :] = state.astype(BF16)


def started(pairs, sems):
    copies = [
        pltpu.make_async_copy(source, target, sems.at[i]) for i, (source, target) in enumerate(pairs)
    ]
    for copy in copies:
        copy.start()
    return copies


def first_state_kernel(place_ref, k_hbm, v_hbm, rate_hbm, *refs):
    own_ref, log_ref, col_ref, rate_ref, k_ref, v_ref, message_ref, sems = refs
    copies = started(((rate_hbm, rate_ref), (k_hbm.at[0], k_ref), (v_hbm.at[0], v_ref)), sems)
    length = k_ref.shape[0]
    copies[0].wait()
    rate = rate_ref[0]
    columns = decay_columns(rate, lower_ones(length))
    col_ref[...] = columns
    log_ref[...] = jnp.zeros_like(log_ref)
    log_ref[:, : rate.shape[0]] = columns[length - 1 :, :]
    message_ref[message_ref.shape[0] - LOG_ROWS :, :] = log_rows(log_ref[...])
    copies[1].wait()
    copies[2].wait()
    own_states(0, k_ref, v_ref, columns, own_ref, message_ref)


def more_state_kernel(first, k_ref, v_ref, col_ref, log_ref, *rest):
    own_ref, message_ref = rest[-2:]
    message_ref[message_ref.shape[0] - LOG_ROWS :, :] = log_rows(log_ref[...])
    own_states(first, k_ref, v_ref, col_ref[...], own_ref, message_ref)


def chain_kernel(phase, first, place_ref, own_ref, log_ref, got_ref, *rest):
    out_ref = rest[-1]
    size = (out_ref.shape[0] - LOG_ROWS) // HEAD_DIM
    right = place_ref[0] == phase
    log = log_ref[...]
    later = read_log(got_ref)
    own_factor = jnp.where(right, 1.0, jnp.exp(later))
    got_factor = jnp.where(right, jnp.exp(log), 1.0)
    for i in range(size):
        h = first + i
        value = (
            own_factor[:, h : h + 1] * own_ref[i]
            + got_factor[:, h : h + 1] * state_rows(got_ref, i).astype(F32)
        )
        out_ref[i * HEAD_DIM : (i + 1) * HEAD_DIM, :] = value.astype(BF16)
    out_ref[size * HEAD_DIM :, :] = log_rows(log + later)


def entering_state(group, got, index):
    state = state_rows(got[0], index)
    for phase in range(1, len(got)):
        state = jnp.where(group == phase + 1, state_rows(got[phase], index), state)
    return jnp.where(group == 0, jnp.zeros_like(state), state)


def weight_copies(places, weight_hbm, weights, sems):
    copies = []
    for i, (index, ref) in enumerate(zip(places, weights)):
        depth = ref.shape[0]
        copies.append(
            pltpu.make_async_copy(weight_hbm.at[pl.ds(index * depth, depth)], ref, sems.at[i])
        )
    for copy in copies:
        copy.start()
    return copies


def load_kernel(places, weight_hbm, *rest):
    token_ref, sems = rest[-2:]
    weights = rest[-2 - len(places) : -2]
    copies = weight_copies(places, weight_hbm, weights, sems)
    token_ref[...] = jnp.zeros_like(token_ref)
    for copy in copies:
        copy.wait()


def local_kernel(copied, k_ref, v_ref, col_ref, rate_ref, weight_hbm, *rest):
    sources, rest = rest[:copied], rest[copied:]
    targets, rest = rest[:copied], rest[copied:]
    local_ref, token_ref = rest[:2]
    weights, sems, more = rest[2:-2], rest[-2], rest[-1]
    loads = started(tuple(zip(sources, targets)), more)
    copies = weight_copies(range(len(weights)), weight_hbm, weights, sems)
    token_ref[...] = jnp.zeros_like(token_ref)
    q_ref = targets[0]
    lower = lower_ones(k_ref.shape[0])
    rows = decay_rows(rate_ref[0], lower)
    loads[0].wait()
    for h in range(local_ref.shape[1] // HEAD_DIM):
        at = head_slice(h)
        scores = lax.dot_general(q_ref[0, :, at], k_ref[:, at], NT, preferred_element_type=F32)
        decay = jnp.exp(jnp.where(lower, col_ref[:, h : h + 1] - rows[h : h + 1, :], NEGATIVE))
        narrow = (scores * decay).astype(BF16)
        local_ref[:, at] = jnp.dot(narrow, v_ref[:, at], preferred_element_type=F32)
    for copy in loads[1:] + copies:
        copy.wait()


def hidden_kernel(phases, first, place_ref, q_ref, col_ref, local_ref, *rest):
    got, hidden_ref = rest[:phases], rest[-1]
    for i in range(hidden_ref.shape[1] // HEAD_DIM):
        h = first + i
        whole = head_slice(h)
        state = entering_state(place_ref[0], got, i)
        inter = jnp.dot(q_ref[0, :, whole], state, preferred_element_type=F32)
        attended = local_ref[:, whole] + inter * jnp.exp(col_ref[:, h : h + 1])
        hidden_ref[:, head_slice(i)] = normalize(attended).astype(BF16)


def final_kernel(first, phases, place_ref, own_ref, log_ref, *rest):
    got, out_ref = rest[:phases], rest[-1]
    keep = jnp.exp(log_ref[...])

    def write(group):
        prefix = got[group - 1] if group > 0 else None
        suffix = got[phases - 1 - group] if group < phases else None
        later = None if suffix is None else jnp.exp(read_log(suffix))
        for i in range(out_ref.shape[0]):
            h = first + i
            value = own_ref[i]
            if prefix is not None:
                value = value + keep[:, h : h + 1] * state_rows(prefix, i).astype(F32)
            if suffix is not None:
                value = later[:, h : h + 1] * value + state_rows(suffix, i).astype(F32)
            out_ref[i] = value

    for group in range(phases + 1):
        pl.when(place_ref[0] == group)(functools.partial(write, group))


def flat_rows(ref, rows_ref):
    rows, steps = ref.shape[0], ref.shape[1]
    for r in range(rows):
        rows_ref[r * steps : (r + 1) * steps, :] = ref[r].astype(F32)


def decode_kernel(count, place_ref, prompt_ref, q_ref, k_ref, v_ref, rate_ref, *rest):
    near, far = rest[:count], rest[count : 2 * count]
    finals = [(c, i) for c, ref in enumerate(near) for i in range(ref.shape[0])]
    out_ref, q_rows, k_rows, v_rows, rate_rows = rest[-5:]
    rows_here, steps = q_ref.shape[0], q_ref.shape[1]
    d_rows = q_rows.shape[0]
    flat_rows(q_ref, q_rows)
    flat_rows(k_ref, k_rows)
    flat_rows(v_ref, v_rows)
    flat_rows(rate_ref, rate_rows)
    rows, cols = identity(d_rows)
    seen = (rows // steps == cols // steps) & (rows >= cols)
    ones = seen.astype(F32)
    rates = rate_rows[...]
    down = -jnp.dot(ones, rates, precision=HIGH, preferred_element_type=F32)
    across = -lax.dot_general(
        rates, ones, (((0,), (1,)), ((), ())), precision=HIGH, preferred_element_type=F32
    )
    grow = jnp.exp(down)
    row_of = lax.broadcasted_iota(jnp.int32, (d_rows, HEAD_DIM), 0) // steps
    prompt = jnp.zeros((d_rows, HEAD_DIM), jnp.int32)
    for r in range(rows_here):
        prompt = jnp.where(row_of == r, prompt_ref[r], prompt)
    mine = prompt == place_ref[1]
    for i in range(rates.shape[1]):
        at = head_slice(i)
        query = q_rows[:, at]
        narrow = query.astype(BF16)
        terms = []
        c, slot = finals[i]
        for ref in (near[c], far[c]):
            top, low = halves(ref[slot])
            both = jnp.dot(
                narrow, jnp.concatenate([top, low], axis=1), preferred_element_type=F32
            )
            terms.append(both[:, :HEAD_DIM] + both[:, HEAD_DIM:])
        base = jnp.where(mine, terms[0], terms[1])
        scores = lax.dot_general(
            query, k_rows[:, at], NT, precision=HIGH, preferred_element_type=F32
        )
        decay = jnp.exp(jnp.where(seen, down[:, i : i + 1] - across[i : i + 1, :], NEGATIVE))
        intra = jnp.dot(scores * decay, v_rows[:, at], precision=HIGH, preferred_element_type=F32)
        q_rows[:, at] = normalize(base * grow[:, i : i + 1] + intra)
    pad = out_ref.shape[0] - d_rows
    value = q_rows[...]
    if pad:
        value = jnp.concatenate([value, jnp.zeros((pad, value.shape[1]), F32)], axis=0)
    out_ref[...] = value.astype(BF16)


def times_weight(rows, weights, column, width):
    total = None
    for i, ref in enumerate(weights):
        depth = ref.shape[0]
        term = jnp.dot(
            rows[:, i * depth : (i + 1) * depth],
            ref[:, pl.ds(column, width)],
            preferred_element_type=F32,
        )
        total = term if total is None else total + term
    return total


def project_kernel(pieces, width, chunks, added, used, place_ref, *rest):
    hidden, rest = rest[:chunks], rest[chunks:]
    addends, weights = rest[:added], rest[added : added + used]
    outs = rest[-len(pieces) :]
    rows = jnp.concatenate([ref[...] for ref in hidden], axis=1)
    for n, ((bits, first, columns), out_ref) in enumerate(zip(pieces, outs)):
        column = pl.multiple_of((place_ref[2] ^ bits) * width + first, HEAD_DIM)
        total = times_weight(rows, weights, column, columns)
        if added:
            total = total + addends[n][...]
        out_ref[...] = total.astype(out_ref.dtype)


def decode_project_kernel(place_ref, rows_ref, *rest):
    weights, outs = rest[:WEIGHT_PARTS], rest[-4:]
    width = outs[0].shape[1]
    rows = rows_ref[...]
    for bits, out_ref in enumerate(outs):
        column = pl.multiple_of((place_ref[2] ^ bits) * width, HEAD_DIM)
        terms = times_weight(rows, weights, column, width)
        out_ref[...] = terms[: out_ref.shape[0]].astype(out_ref.dtype)


def relay_kernel(own_ref, got_ref, *rest):
    out_ref = rest[-1]
    out_ref[...] = (own_ref[...] + got_ref[...].astype(F32)).astype(BF16)


def finish_kernel(own_a, own_b, ax, ay, bx, by, d_own, d_x, d_y, d_far, *rest):
    prefill_hbm, decode_ref, out_ref, sems = rest
    split = own_a.shape[1]
    count = sems.shape[0]
    size = out_ref.shape[0] // count
    copies = []
    for c in range(count):
        at = slice(c * size, (c + 1) * size)
        for first, own, x_ref, y_ref in ((0, own_a, ax, ay), (split, own_b, bx, by)):
            total = own[at] + x_ref[at].astype(F32) + y_ref[at].astype(F32)
            out_ref[at, first : first + own.shape[1]] = total.astype(BF16)
        copy = pltpu.make_async_copy(
            out_ref.at[pl.ds(c * size, size)], prefill_hbm.at[0, pl.ds(c * size, size)], sems.at[c]
        )
        copy.start()
        copies.append(copy)
    rows, steps = decode_ref.shape[0], decode_ref.shape[1]
    total = d_own[...] + d_x[...].astype(F32) + d_y[...].astype(F32) + d_far[...].astype(F32)
    for r in range(rows):
        decode_ref[r] = total[r * steps : (r + 1) * steps].astype(BF16)
    for copy in copies:
        copy.wait()


def swap(array, axis, size, bit):
    return lax.ppermute(array, axis, [(i, i ^ bit) for i in range(size)])


def body(
    prefill_query,
    prefill_key,
    prefill_value,
    prefill_rate,
    out_weight,
    decode_query,
    decode_key,
    decode_value,
    decode_rate,
    prompt_of_row,
    *,
    groups,
    reps,
    parts,
):
    length = prefill_query.shape[1]
    features = prefill_query.shape[2]
    heads = prefill_rate.shape[1]
    rows_here, steps = decode_query.shape[0], decode_query.shape[1]
    d_rows = rows_here * steps
    d_pad = -(-d_rows // 16) * 16
    place = jnp.stack([lax.axis_index("ctx"), lax.axis_index("rep"), lax.axis_index("head")])
    place = place.astype(jnp.int32)
    count = min(CHUNKS, heads)
    edges = [heads * c // count for c in range(count + 1)]
    chunks = [(a, b - a) for a, b in zip(edges[:-1], edges[1:])]
    phases = groups - 1
    state_elements = heads * HEAD_DIM * HEAD_DIM

    def in_hbm(array):
        return pltpu.with_memory_space_constraint(array, pltpu.HBM)

    def in_vmem(array):
        return pltpu.with_memory_space_constraint(array, pltpu.VMEM)

    def message_shape(size):
        return sds((size * HEAD_DIM + LOG_ROWS, HEAD_DIM), BF16)

    decode_shape = (rows_here, steps, features)
    made = call(
        first_state_kernel,
        "own_state",
        [SMEM] + [HBM] * 3,
        [
            pltpu.VMEM((chunks[0][1], HEAD_DIM, HEAD_DIM), F32),
            pltpu.VMEM((1, HEAD_DIM), F32),
            pltpu.VMEM((length, heads), F32),
            pltpu.VMEM((1, heads, length), F32),
            pltpu.VMEM((length, features), BF16),
            pltpu.VMEM((length, features), BF16),
            message_shape(chunks[0][1]),
        ],
        [pltpu.SemaphoreType.DMA((3,))],
        cost(4 * length * features * HEAD_DIM, 16 * length * features),
    )(place, in_hbm(prefill_key), in_hbm(prefill_value), in_hbm(prefill_rate))
    own, log_row, columns, rate, keys, values = map(in_vmem, made[:6])
    owns, values_out = [own], [made[6]]
    weight_hbm = in_hbm(out_weight)
    weight_part = pltpu.VMEM((features // WEIGHT_PARTS, out_weight.shape[1]), BF16)
    token = sds((8, HEAD_DIM), F32)
    arrays = (prefill_query, decode_query, decode_key, decode_value)
    queries, d_query, d_key, d_value, local, local_token, *weights = call(
        functools.partial(local_kernel, len(arrays)),
        "local_attention",
        [VMEM] * 4 + [HBM] * (1 + len(arrays)),
        [pltpu.VMEM(array.shape, BF16) for array in arrays]
        + [pltpu.VMEM((length, features), F32), token]
        + [weight_part] * EARLY_PARTS,
        [pltpu.SemaphoreType.DMA((EARLY_PARTS,)), pltpu.SemaphoreType.DMA((len(arrays),))],
        cost(4 * length * length * features, 12 * length * features, heads * length * length),
    )(keys, values, columns, rate, weight_hbm, *map(in_hbm, arrays))
    queries, d_query, d_key, d_value, local = map(
        in_vmem, (queries, d_query, d_key, d_value, local)
    )
    for first, size in chunks[1:]:
        made = call(
            functools.partial(more_state_kernel, first),
            "more_state",
            [VMEM] * 4 + [ANY],
            [pltpu.VMEM((size, HEAD_DIM, HEAD_DIM), F32), message_shape(size)],
            (),
            cost(4 * length * size * HEAD_DIM * HEAD_DIM, 8 * length * features),
        )(keys, values, columns, log_row, local_token)
        owns.append(in_vmem(made[0]))
        values_out.append(made[1])

    todo = list(LATER_PARTS)

    def load_weight(*after):
        if not todo:
            return []
        places = range(len(weights), len(weights) + todo.pop(0))
        *loaded, done = call(
            functools.partial(load_kernel, places),
            "load_weight",
            [HBM] + [ANY] * len(after),
            [weight_part] * len(places) + [token],
            [pltpu.SemaphoreType.DMA((len(places),))],
            cost(1, 1),
        )(weight_hbm, *after)
        weights.extend(loaded)
        return [done]

    received = []
    after = values_out[-1:]
    for phase in range(phases):
        pairs = []
        for g in range(groups):
            for r in range(reps):
                if g in (phase, groups - 2 - phase):
                    other = (g + 1, r)
                elif g in (phase + 1, groups - 1 - phase):
                    other = (g - 1, r)
                else:
                    other = (g, r ^ 1)
                pairs.append((g * reps + r, other[0] * reps + other[1]))
        if phase > 0:
            values_out = []
            for c, (first, size) in enumerate(chunks):
                value = call(
                    functools.partial(chain_kernel, phase, first),
                    "chain",
                    [SMEM, VMEM, VMEM, VMEM] + [ANY] * len(after),
                    message_shape(size),
                    (),
                    cost(2 * size * HEAD_DIM * HEAD_DIM, 24 * size * HEAD_DIM * HEAD_DIM),
                )(place, owns[c], log_row, received[-1][c], *after)
                values_out.append(value)
                after = load_weight(value) if c == 0 else []
        received.append([lax.ppermute(value, ("ctx", "rep"), pairs) for value in values_out])
    loaded = []
    while todo:
        loaded = load_weight(values_out[-1], *loaded)
    weights = [in_vmem(part) for part in weights]

    def make_hidden(c, *after):
        first, size = chunks[c]
        return call(
            functools.partial(hidden_kernel, phases, first),
            "hidden",
            [SMEM] + [VMEM] * (3 + phases) + [ANY] * len(after),
            sds((length, size * HEAD_DIM), BF16),
            (),
            cost(2 * length * size * HEAD_DIM * HEAD_DIM, 20 * length * size * HEAD_DIM),
        )(place, queries, columns, local, *[received[phase][c] for phase in range(phases)], *after)

    def make_final(c, *after):
        first, size = chunks[c]
        final = call(
            functools.partial(final_kernel, first, phases),
            "final_state",
            [SMEM, VMEM, VMEM] + [VMEM] * phases + [ANY] * len(after),
            sds((size, HEAD_DIM, HEAD_DIM), F32),
            (),
            cost(4 * state_elements // count, state_elements * 4),
        )(place, owns[c], log_row, *[got[c] for got in received], *after)
        return final, swap(final, "rep", reps, 1)

    hidden, finals = [make_hidden(0, *loaded)], []
    for c in range(1, count):
        finals.append(make_final(c - 1, hidden[-1]))
        hidden.append(make_hidden(c, finals[-1][0]))

    def decode_rows(finals, others, *after):
        flat = pltpu.VMEM((d_rows, features), F32)
        return call(
            functools.partial(decode_kernel, count),
            "decode_rows",
            [SMEM, SMEM] + [VMEM] * (4 + 2 * count) + [ANY] * len(after),
            sds((d_pad, features), BF16),
            [flat, flat, flat, pltpu.VMEM((d_rows, heads), F32)],
            cost(16 * d_rows * features * HEAD_DIM, state_elements),
        )(
            place,
            prompt_of_row,
            d_query,
            d_key,
            d_value,
            jnp.transpose(decode_rate, (0, 2, 1)),
            *finals,
            *others,
            *after,
        )

    out_columns = out_weight.shape[1]
    if parts != 4 or (out_columns // parts) % 256 != 0 or length % 64 != 0:
        rows_all = jnp.concatenate([jnp.concatenate(hidden, axis=1), decode_rows(*zip(*finals, make_final(count - 1)))], axis=0)
        terms = jnp.dot(rows_all, out_weight, preferred_element_type=F32)
        summed = lax.psum_scatter(terms, "head", scatter_dimension=1, tiled=True)
        prefill_out = summed[:length].astype(BF16)[None]
        decode_out = summed[length : length + d_rows].astype(BF16)
        return prefill_out, decode_out.reshape(rows_here, steps, -1)

    width = out_columns // parts
    split = (width * 5 // 12) // HEAD_DIM * HEAD_DIM
    side_x, side_y = (0, split), (split, width - split)

    def project(pieces, dtype, inputs=None, parts_used=None, addends=(), after=()):
        dtypes = dtype if isinstance(dtype, tuple) else (dtype,) * len(pieces)
        inputs = hidden if inputs is None else inputs
        used = weights if parts_used is None else weights[parts_used]
        moved = sum(columns for _, _, columns in pieces)
        depth = sum(array.shape[1] for array in inputs)
        return call(
            functools.partial(project_kernel, pieces, width, len(inputs), len(addends), len(used)),
            "project",
            [SMEM] + [VMEM] * (len(inputs) + len(addends) + len(used)) + [ANY] * len(after),
            [sds((length, columns), kind) for (_, _, columns), kind in zip(pieces, dtypes)],
            (),
            cost(2 * length * depth * moved, depth * moved * 2),
        )(place, *inputs, *addends, *used, *after)

    def relay(own_term, got):
        return call(
            relay_kernel,
            "relay",
            [VMEM, VMEM],
            sds(own_term.shape, BF16),
            (),
            cost(own_term.size, own_term.size * 8),
        )(own_term, got)

    far = [(3, *side_x), (3, *side_y)]
    if count == 2 and chunks[0][1] * HEAD_DIM * 2 == features and WEIGHT_PARTS % 2 == 0:
        early = slice(0, WEIGHT_PARTS // 2)
        late = slice(WEIGHT_PARTS // 2, WEIGHT_PARTS)
        begun = project(far, F32, hidden[:1], early)
        to_x, to_y = project(far, BF16, hidden[1:], late, begun)
    else:
        to_x, to_y = project(far, BF16)
    far_a = swap(to_x, "head", parts, 1)
    far_b = swap(to_y, "head", parts, 2)
    near_y, near_x = project([(2, *side_y), (1, *side_x)], BF16)
    x_a = swap(near_x, "head", parts, 1)
    y_b = swap(near_y, "head", parts, 2)
    finals.append(make_final(count - 1, to_y))
    d_hidden = decode_rows(*zip(*finals), near_y)
    pass_a, pass_b = project([(2, *side_x), (1, *side_y)], F32, after=(d_hidden,))
    own_a, own_b = project([(0, *side_x), (0, *side_y)], F32)
    sent_a, sent_b = relay(pass_a, far_a), relay(pass_b, far_b)
    y_a = swap(sent_a, "head", parts, 2)
    x_b = swap(sent_b, "head", parts, 1)

    d_own, d_x, d_y, d_far = call(
        decode_project_kernel,
        "decode_project",
        [SMEM] + [VMEM] * (1 + WEIGHT_PARTS) + [ANY] * 2,
        [sds((d_rows, width), F32)] + [sds((d_rows, width), BF16)] * 3,
        (),
        cost(2 * d_pad * features * out_columns, features * out_columns // 8),
    )(place, d_hidden, *weights, sent_a, sent_b)
    prefill_out, decode_out = call(
        finish_kernel,
        "finish",
        [VMEM] * 10,
        [sds((1, length, width), BF16), sds((rows_here, steps, width), BF16)],
        [pltpu.VMEM((length, width), BF16), pltpu.SemaphoreType.DMA((4,))],
        cost(3 * length * width, 10 * length * width),
        out_specs=[HBM, VMEM],
    )(
        own_a,
        own_b,
        x_a,
        y_a,
        x_b,
        y_b,
        d_own,
        swap(d_x, "head", parts, 1),
        swap(d_y, "head", parts, 2),
        swap(d_far, "head", parts, 3),
    )
    return prefill_out, decode_out


def solution(mesh):
    return jax.shard_map(
        functools.partial(
            body, groups=mesh.shape["ctx"], reps=mesh.shape["rep"], parts=mesh.shape["head"]
        ),
        mesh=mesh,
        in_specs=(
            P("rep", "ctx", "head"),
            P("rep", "ctx", "head"),
            P("rep", "ctx", "head"),
            P("rep", "head", "ctx"),
            P("head", None),
            P(("ctx", "rep"), None, "head"),
            P(("ctx", "rep"), None, "head"),
            P(("ctx", "rep"), None, "head"),
            P(("ctx", "rep"), "head", None),
            P(("ctx", "rep")),
        ),
        out_specs=(P("rep", "ctx", "head"), P(("ctx", "rep"), None, "head")),
        check_vma=False,
    )
```

```python
import functools

import jax
import jax.numpy as jnp
from jax import lax
from jax.experimental import pallas as pl
from jax.experimental.pallas import tpu as pltpu
from jax.sharding import PartitionSpec as P

HEAD_DIM = 128
EPSILON = 1e-06
NEGATIVE = -1e30
HIGH = lax.Precision.HIGHEST
CHUNKS = 2
WEIGHT_PARTS = 8
EARLY_PARTS = 3
LATER_PARTS = (2, 3)
VMEM_BYTES = 8 * 2**20
F32 = jnp.float32
BF16 = jnp.bfloat16
NT = (((1,), (1,)), ((), ()))
TN = (((0,), (0,)), ((), ()))


def params():
    return pltpu.CompilerParams(vmem_limit_bytes=VMEM_BYTES)


def cost(flops, moved, exps=0):
    return pl.CostEstimate(flops=int(flops), bytes_accessed=int(moved), transcendentals=int(exps))


def normalize(array):
    return array * lax.rsqrt(jnp.mean(array * array, axis=-1, keepdims=True) + EPSILON)


def lower_ones(length):
    rows = lax.broadcasted_iota(jnp.int32, (length, length), 0)
    cols = lax.broadcasted_iota(jnp.int32, (length, length), 1)
    return rows >= cols


def decay_columns(rate, lower):
    return -lax.dot_general(lower.astype(F32), rate, NT, precision=HIGH, preferred_element_type=F32)


def decay_rows(rate, lower):
    return -lax.dot_general(rate, lower.astype(F32), NT, precision=HIGH, preferred_element_type=F32)


def identity(size):
    rows = lax.broadcasted_iota(jnp.int32, (size, size), 0)
    cols = lax.broadcasted_iota(jnp.int32, (size, size), 1)
    return rows, cols


def head_slice(index):
    return slice(index * HEAD_DIM, (index + 1) * HEAD_DIM)


def halves(array):
    top = array.astype(BF16)
    return top, (array - top.astype(F32)).astype(BF16)

VMEM = pl.BlockSpec(memory_space=pltpu.VMEM)
SMEM = pl.BlockSpec(memory_space=pltpu.SMEM)
ANY = pl.BlockSpec(memory_space=pl.ANY)
HBM = pl.BlockSpec(memory_space=pltpu.HBM)


def call(kernel, name, in_specs, out_shape, scratch=(), estimate=None, out_specs=None):
    if out_specs is None:
        out_specs = jax.tree.map(lambda _: VMEM, out_shape)
    return pl.pallas_call(
        kernel,
        in_specs=in_specs,
        out_specs=out_specs,
        out_shape=out_shape,
        scratch_shapes=list(scratch),
        compiler_params=params(),
        cost_estimate=estimate,
        name=name,
    )


def sds(shape, dtype):
    return jax.ShapeDtypeStruct(shape, dtype)


LOG_ROWS = 16


def log_rows(log):
    top = log.astype(BF16).astype(F32)
    mid = (log - top).astype(BF16).astype(F32)
    row = lax.broadcasted_iota(jnp.int32, (LOG_ROWS, HEAD_DIM), 0)
    rest = jnp.where(row == 2, log - top - mid, 0.0)
    return jnp.where(row == 0, top, jnp.where(row == 1, mid, rest)).astype(BF16)


def read_log(message_ref):
    rows = message_ref.shape[0]
    facts = message_ref[rows - LOG_ROWS :, :].astype(F32)
    return facts[0:1] + facts[1:2] + facts[2:3]


def state_rows(message_ref, index):
    return message_ref[index * HEAD_DIM : (index + 1) * HEAD_DIM, :]


def own_states(first, k_ref, v_ref, columns, own_ref, message_ref):
    length = columns.shape[0]
    factor = jnp.exp(columns[length - 1 :, :] - columns)
    for i in range(own_ref.shape[0]):
        h = first + i
        at = head_slice(h)
        weighted = k_ref[:, at].astype(F32) * factor[:, h : h + 1]
        top, rest = halves(weighted)
        both = lax.dot_general(
            jnp.concatenate([top, rest], axis=1), v_ref[:, at], TN, preferred_element_type=F32
        )
        state = both[:HEAD_DIM] + both[HEAD_DIM:]
        own_ref[i] = state
        message_ref[i * HEAD_DIM : (i + 1) * HEAD_DIM, :] = state.astype(BF16)


def started(pairs, sems):
    copies = [
        pltpu.make_async_copy(source, target, sems.at[i]) for i, (source, target) in enumerate(pairs)
    ]
    for copy in copies:
        copy.start()
    return copies


def first_state_kernel(place_ref, k_hbm, v_hbm, rate_hbm, *refs):
    own_ref, log_ref, col_ref, rate_ref, k_ref, v_ref, message_ref, sems = refs
    copies = started(((rate_hbm, rate_ref), (k_hbm.at[0], k_ref), (v_hbm.at[0], v_ref)), sems)
    length = k_ref.shape[0]
    copies[0].wait()
    rate = rate_ref[0]
    columns = decay_columns(rate, lower_ones(length))
    col_ref[...] = columns
    log_ref[...] = jnp.zeros_like(log_ref)
    log_ref[:, : rate.shape[0]] = columns[length - 1 :, :]
    message_ref[message_ref.shape[0] - LOG_ROWS :, :] = log_rows(log_ref[...])
    copies[1].wait()
    copies[2].wait()
    own_states(0, k_ref, v_ref, columns, own_ref, message_ref)


def more_state_kernel(first, k_ref, v_ref, col_ref, log_ref, *rest):
    own_ref, message_ref = rest[-2:]
    message_ref[message_ref.shape[0] - LOG_ROWS :, :] = log_rows(log_ref[...])
    own_states(first, k_ref, v_ref, col_ref[...], own_ref, message_ref)


def chain_kernel(phase, first, place_ref, own_ref, log_ref, got_ref, *rest):
    out_ref = rest[-1]
    size = (out_ref.shape[0] - LOG_ROWS) // HEAD_DIM
    right = place_ref[0] == phase
    log = log_ref[...]
    later = read_log(got_ref)
    own_factor = jnp.where(right, 1.0, jnp.exp(later))
    got_factor = jnp.where(right, jnp.exp(log), 1.0)
    for i in range(size):
        h = first + i
        value = (
            own_factor[:, h : h + 1] * own_ref[i]
            + got_factor[:, h : h + 1] * state_rows(got_ref, i).astype(F32)
        )
        out_ref[i * HEAD_DIM : (i + 1) * HEAD_DIM, :] = value.astype(BF16)
    out_ref[size * HEAD_DIM :, :] = log_rows(log + later)


def entering_state(group, got, index):
    state = state_rows(got[0], index)
    for phase in range(1, len(got)):
        state = jnp.where(group == phase + 1, state_rows(got[phase], index), state)
    return jnp.where(group == 0, jnp.zeros_like(state), state)


def weight_copies(places, weight_hbm, weights, sems):
    copies = []
    for i, (index, ref) in enumerate(zip(places, weights)):
        depth = ref.shape[0]
        copies.append(
            pltpu.make_async_copy(weight_hbm.at[pl.ds(index * depth, depth)], ref, sems.at[i])
        )
    for copy in copies:
        copy.start()
    return copies


def load_kernel(places, weight_hbm, *rest):
    token_ref, sems = rest[-2:]
    weights = rest[-2 - len(places) : -2]
    copies = weight_copies(places, weight_hbm, weights, sems)
    token_ref[...] = jnp.zeros_like(token_ref)
    for copy in copies:
        copy.wait()


def local_kernel(copied, k_ref, v_ref, col_ref, rate_ref, weight_hbm, *rest):
    sources, rest = rest[:copied], rest[copied:]
    targets, rest = rest[:copied], rest[copied:]
    local_ref, token_ref = rest[:2]
    weights, sems, more = rest[2:-2], rest[-2], rest[-1]
    loads = started(tuple(zip(sources, targets)), more)
    copies = weight_copies(range(len(weights)), weight_hbm, weights, sems)
    token_ref[...] = jnp.zeros_like(token_ref)
    q_ref = targets[0]
    lower = lower_ones(k_ref.shape[0])
    rows = decay_rows(rate_ref[0], lower)
    loads[0].wait()
    for h in range(local_ref.shape[1] // HEAD_DIM):
        at = head_slice(h)
        scores = lax.dot_general(q_ref[0, :, at], k_ref[:, at], NT, preferred_element_type=F32)
        decay = jnp.exp(jnp.where(lower, col_ref[:, h : h + 1] - rows[h : h + 1, :], NEGATIVE))
        narrow = (scores * decay).astype(BF16)
        local_ref[:, at] = jnp.dot(narrow, v_ref[:, at], preferred_element_type=F32)
    for copy in loads[1:] + copies:
        copy.wait()


def hidden_kernel(phases, first, place_ref, q_ref, col_ref, local_ref, *rest):
    got, hidden_ref = rest[:phases], rest[-1]
    for i in range(hidden_ref.shape[1] // HEAD_DIM):
        h = first + i
        whole = head_slice(h)
        state = entering_state(place_ref[0], got, i)
        inter = jnp.dot(q_ref[0, :, whole], state, preferred_element_type=F32)
        attended = local_ref[:, whole] + inter * jnp.exp(col_ref[:, h : h + 1])
        hidden_ref[:, head_slice(i)] = normalize(attended).astype(BF16)


def final_kernel(first, phases, place_ref, own_ref, log_ref, *rest):
    got, out_ref = rest[:phases], rest[-1]
    keep = jnp.exp(log_ref[...])

    def write(group):
        prefix = got[group - 1] if group > 0 else None
        suffix = got[phases - 1 - group] if group < phases else None
        later = None if suffix is None else jnp.exp(read_log(suffix))
        for i in range(out_ref.shape[0]):
            h = first + i
            value = own_ref[i]
            if prefix is not None:
                value = value + keep[:, h : h + 1] * state_rows(prefix, i).astype(F32)
            if suffix is not None:
                value = later[:, h : h + 1] * value + state_rows(suffix, i).astype(F32)
            out_ref[i] = value

    for group in range(phases + 1):
        pl.when(place_ref[0] == group)(functools.partial(write, group))


def flat_rows(ref, rows_ref):
    rows, steps = ref.shape[0], ref.shape[1]
    for r in range(rows):
        rows_ref[r * steps : (r + 1) * steps, :] = ref[r].astype(F32)


def decode_kernel(count, place_ref, prompt_ref, q_ref, k_ref, v_ref, rate_ref, *rest):
    near, far = rest[:count], rest[count : 2 * count]
    finals = [(c, i) for c, ref in enumerate(near) for i in range(ref.shape[0])]
    out_ref, q_rows, k_rows, v_rows, rate_rows = rest[-5:]
    rows_here, steps = q_ref.shape[0], q_ref.shape[1]
    d_rows = q_rows.shape[0]
    flat_rows(q_ref, q_rows)
    flat_rows(k_ref, k_rows)
    flat_rows(v_ref, v_rows)
    flat_rows(rate_ref, rate_rows)
    rows, cols = identity(d_rows)
    seen = (rows // steps == cols // steps) & (rows >= cols)
    ones = seen.astype(F32)
    rates = rate_rows[...]
    down = -jnp.dot(ones, rates, precision=HIGH, preferred_element_type=F32)
    across = -lax.dot_general(
        rates, ones, (((0,), (1,)), ((), ())), precision=HIGH, preferred_element_type=F32
    )
    grow = jnp.exp(down)
    row_of = lax.broadcasted_iota(jnp.int32, (d_rows, HEAD_DIM), 0) // steps
    prompt = jnp.zeros((d_rows, HEAD_DIM), jnp.int32)
    for r in range(rows_here):
        prompt = jnp.where(row_of == r, prompt_ref[r], prompt)
    mine = prompt == place_ref[1]
    for i in range(rates.shape[1]):
        at = head_slice(i)
        query = q_rows[:, at]
        narrow = query.astype(BF16)
        terms = []
        c, slot = finals[i]
        for ref in (near[c], far[c]):
            top, low = halves(ref[slot])
            both = jnp.dot(
                narrow, jnp.concatenate([top, low], axis=1), preferred_element_type=F32
            )
            terms.append(both[:, :HEAD_DIM] + both[:, HEAD_DIM:])
        base = jnp.where(mine, terms[0], terms[1])
        scores = lax.dot_general(
            query, k_rows[:, at], NT, precision=HIGH, preferred_element_type=F32
        )
        decay = jnp.exp(jnp.where(seen, down[:, i : i + 1] - across[i : i + 1, :], NEGATIVE))
        intra = jnp.dot(scores * decay, v_rows[:, at], precision=HIGH, preferred_element_type=F32)
        q_rows[:, at] = normalize(base * grow[:, i : i + 1] + intra)
    pad = out_ref.shape[0] - d_rows
    value = q_rows[...]
    if pad:
        value = jnp.concatenate([value, jnp.zeros((pad, value.shape[1]), F32)], axis=0)
    out_ref[...] = value.astype(BF16)


def times_weight(rows, weights, column, width):
    total = None
    for i, ref in enumerate(weights):
        depth = ref.shape[0]
        term = jnp.dot(
            rows[:, i * depth : (i + 1) * depth],
            ref[:, pl.ds(column, width)],
            preferred_element_type=F32,
        )
        total = term if total is None else total + term
    return total


def project_kernel(pieces, width, chunks, added, place_ref, *rest):
    hidden, rest = rest[:chunks], rest[chunks:]
    addends, weights = rest[:added], rest[added : -len(pieces)]
    outs = rest[-len(pieces) :]
    rows = jnp.concatenate([ref[...] for ref in hidden], axis=1)
    for n, ((bits, first, columns), out_ref) in enumerate(zip(pieces, outs)):
        column = pl.multiple_of((place_ref[2] ^ bits) * width + first, HEAD_DIM)
        total = times_weight(rows, weights, column, columns)
        if added:
            total = total + addends[n][...]
        out_ref[...] = total.astype(out_ref.dtype)


def decode_project_kernel(place_ref, rows_ref, *rest):
    weights, outs = rest[:WEIGHT_PARTS], rest[-4:]
    width = outs[0].shape[1]
    rows = rows_ref[...]
    for bits, out_ref in enumerate(outs):
        column = pl.multiple_of((place_ref[2] ^ bits) * width, HEAD_DIM)
        terms = times_weight(rows, weights, column, width)
        out_ref[...] = terms[: out_ref.shape[0]].astype(out_ref.dtype)


def relay_kernel(own_ref, got_ref, *rest):
    out_ref = rest[-1]
    out_ref[...] = (own_ref[...] + got_ref[...].astype(F32)).astype(BF16)


def finish_kernel(own_a, own_b, ax, ay, bx, by, d_own, d_x, d_y, d_far, *rest):
    prefill_hbm, decode_ref, out_ref, sems = rest
    split = own_a.shape[1]
    count = sems.shape[0]
    size = out_ref.shape[0] // count
    copies = []
    for c in range(count):
        at = slice(c * size, (c + 1) * size)
        for first, own, x_ref, y_ref in ((0, own_a, ax, ay), (split, own_b, bx, by)):
            total = own[at] + x_ref[at].astype(F32) + y_ref[at].astype(F32)
            out_ref[at, first : first + own.shape[1]] = total.astype(BF16)
        copy = pltpu.make_async_copy(
            out_ref.at[pl.ds(c * size, size)], prefill_hbm.at[0, pl.ds(c * size, size)], sems.at[c]
        )
        copy.start()
        copies.append(copy)
    rows, steps = decode_ref.shape[0], decode_ref.shape[1]
    total = d_own[...] + d_x[...].astype(F32) + d_y[...].astype(F32) + d_far[...].astype(F32)
    for r in range(rows):
        decode_ref[r] = total[r * steps : (r + 1) * steps].astype(BF16)
    for copy in copies:
        copy.wait()


def swap(array, axis, size, bit):
    return lax.ppermute(array, axis, [(i, i ^ bit) for i in range(size)])


def body(
    prefill_query,
    prefill_key,
    prefill_value,
    prefill_rate,
    out_weight,
    decode_query,
    decode_key,
    decode_value,
    decode_rate,
    prompt_of_row,
    *,
    groups,
    reps,
    parts,
):
    length = prefill_query.shape[1]
    features = prefill_query.shape[2]
    heads = prefill_rate.shape[1]
    rows_here, steps = decode_query.shape[0], decode_query.shape[1]
    d_rows = rows_here * steps
    d_pad = -(-d_rows // 16) * 16
    place = jnp.stack([lax.axis_index("ctx"), lax.axis_index("rep"), lax.axis_index("head")])
    place = place.astype(jnp.int32)
    count = min(CHUNKS, heads)
    edges = [heads * c // count for c in range(count + 1)]
    chunks = [(a, b - a) for a, b in zip(edges[:-1], edges[1:])]
    phases = groups - 1
    state_elements = heads * HEAD_DIM * HEAD_DIM

    def in_hbm(array):
        return pltpu.with_memory_space_constraint(array, pltpu.HBM)

    def in_vmem(array):
        return pltpu.with_memory_space_constraint(array, pltpu.VMEM)

    def message_shape(size):
        return sds((size * HEAD_DIM + LOG_ROWS, HEAD_DIM), BF16)

    decode_shape = (rows_here, steps, features)
    made = call(
        first_state_kernel,
        "own_state",
        [SMEM] + [HBM] * 3,
        [
            pltpu.VMEM((chunks[0][1], HEAD_DIM, HEAD_DIM), F32),
            pltpu.VMEM((1, HEAD_DIM), F32),
            pltpu.VMEM((length, heads), F32),
            pltpu.VMEM((1, heads, length), F32),
            pltpu.VMEM((length, features), BF16),
            pltpu.VMEM((length, features), BF16),
            message_shape(chunks[0][1]),
        ],
        [pltpu.SemaphoreType.DMA((3,))],
        cost(4 * length * features * HEAD_DIM, 16 * length * features),
    )(place, in_hbm(prefill_key), in_hbm(prefill_value), in_hbm(prefill_rate))
    own, log_row, columns, rate, keys, values = map(in_vmem, made[:6])
    owns, values_out = [own], [made[6]]
    weight_hbm = in_hbm(out_weight)
    weight_part = pltpu.VMEM((features // WEIGHT_PARTS, out_weight.shape[1]), BF16)
    token = sds((8, HEAD_DIM), F32)
    arrays = (prefill_query, decode_query, decode_key, decode_value)
    queries, d_query, d_key, d_value, local, local_token, *weights = call(
        functools.partial(local_kernel, len(arrays)),
        "local_attention",
        [VMEM] * 4 + [HBM] * (1 + len(arrays)),
        [pltpu.VMEM(array.shape, BF16) for array in arrays]
        + [pltpu.VMEM((length, features), F32), token]
        + [weight_part] * EARLY_PARTS,
        [pltpu.SemaphoreType.DMA((EARLY_PARTS,)), pltpu.SemaphoreType.DMA((len(arrays),))],
        cost(4 * length * length * features, 12 * length * features, heads * length * length),
    )(keys, values, columns, rate, weight_hbm, *map(in_hbm, arrays))
    queries, d_query, d_key, d_value, local = map(
        in_vmem, (queries, d_query, d_key, d_value, local)
    )
    for first, size in chunks[1:]:
        made = call(
            functools.partial(more_state_kernel, first),
            "more_state",
            [VMEM] * 4 + [ANY],
            [pltpu.VMEM((size, HEAD_DIM, HEAD_DIM), F32), message_shape(size)],
            (),
            cost(4 * length * size * HEAD_DIM * HEAD_DIM, 8 * length * features),
        )(keys, values, columns, log_row, local_token)
        owns.append(in_vmem(made[0]))
        values_out.append(made[1])

    todo = list(LATER_PARTS)

    def load_weight(*after):
        if not todo:
            return []
        places = range(len(weights), len(weights) + todo.pop(0))
        *loaded, done = call(
            functools.partial(load_kernel, places),
            "load_weight",
            [HBM] + [ANY] * len(after),
            [weight_part] * len(places) + [token],
            [pltpu.SemaphoreType.DMA((len(places),))],
            cost(1, 1),
        )(weight_hbm, *after)
        weights.extend(loaded)
        return [done]

    received = []
    after = values_out[-1:]
    for phase in range(phases):
        pairs = []
        for g in range(groups):
            for r in range(reps):
                if g in (phase, groups - 2 - phase):
                    other = (g + 1, r)
                elif g in (phase + 1, groups - 1 - phase):
                    other = (g - 1, r)
                else:
                    other = (g, r ^ 1)
                pairs.append((g * reps + r, other[0] * reps + other[1]))
        if phase > 0:
            values_out = []
            for c, (first, size) in enumerate(chunks):
                value = call(
                    functools.partial(chain_kernel, phase, first),
                    "chain",
                    [SMEM, VMEM, VMEM, VMEM] + [ANY] * len(after),
                    message_shape(size),
                    (),
                    cost(2 * size * HEAD_DIM * HEAD_DIM, 24 * size * HEAD_DIM * HEAD_DIM),
                )(place, owns[c], log_row, received[-1][c], *after)
                values_out.append(value)
                after = load_weight(value) if c == 0 else []
        received.append([lax.ppermute(value, ("ctx", "rep"), pairs) for value in values_out])
    loaded = []
    while todo:
        loaded = load_weight(values_out[-1], *loaded)
    weights = [in_vmem(part) for part in weights]

    def make_hidden(c, *after):
        first, size = chunks[c]
        return call(
            functools.partial(hidden_kernel, phases, first),
            "hidden",
            [SMEM] + [VMEM] * (3 + phases) + [ANY] * len(after),
            sds((length, size * HEAD_DIM), BF16),
            (),
            cost(2 * length * size * HEAD_DIM * HEAD_DIM, 20 * length * size * HEAD_DIM),
        )(place, queries, columns, local, *[received[phase][c] for phase in range(phases)], *after)

    def make_final(c, *after):
        first, size = chunks[c]
        final = call(
            functools.partial(final_kernel, first, phases),
            "final_state",
            [SMEM, VMEM, VMEM] + [VMEM] * phases + [ANY] * len(after),
            sds((size, HEAD_DIM, HEAD_DIM), F32),
            (),
            cost(4 * state_elements // count, state_elements * 4),
        )(place, owns[c], log_row, *[got[c] for got in received], *after)
        return final, swap(final, "rep", reps, 1)

    hidden, finals = [make_hidden(0, *loaded)], []
    for c in range(1, count):
        finals.append(make_final(c - 1, hidden[-1]))
        hidden.append(make_hidden(c, finals[-1][0]))

    def decode_rows(finals, others, *after):
        flat = pltpu.VMEM((d_rows, features), F32)
        return call(
            functools.partial(decode_kernel, count),
            "decode_rows",
            [SMEM, SMEM] + [VMEM] * (4 + 2 * count) + [ANY] * len(after),
            sds((d_pad, features), BF16),
            [flat, flat, flat, pltpu.VMEM((d_rows, heads), F32)],
            cost(16 * d_rows * features * HEAD_DIM, state_elements),
        )(
            place,
            prompt_of_row,
            d_query,
            d_key,
            d_value,
            jnp.transpose(decode_rate, (0, 2, 1)),
            *finals,
            *others,
            *after,
        )

    out_columns = out_weight.shape[1]
    if parts != 4 or (out_columns // parts) % 256 != 0 or length % 64 != 0:
        rows_all = jnp.concatenate([jnp.concatenate(hidden, axis=1), decode_rows(*zip(*finals, make_final(count - 1)))], axis=0)
        terms = jnp.dot(rows_all, out_weight, preferred_element_type=F32)
        summed = lax.psum_scatter(terms, "head", scatter_dimension=1, tiled=True)
        prefill_out = summed[:length].astype(BF16)[None]
        decode_out = summed[length : length + d_rows].astype(BF16)
        return prefill_out, decode_out.reshape(rows_here, steps, -1)

    width = out_columns // parts
    split = (width * 5 // 12) // HEAD_DIM * HEAD_DIM
    side_x, side_y = (0, split), (split, width - split)

    def project(pieces, dtype, inputs=None, parts_used=None, addends=()):
        dtypes = dtype if isinstance(dtype, tuple) else (dtype,) * len(pieces)
        inputs = hidden if inputs is None else inputs
        used = weights if parts_used is None else weights[parts_used]
        moved = sum(columns for _, _, columns in pieces)
        depth = sum(array.shape[1] for array in inputs)
        return call(
            functools.partial(project_kernel, pieces, width, len(inputs), len(addends)),
            "project",
            [SMEM] + [VMEM] * (len(inputs) + len(addends) + len(used)),
            [sds((length, columns), kind) for (_, _, columns), kind in zip(pieces, dtypes)],
            (),
            cost(2 * length * depth * moved, depth * moved * 2),
        )(place, *inputs, *addends, *used)

    def relay(own_term, got):
        return call(
            relay_kernel,
            "relay",
            [VMEM, VMEM],
            sds(own_term.shape, BF16),
            (),
            cost(own_term.size, own_term.size * 8),
        )(own_term, got)

    far = [(3, *side_x), (3, *side_y)]
    if count == 2 and chunks[0][1] * HEAD_DIM * 2 == features and WEIGHT_PARTS % 2 == 0:
        early = slice(0, WEIGHT_PARTS // 2)
        late = slice(WEIGHT_PARTS // 2, WEIGHT_PARTS)
        begun = project(far, F32, hidden[:1], early)
        to_x, to_y = project(far, BF16, hidden[1:], late, begun)
    else:
        to_x, to_y = project(far, BF16)
    far_a = swap(to_x, "head", parts, 1)
    far_b = swap(to_y, "head", parts, 2)
    near_y, near_x = project([(2, *side_y), (1, *side_x)], BF16)
    x_a = swap(near_x, "head", parts, 1)
    y_b = swap(near_y, "head", parts, 2)
    pass_a, pass_b = project([(2, *side_x), (1, *side_y)], F32)
    own_a, own_b = project([(0, *side_x), (0, *side_y)], F32)
    sent_a, sent_b = relay(pass_a, far_a), relay(pass_b, far_b)
    y_a = swap(sent_a, "head", parts, 2)
    x_b = swap(sent_b, "head", parts, 1)

    finals.append(make_final(count - 1, to_y))
    d_hidden = decode_rows(*zip(*finals), sent_a, sent_b)
    d_own, d_x, d_y, d_far = call(
        decode_project_kernel,
        "decode_project",
        [SMEM] + [VMEM] * (1 + WEIGHT_PARTS),
        [sds((d_rows, width), F32)] + [sds((d_rows, width), BF16)] * 3,
        (),
        cost(2 * d_pad * features * out_columns, features * out_columns // 8),
    )(place, d_hidden, *weights)
    prefill_out, decode_out = call(
        finish_kernel,
        "finish",
        [VMEM] * 10,
        [sds((1, length, width), BF16), sds((rows_here, steps, width), BF16)],
        [pltpu.VMEM((length, width), BF16), pltpu.SemaphoreType.DMA((4,))],
        cost(3 * length * width, 10 * length * width),
        out_specs=[HBM, VMEM],
    )(
        own_a,
        own_b,
        x_a,
        y_a,
        x_b,
        y_b,
        d_own,
        swap(d_x, "head", parts, 1),
        swap(d_y, "head", parts, 2),
        swap(d_far, "head", parts, 3),
    )
    return prefill_out, decode_out


def solution(mesh):
    return jax.shard_map(
        functools.partial(
            body, groups=mesh.shape["ctx"], reps=mesh.shape["rep"], parts=mesh.shape["head"]
        ),
        mesh=mesh,
        in_specs=(
            P("rep", "ctx", "head"),
            P("rep", "ctx", "head"),
            P("rep", "ctx", "head"),
            P("rep", "head", "ctx"),
            P("head", None),
            P(("ctx", "rep"), None, "head"),
            P(("ctx", "rep"), None, "head"),
            P(("ctx", "rep"), None, "head"),
            P(("ctx", "rep"), "head", None),
            P(("ctx", "rep")),
        ),
        out_specs=(P("rep", "ctx", "head"), P(("ctx", "rep"), None, "head")),
        check_vma=False,
    )
```
